256 devices in a mesh: section: 2 (over core), mp: 8 (over z), dp: 16 (over y, x).
Axes of the slice: x: 4, y: 4, z: 8, core: 2. Of those that a mesh axis runs over, the one named last changes fastest.
Arguments:
- patches: bfloat16 [16, 256, 6144], P('dp', ('section', 'mp')), may hold values from -6 to 6
- vis_index: int32 [16, 256], P('dp', ('section', 'mp')), may hold values from 0 to 1023, as said below
- input_weight: bfloat16 [6144, 3, 3072], P('section', None, 'mp'), may hold values from -0.078125 to 0.078125
- output_weight: bfloat16 [3072, 6144], P('mp', 'section'), may hold values from -1.75 to 1.75
- embed_weight: bfloat16 [6144, 512], P(('section', 'mp')), may hold values from -0.078125 to 0.078125
- mask_token: bfloat16 [512], replicated, may hold values from -5 to 5
- position_table: bfloat16 [1024, 512], P(('section', 'mp')), may hold values from -5 to 5
- decoder_input: bfloat16 [512, 3, 512], replicated, may hold values from -0.25 to 0.25
- decoder_output: bfloat16 [512, 512], replicated, may hold values from -0.25 to 0.25
- pixel_weight: bfloat16 [512, 768], replicated, may hold values from -0.25 to 0.25
- target: bfloat16 [16, 1024, 768], P('dp', ('section', 'mp')), may hold values from -6 to 6
Outputs:
- prediction: bfloat16 [16, 1024, 768], P('dp', ('section', 'mp'))
- patch_grad: bfloat16 [16, 256, 6144], P('dp', ('section', 'mp'))
The draws below stay inside these ranges and needn't reach their ends.
Inputs may be any that keep to these rules, and one draw needn't show every extreme that they name: `vis_index`: in each scene the 256 positions are distinct. Split a scene's visible patches into 16 aligned blocks of 16 and the positions into 16 aligned ranges of 64: each block has exactly 2 patches in a quarter of the ranges (rounded down), none in another quarter and 1 in each other range.
All inputs are finite; a program needn't handle non-finite values.
Results may differ from the reference program's by a relative error of at most 0.03.
Values may be sent and summed in bfloat16 or wider, within the bound.
No kernel may reach another device: no remote copies, remote signals or barrier semaphores. Data moves between devices by JAX's collectives and lax.ppermute only.
A program may use at most 128 MiB of HBM per device.

```python
import jax
import jax.numpy as jnp
from jax import lax

D = 6144
HEADS = 24
HD = 128
DW = 512
DHEADS = 16
DHD = 32
PIX = 768
VIS = 256
NPOS = 1024
SCENES = 16
N_SECTION = 2
N_MP = 8


def draw_vis_index(key, part):
    key = jax.random.fold_in(key, 11)
    group_size = N_SECTION * N_MP
    tok_dev = VIS // group_size
    pos_dev = NPOS // group_size
    base_count = tok_dev // group_size
    quarter = group_size // 4

    def one_scene(scene_key):
        order_key, shuffle_key, slot_key = jax.random.split(scene_key, 3)
        order_rank = jax.vmap(lambda sub_key: jnp.argsort(jax.random.permutation(sub_key, group_size)))(jax.random.split(order_key, group_size))
        first_block = (jnp.arange(group_size) + 1) % group_size
        order_rank = order_rank.at[0].set(first_block)
        counts = jnp.where(order_rank < quarter, 2 * base_count, jnp.where(order_rank < 2 * quarter, 0, base_count))
        destination = jax.vmap(lambda count_row: jnp.repeat(jnp.arange(group_size), count_row, total_repeat_length=tok_dev))(counts)
        shuffles = jax.vmap(lambda sub_key: jax.random.permutation(sub_key, tok_dev))(jax.random.split(shuffle_key, group_size))
        destination = jnp.take_along_axis(destination, shuffles, axis=1).reshape(-1)
        dest_hot = (destination[:, None] == jnp.arange(group_size)[None, :]).astype(jnp.int32)
        arrival = jnp.sum((jnp.cumsum(dest_hot, axis=0) - dest_hot) * dest_hot, axis=1)
        slot_perm = jax.vmap(lambda sub_key: jax.random.permutation(sub_key, pos_dev))(jax.random.split(slot_key, group_size))
        ranges = jnp.arange(group_size)
        anchor = jnp.where(ranges == 0, 0, jnp.where(ranges == group_size - 1, pos_dev - 1, slot_perm[:, 0]))
        slot_perm = (slot_perm - slot_perm[:, :1] + anchor[:, None]) % pos_dev
        local_slot = slot_perm[destination, arrival]
        return (destination * pos_dev + local_slot).astype(jnp.int32)
    return jax.vmap(one_scene)(jax.random.split(key, SCENES))


def block_levels(own_key, dims, pieces, low, high):
    def one(axis_at, blocks):
        steps = jax.random.uniform(jax.random.fold_in(jax.random.fold_in(own_key, 6), axis_at), (blocks,), jnp.float32, low / len(pieces), high / len(pieces))
        return jnp.repeat(jnp.exp(steps), dims[axis_at] // blocks).reshape((-1,) + (1,) * (len(dims) - axis_at - 1))

    loudness = one(*pieces[0])
    for cut in pieces[1:]:
        loudness = loudness * one(*cut)
    return loudness


def noise(stream_key, shape, scale, limit, shards=(), held_as=jnp.bfloat16):
    level = block_levels(stream_key, shape, shards, -0.22, 0.18) if shards else 1.0
    array = jax.random.normal(stream_key, shape, jnp.float32) * scale * level
    return jnp.minimum(jnp.maximum(array, -limit), limit).astype(held_as)


def setup_inputs(seed: int = 0) -> dict:
    seeds = jax.random.split(jax.random.key(seed), 12)
    patches = noise(seeds[0], (SCENES, VIS, D), 1.0, 6.0, ((0, 16), (1, 16)))
    vis_index = draw_vis_index(jax.random.fold_in(seeds[11], 71), 0)
    input_weight = noise(seeds[2], (D, 3, HEADS * HD), D ** -0.5, 0.078125, ((0, 2), (2, 8)))
    output_weight = noise(seeds[3], (HEADS * HD, D), (max(1, HEADS * HD // 256)) ** -0.5, 1.75, ((0, 8), (1, 2)))
    embed_weight = noise(seeds[4], (D, DW), D ** -0.5, 0.078125, ((0, 16),))
    mask_token = noise(seeds[5], (DW,), 1.0, 5.0)
    position_table = noise(seeds[6], (NPOS, DW), 1.0, 5.0, ((0, 16),))
    decoder_input = noise(seeds[7], (DW, 3, DW), DW ** -0.5, 0.25)
    decoder_output = noise(seeds[8], (DW, DW), DW ** -0.5, 0.25)
    pixel_weight = noise(seeds[9], (DW, PIX), DW ** -0.5, 0.25)
    target = noise(seeds[10], (SCENES, NPOS, PIX), 1.0, 6.0, ((0, 16), (1, 16)))
    return {"patches": patches, "vis_index": vis_index, "input_weight": input_weight, "output_weight": output_weight, "embed_weight": embed_weight, "mask_token": mask_token, "position_table": position_table, "decoder_input": decoder_input, "decoder_output": decoder_output, "pixel_weight": pixel_weight, "target": target}


EPSILON = 1e-06

def to_low(values):
    return lax.optimization_barrier(values.astype(jnp.bfloat16)).astype(jnp.float32)

def layer_norm(values):
    centre = lax.optimization_barrier(jnp.mean(values, axis=-1, keepdims=True))
    centered = values - centre
    inverse = lax.rsqrt(lax.optimization_barrier(jnp.mean(centered * centered, axis=-1, keepdims=True)) + EPSILON)
    return (centered * inverse, inverse)

def norm_back(normed, inverse, gradient):
    mean_grad = lax.optimization_barrier(jnp.mean(gradient, axis=-1, keepdims=True))
    mean_dot = lax.optimization_barrier(jnp.mean(gradient * normed, axis=-1, keepdims=True))
    return inverse * (gradient - mean_grad - normed * mean_dot)

def attend(queries, key_rows, values, factor):
    scores = jnp.einsum('hqd,hkd->hqk', queries.astype(jnp.float32), key_rows.astype(jnp.float32)) * factor
    exponent = jnp.exp(scores)
    attn_probs = exponent / lax.optimization_barrier(jnp.sum(exponent, axis=-1, keepdims=True))
    probs_low = to_low(attn_probs)
    result = jnp.einsum('hqk,hkd->hqd', probs_low, values.astype(jnp.float32))
    return (result.astype(jnp.bfloat16), attn_probs, probs_low)

def attend_back(queries, key_rows, values, attn_probs, probs_low, out_grad, factor, blocks):
    out_full = out_grad.astype(jnp.float32)
    query_full = queries.astype(jnp.float32)
    prob_grad = jnp.einsum('hqd,hkd->hqk', out_full, values.astype(jnp.float32))
    row_delta = lax.optimization_barrier(jnp.sum(attn_probs * prob_grad, axis=-1, keepdims=True))
    score_grad = to_low(attn_probs * (prob_grad - row_delta))
    query_grad = jnp.einsum('hqk,hkd->hqd', score_grad, key_rows.astype(jnp.float32)) * factor
    heads, length, depth = queries.shape
    span = length // blocks
    score_blocks = score_grad.reshape(heads, blocks, span, -1)
    prob_blocks = probs_low.reshape(heads, blocks, span, -1)
    key_grad = jnp.einsum('hgqk,hgqd->ghkd', score_blocks, query_full.reshape(heads, blocks, span, depth)) * factor
    value_grad = jnp.einsum('hgqk,hgqd->ghkd', prob_blocks, out_full.reshape(heads, blocks, span, depth))
    if blocks == 1:
        return (query_grad, key_grad[0], value_grad[0])
    return (query_grad, lax.optimization_barrier(jnp.sum(to_low(key_grad), axis=0)), lax.optimization_barrier(jnp.sum(to_low(value_grad), axis=0)))

def scene_pass(patches, vis_index, target, input_weight, output_weight, embed_weight, mask_token, position_table, decoder_input, decoder_output, pixel_weight):
    tokens = patches.astype(jnp.float32)
    normed, inverse = layer_norm(tokens)
    head_width = HEADS * HD
    input_flat = input_weight.reshape(D, 3 * head_width)
    mixture = jnp.dot(normed.astype(jnp.bfloat16), input_flat, preferred_element_type=jnp.float32)
    mixture = mixture.reshape(VIS, 3, HEADS, HD).transpose(1, 2, 0, 3)
    query_hat, query_inv = layer_norm(mixture[0])
    key_hat, key_inv = layer_norm(mixture[1])
    enc_factor = HD ** (-0.5)
    query_low = query_hat.astype(jnp.bfloat16)
    key_low = key_hat.astype(jnp.bfloat16)
    value_low = mixture[2].astype(jnp.bfloat16)
    attended, enc_probs, enc_low = attend(query_low, key_low, value_low, enc_factor)
    attended_flat = attended.transpose(1, 0, 2).reshape(VIS, head_width)
    layer = (tokens + jnp.dot(attended_flat, output_weight, preferred_element_type=jnp.float32)).astype(jnp.bfloat16)
    embedded = jnp.dot(layer, embed_weight, preferred_element_type=jnp.float32).astype(jnp.bfloat16)
    visible = jnp.zeros((NPOS,), jnp.float32).at[vis_index].set(1.0)
    filled = jnp.broadcast_to(mask_token, (NPOS, DW)).at[vis_index].set(embedded)
    stream = filled.astype(jnp.float32) + position_table.astype(jnp.float32)
    stream_hat, stream_inv = layer_norm(stream)
    decoder_flat = decoder_input.reshape(DW, 3 * DW)
    dec_mix = jnp.dot(stream_hat.astype(jnp.bfloat16), decoder_flat, preferred_element_type=jnp.float32)
    dec_mix = dec_mix.reshape(NPOS, 3, DHEADS, DHD).transpose(1, 2, 0, 3)
    dquery_hat, dquery_inv = layer_norm(dec_mix[0])
    dkey_hat, dkey_inv = layer_norm(dec_mix[1])
    dec_factor = DHD ** (-0.5)
    dquery_low = dquery_hat.astype(jnp.bfloat16)
    dkey_low = dkey_hat.astype(jnp.bfloat16)
    dvalue_low = dec_mix[2].astype(jnp.bfloat16)
    dec_att, dec_probs, dec_low = attend(dquery_low, dkey_low, dvalue_low, dec_factor)
    dec_flat = dec_att.transpose(1, 0, 2).reshape(NPOS, DW)
    second = stream + jnp.dot(dec_flat, decoder_output, preferred_element_type=jnp.float32)
    final_hat, final_inv = layer_norm(second)
    pred_full = jnp.dot(final_hat.astype(jnp.bfloat16), pixel_weight, preferred_element_type=jnp.float32)
    prediction = pred_full.astype(jnp.bfloat16)
    error_rows = jnp.where(visible[:, None] > 0, 0.0, pred_full - target.astype(jnp.float32)).astype(jnp.bfloat16)
    grad_final = jnp.dot(error_rows, pixel_weight.T, preferred_element_type=jnp.float32)
    grad_second = norm_back(final_hat, final_inv, grad_final)
    grad_att = jnp.dot(grad_second.astype(jnp.bfloat16), decoder_output.T, preferred_element_type=jnp.float32).astype(jnp.bfloat16)
    grad_att = grad_att.reshape(NPOS, DHEADS, DHD).transpose(1, 0, 2)
    gquery, gkey, gvalue = attend_back(dquery_low, dkey_low, dvalue_low, dec_probs, dec_low, grad_att, dec_factor, N_SECTION * N_MP)
    gquery = norm_back(dquery_hat, dquery_inv, gquery)
    gkey = norm_back(dkey_hat, dkey_inv, gkey)
    grad_mix = jnp.stack([gquery, gkey, gvalue]).transpose(2, 0, 1, 3).reshape(NPOS, 3 * DW).astype(jnp.bfloat16)
    grad_hat = jnp.dot(grad_mix, decoder_flat.T, preferred_element_type=jnp.float32)
    grad_stream = grad_second + norm_back(stream_hat, stream_inv, grad_hat)
    grad_embedded = grad_stream[vis_index].astype(jnp.bfloat16)
    grad_layer = jnp.dot(grad_embedded, embed_weight.T, preferred_element_type=jnp.float32).astype(jnp.bfloat16)
    grad_attended = jnp.dot(grad_layer, output_weight.T, preferred_element_type=jnp.float32).astype(jnp.bfloat16)
    grad_attended = grad_attended.reshape(VIS, HEADS, HD).transpose(1, 0, 2)
    equery, ekey, evalue = attend_back(query_low, key_low, value_low, enc_probs, enc_low, grad_attended, enc_factor, 1)
    equery = norm_back(query_hat, query_inv, equery)
    ekey = norm_back(key_hat, key_inv, ekey)
    grad_mixture = jnp.stack([equery, ekey, evalue]).transpose(2, 0, 1, 3).reshape(VIS, 3 * head_width).astype(jnp.bfloat16)
    grad_normed = jnp.dot(grad_mixture, input_flat.T, preferred_element_type=jnp.float32)
    patch_grad = (grad_layer.astype(jnp.float32) + norm_back(normed, inverse, grad_normed)).astype(jnp.bfloat16)
    return (prediction, patch_grad)

def reference(patches, vis_index, input_weight, output_weight, embed_weight, mask_token, position_table, decoder_input, decoder_output, pixel_weight, target):

    def one_scene(scene_args):
        return scene_pass(scene_args[0], scene_args[1], scene_args[2], input_weight, output_weight, embed_weight, mask_token, position_table, decoder_input, decoder_output, pixel_weight)
    prediction, patch_grad = lax.map(one_scene, (patches, vis_index, target))
    return (prediction, patch_grad)
```

```python
import math

import jax
import jax.numpy as jnp
from jax import lax
from jax.experimental import pallas as pl
from jax.experimental.pallas import tpu as pltpu
from jax.sharding import PartitionSpec as P

HD = 128
DHEADS = 16
DHD = 32
EPSILON = 1e-06
LOG2E = math.log2(math.e)
F32 = jnp.float32
BF16 = jnp.bfloat16
OFFSETS = (0, -1, 1, -2, 2, -3, 3, -4)


def dot(a, b):
    return lax.dot_general(a, b, (((1,), (0,)), ((), ())), preferred_element_type=F32)


def dot_nt(a, b):
    return lax.dot_general(a, b, (((1,), (1,)), ((), ())), preferred_element_type=F32)


def dot_tn(a, b):
    return lax.dot_general(a, b, (((0,), (0,)), ((), ())), preferred_element_type=F32)


def row_norm(values, axis=-1):
    centre = jnp.mean(values, axis=axis, keepdims=True)
    centered = values - centre
    inverse = lax.rsqrt(jnp.mean(centered * centered, axis=axis, keepdims=True) + EPSILON)
    return centered * inverse, inverse


def norm_back(normed, inverse, gradient, axis=-1):
    mean_grad = jnp.mean(gradient, axis=axis, keepdims=True)
    mean_dot = jnp.mean(gradient * normed, axis=axis, keepdims=True)
    return inverse * (gradient - mean_grad - normed * mean_dot)


def lanes(columns, rows):
    lane = lax.broadcasted_iota(jnp.int32, (rows, 128), 1)
    out = jnp.zeros((rows, 128), F32)
    for at, column in enumerate(columns):
        out = jnp.where(lane == at, column, out)
    return out


def call(kernel, out_shape, *args, scratch=(), smem=1, limit=56):
    specs = [pl.BlockSpec(memory_space=pltpu.SMEM)] * smem
    specs += [pl.BlockSpec(memory_space=pltpu.VMEM)] * (len(args) - smem)
    return pl.pallas_call(
        kernel,
        out_shape=out_shape,
        in_specs=specs,
        out_specs=jax.tree.map(lambda _: pl.BlockSpec(memory_space=pltpu.VMEM), out_shape),
        scratch_shapes=list(scratch),
        compiler_params=pltpu.CompilerParams(vmem_limit_bytes=limit * 2**20),
    )(*args)


def sds(shape, dtype):
    return jax.ShapeDtypeStruct(shape, dtype)


def project_kernel(ids, *refs):
    chunks = refs[:8]
    w, wo, we = refs[8:11]
    x_out, p_own, p_send, stats, wp_out, xp_own, xp_send = refs[11:18]
    xc, wt = refs[18:]
    half = w.shape[0]
    slab = half // 8
    tok = x_out.shape[2]
    group = 8 * tok
    pieces = wt.shape[0] // 32
    m = ids[1]
    for chunk, offset in zip(chunks, OFFSETS):
        at = lax.rem(m + offset + 8, 8)
        value = chunk[:, :half]
        x_out[0, at] = value[:tok]
        x_out[1, at] = value[tok:]
        wide = value.astype(F32)
        centre = jnp.mean(wide, axis=1, keepdims=True)
        centered = wide - centre
        spread = jnp.sum(centered * centered, axis=1, keepdims=True)
        low = centered.astype(BF16)
        both = lanes((centre, spread), 2 * tok)
        row = pl.multiple_of(at * tok, tok)
        xc[pl.ds(row, tok), :] = low[:tok]
        xc[pl.ds(row + group, tok), :] = low[tok:]
        stats[pl.ds(row, tok), :] = both[:tok]
        stats[pl.ds(row + group, tok), :] = both[tok:]
        column = pl.multiple_of(at * slab, 128)
        for piece in range(pieces):
            wt[piece * 32 : piece * 32 + 32, pl.ds(column, slab)] = chunk[
                :, half + piece * slab : half + (piece + 1) * slab
            ]
    xc[2 * group :, :] = jnp.ones((16, half), BF16)
    wp_out[...] = dot_nt(wt[...], wo[...])
    own_column = pl.multiple_of(m * slab, 128)
    raw = jnp.concatenate(
        [x_out[0, :, :, pl.ds(own_column, slab)], x_out[1, :, :, pl.ds(own_column, slab)]]
    ).reshape(2 * group, slab)
    part = dot(raw, we[...])
    xp_own[...] = part[:group]
    xp_send[...] = part[group:].astype(BF16)
    product = dot(xc[...], w[...])
    p_own[...] = product
    p_send[...] = product.astype(BF16)


def attend_kernel(ids, p_own, p_other, st_own, st_other, att, e_out, q_out, k_out, v_out, aux):
    rows = st_own.shape[0]
    group = rows // 2
    width = p_own.shape[1] // 3
    heads = width // HD
    model = 2 * 8 * width
    stats_other = jnp.concatenate([st_other[group:, :], st_other[:group, :]])
    m_own, s_own = st_own[:, 0:1], st_own[:, 1:2]
    m_other, s_other = stats_other[:, 0:1], stats_other[:, 1:2]
    gap = (m_own - m_other) * 0.5
    centre = (m_own + m_other) * 0.5
    inverse = lax.rsqrt((s_own + s_other) / model + gap * gap + EPSILON)
    slope = p_own[rows : rows + 1, :] - p_other[rows : rows + 1, :].astype(F32)
    columns = [centre, inverse]
    inv_q, inv_k, inv_l = [], [], []
    factor = LOG2E * HD**-0.5

    def mixture(at):
        cols = slice(at * HD, (at + 1) * HD)
        other = jnp.concatenate([p_other[group:rows, cols], p_other[:group, cols]]).astype(F32)
        return inverse * (p_own[:rows, cols] + other + gap * slope[:, cols])

    for head in range(heads):
        cols = slice(head * HD, (head + 1) * HD)
        q_hat, q_inv = row_norm(mixture(head))
        k_hat, k_inv = row_norm(mixture(heads + head))
        v_low = mixture(2 * heads + head).astype(BF16)
        e = jnp.exp2(dot_nt(q_hat.astype(BF16), k_hat.astype(BF16)) * factor)
        l_inv = 1.0 / jnp.sum(e, axis=1, keepdims=True)
        e_low = e.astype(BF16)
        att[:, cols] = (dot(e_low[:group], v_low) * l_inv[:group]).astype(BF16)
        e_out[head] = e_low
        q_out[:, cols] = q_hat
        k_out[:, cols] = k_hat
        v_out[:, cols] = v_low
        inv_q.append(q_inv)
        inv_k.append(k_inv)
        inv_l.append(l_inv)
    aux[...] = lanes(columns + inv_l + inv_q + inv_k, rows)


def encoder_back_kernel(ids, g_own, g_other, wpt, e_in, q_in, k_in, v_in, aux, x_in, w, we, out, gmix):
    rows = q_in.shape[0]
    group = rows // 2
    width = q_in.shape[1]
    heads = width // HD
    half = w.shape[0]
    slab = half // 8
    tok = x_in.shape[2]
    m = ids[1]
    factor = HD**-0.5
    gemb = jnp.concatenate([g_own[...], g_other[...]])
    gatt = dot(gemb, wpt[...]).astype(BF16)
    for head in range(heads):
        cols = slice(head * HD, (head + 1) * HD)
        g_head = gatt[:, cols]
        q_hat, k_hat, v_low = q_in[:, cols], k_in[:, cols], v_in[:, cols]
        l_inv = aux[:, 2 + head : 3 + head]
        q_inv = aux[:, 2 + heads + head : 3 + heads + head]
        k_inv = aux[:, 2 + 2 * heads + head : 3 + 2 * heads + head]
        p = e_in[head].astype(F32) * l_inv
        gp = dot_nt(g_head, v_low)
        delta = jnp.sum(p * gp, axis=1, keepdims=True)
        gs = (p * (gp - delta)).astype(BF16)
        gq = dot(gs, k_hat.astype(BF16)) * factor
        gk = dot_tn(gs, q_hat.astype(BF16)) * factor
        gv = dot_tn(p.astype(BF16), g_head)
        gmix[:, head * HD : (head + 1) * HD] = norm_back(q_hat, q_inv, gq).astype(BF16)
        gmix[:, width + head * HD : width + (head + 1) * HD] = norm_back(k_hat, k_inv, gk).astype(BF16)
        gmix[:, 2 * width + head * HD : 2 * width + (head + 1) * HD] = gv.astype(BF16)
    glayer = dot_nt(gemb, we[...])
    centre, inverse = aux[:, 0:1], aux[:, 1:2]
    total = jnp.zeros((rows, 1), F32)
    total_dot = jnp.zeros((rows, 1), F32)
    for block in range(8):
        cols = slice(block * slab, (block + 1) * slab)
        g = dot_nt(gmix[...], w[cols, :])
        normed = (x_in[:, :, :, cols].reshape(rows, slab).astype(F32) - centre) * inverse
        total = total + jnp.sum(g, axis=1, keepdims=True)
        total_dot = total_dot + jnp.sum(g * normed, axis=1, keepdims=True)
        mine = jnp.where(block == m, 1.0, 0.0)
        value = (g * inverse + glayer * mine).astype(BF16).reshape(2, 8, tok, slab)
        out[:, :tok, cols] = value[0]
        out[:, tok:, cols] = value[1]
    sums = lanes((total, total_dot), rows).astype(BF16).reshape(2, 8, tok, 128)
    out[:, :tok, half:] = sums[0]
    out[:, tok:, half:] = sums[1]


def final_kernel(ids, own, other, x_own, out):
    s = ids[0]
    half = x_own.shape[1] // 2
    model = x_own.shape[1]
    normed, inverse = row_norm(x_own[...].astype(F32))
    mine, theirs = own[...], other[...].astype(F32)
    total = (mine[:, half : half + 1] + theirs[:, half : half + 1]) / model
    total_dot = (mine[:, half + 1 : half + 2] + theirs[:, half + 1 : half + 2]) / model
    first = jnp.where(s == 0, mine[:, :half], theirs[:, :half])
    second = jnp.where(s == 0, theirs[:, :half], mine[:, :half])
    out[:, :half] = (first - inverse * (total + normed[:, :half] * total_dot)).astype(BF16)
    out[:, half:] = (second - inverse * (total + normed[:, half:] * total_dot)).astype(BF16)


def head_norm_t(values):
    width, n = values.shape
    hat, inverse = row_norm(values.reshape(DHEADS, DHD, n), axis=1)
    return hat.reshape(width, n), inverse


def head_back_t(hat, inverse, gradient):
    width, n = hat.shape
    back = norm_back(
        hat.reshape(DHEADS, DHD, n), inverse, gradient.reshape(DHEADS, DHD, n), axis=1
    )
    return back.reshape(width, n)


def mask_kernel(ids, vis_col, pos_all, mask, w_t, w, pos_vis, hidden, k_t, v):
    npos, width = pos_all.shape
    nvis = vis_col.shape[0]
    hot = vis_col[...] == lax.broadcasted_iota(jnp.int32, (nvis, npos), 1)
    hot_f = jnp.where(hot, 1.0, 0.0)
    pos_vis[...] = dot(hot_f.astype(BF16), pos_all[...])
    hidden[...] = 1.0 - jnp.sum(hot_f, axis=0, keepdims=True)
    hat, _ = row_norm(pos_all[...].astype(F32) + mask[...].astype(F32))
    low = hat.astype(BF16)
    key_hat, _ = head_norm_t(dot_nt(w_t[width : 2 * width, :], low))
    k_t[...] = key_hat.astype(BF16)
    v[...] = dot(low, w[:, 2 * width :]).astype(BF16)


def decoder_kernel(
    ids, vis_row, emb_own, emb_other, pos_vis, hidden, km_t, vm, pos_own, mask, w_t, w, w_out, w_pix, target,
    pred, g_own, g_other, em_ref, ev_ref,
):
    npos_dev, width = pos_own.shape
    nvis = pos_vis.shape[0]
    group = nvis // 2
    member = ids[2]
    groups = width // 128
    per = 128 // DHD
    rows = per * npos_dev
    factor = DHD**-0.5
    emb = jnp.concatenate([emb_own[...], emb_other[...]])
    vis_hat, vis_inv = row_norm(emb.astype(F32) + pos_vis[...])
    vis_low = vis_hat.astype(BF16)
    kv_hat, kv_inv = head_norm_t(dot_nt(w_t[width : 2 * width, :], vis_low))
    kv_t = kv_hat.astype(BF16)
    vv = dot(vis_low, w[:, 2 * width :]).astype(BF16)
    position = lax.broadcasted_iota(jnp.int32, (npos_dev, nvis), 0) + member * npos_dev
    hot = jnp.where(position == vis_row[...], 1.0, 0.0)
    seen = jnp.sum(hot, axis=1, keepdims=True)
    hot_low = hot.astype(BF16)
    filled = dot(hot_low, emb) + (1.0 - seen) * mask[...].astype(F32)
    stream = filled + pos_own[...].astype(F32)
    own_hat, own_inv = row_norm(stream)
    q_t, q_inv = head_norm_t(dot_nt(w_t[:width, :], own_hat.astype(BF16)))
    q_low = q_t.T.astype(BF16)
    head_mask = (
        lax.broadcasted_iota(jnp.int32, (rows, 128), 0) // npos_dev
        == lax.broadcasted_iota(jnp.int32, (rows, 128), 1) // DHD
    )

    def spread(values):
        return jnp.where(head_mask, jnp.concatenate([values] * per, axis=0), jnp.zeros((), values.dtype))

    def gather(values):
        return jnp.sum(jnp.where(head_mask, values, 0.0).reshape(per, npos_dev, 128), axis=0)

    attended, inv_l = [], []
    for at in range(groups):
        cols = slice(at * 128, (at + 1) * 128)
        q_wide = spread(q_low[:, cols])
        em = jnp.exp2(dot(q_wide, km_t[cols, :]) * (factor * LOG2E)) * hidden[...]
        ev = jnp.exp2(dot(q_wide, kv_t[cols, :]) * (factor * LOG2E))
        l_inv = 1.0 / (jnp.sum(em, axis=1, keepdims=True) + jnp.sum(ev, axis=1, keepdims=True))
        em_low, ev_low = em.astype(BF16), ev.astype(BF16)
        em_ref[at] = em_low
        ev_ref[at] = ev_low
        attended.append(gather((dot(em_low, vm[:, cols]) + dot(ev_low, vv[:, cols])) * l_inv))
        inv_l.append(l_inv)
    att = jnp.concatenate(attended, axis=1)
    second = stream + dot(att.astype(BF16), w_out[...])
    final_hat, final_inv = row_norm(second)
    full = dot(final_hat.astype(BF16), w_pix[...])
    pred[...] = full.astype(BF16)
    error = jnp.where(seen > 0, 0.0, full - target[...].astype(F32)).astype(BF16)
    g_second = norm_back(final_hat, final_inv, dot_nt(error, w_pix[...]))
    g_att = dot_nt(g_second.astype(BF16), w_out[...]).astype(BF16)
    product = g_att.astype(F32) * att
    gq, gk_t, gv = [], [], []
    for at in range(groups):
        cols = slice(at * 128, (at + 1) * 128)
        q_wide = spread(q_low[:, cols])
        g_wide = spread(g_att[:, cols])
        delta = jnp.sum(spread(product[:, cols]), axis=1, keepdims=True)
        l_inv = inv_l[at]
        pv = ev_ref[at].astype(F32) * l_inv
        gs_v = (pv * (dot_nt(g_wide, vv[:, cols]) - delta)).astype(BF16)
        pm = em_ref[at].astype(F32) * l_inv
        gs_m = (pm * (dot_nt(g_wide, vm[:, cols]) - delta)).astype(BF16)
        gq.append(gather(dot_nt(gs_m, km_t[cols, :]) + dot_nt(gs_v, kv_t[cols, :])) * factor)
        gk_t.append(dot_tn(q_wide, gs_v) * factor)
        gv.append(dot_tn(pv.astype(BF16), g_wide).astype(BF16))
    gq_back = head_back_t(q_t, q_inv, jnp.concatenate(gq, axis=1).T).T.astype(BF16)
    g_stream_own = g_second + norm_back(own_hat, own_inv, dot_nt(gq_back, w[:, :width]))
    gk_back = head_back_t(kv_hat, kv_inv, jnp.concatenate(gk_t, axis=0)).T.astype(BF16)
    from_keys = dot_nt(gk_back, w[:, width : 2 * width]) + dot_nt(jnp.concatenate(gv, axis=1), w[:, 2 * width :])
    part = norm_back(vis_hat, vis_inv, from_keys) + dot_tn(hot_low, g_stream_own.astype(BF16))
    g_own[...] = part[:group]
    g_other[...] = part[group:].astype(BF16)


def shards(
    patches,
    vis_index,
    input_weight,
    output_weight,
    embed_weight,
    mask_token,
    position_table,
    decoder_input,
    decoder_output,
    pixel_weight,
    target,
):
    section = lax.axis_index("section")
    column = lax.axis_index("mp")
    member = lax.axis_index(("section", "mp"))
    copies = lax.axis_size("dp")
    ids = jnp.stack([section, column, member]).astype(jnp.int32)
    x_own = patches[0]
    tok, model = x_own.shape
    half = model // 2
    slab, dec_width = embed_weight.shape
    width = output_weight.shape[0]
    heads = width // HD
    group = 8 * tok
    nvis = 2 * group
    pos_dev = position_table.shape[0]
    npos = 16 * pos_dev

    def swap(value):
        return lax.ppermute(value, "section", [(0, 1), (1, 0)])

    def shift(value, by):
        return lax.ppermute(value, "mp", [(i, (i + by) % 8) for i in range(8)])

    def exchange(value, axis):
        return lax.all_to_all(value, axis, 0, 0, tiled=True)

    mine = lax.dynamic_slice_in_dim(x_own, section * half, half, 1)
    theirs = swap(lax.dynamic_slice_in_dim(x_own, (1 - section) * half, half, 1))
    dec_cols = dec_width // copies
    we_t = lax.dynamic_slice_in_dim(embed_weight, lax.axis_index("dp") * dec_cols, dec_cols, 1).T
    we_t = we_t.reshape(dec_cols // 32, 32, slab).transpose(1, 0, 2).reshape(32, -1)
    chunk = jnp.concatenate([jnp.concatenate([mine, theirs]), we_t], axis=1)
    chunks = {0: chunk}
    right = left = chunk
    for step in range(1, 5):
        right = shift(right, 1)
        chunks[-step] = right
        if step < 4:
            left = shift(left, -1)
            chunks[step] = left

    codes = jnp.zeros((16, dec_width), F32)
    codes = codes.at[0, :tok].set((vis_index[0] // 32).astype(F32)).at[1, :tok].set((vis_index[0] % 32).astype(F32))
    table = jnp.concatenate([position_table, codes.astype(BF16)])
    table = lax.all_gather(table, ("section", "mp"), axis=0, tiled=False)
    pos_all = table[:, :pos_dev].reshape(npos, dec_width)
    codes = table[:, pos_dev : pos_dev + 2, :tok].astype(jnp.int32)
    vis = (codes[:, 0] * 32 + codes[:, 1]).reshape(2, group)
    vis = jnp.where(section == 0, vis, vis[::-1]).reshape(nvis)

    w_in = input_weight.reshape(half, 3 * width)
    x_all, p_own, p_send, stats, wp_part, xp_own, xp_send = call(
        project_kernel,
        (
            sds((2, 8, tok, half), BF16),
            sds((nvis + 16, 3 * width), F32),
            sds((nvis + 16, 3 * width), BF16),
            sds((nvis, 128), F32),
            sds((dec_cols, width), F32),
            sds((group, dec_width), F32),
            sds((group, dec_width), BF16),
        ),
        ids,
        *[chunks[offset] for offset in OFFSETS],
        w_in,
        output_weight,
        embed_weight,
        scratch=(pltpu.VMEM((nvis + 16, half), BF16), pltpu.VMEM((dec_cols, half), BF16)),
    )
    p_other = swap(p_send)
    stats_other = swap(stats)
    wp_piece = (wp_part + swap(wp_part.astype(BF16)).astype(F32)).astype(BF16)
    wpt = exchange(jnp.broadcast_to(wp_piece, (copies, dec_cols, width)), "dp").reshape(dec_width, width)
    xp_other = swap(xp_send)

    att, e_enc, q_enc, k_enc, v_enc, aux = call(
        attend_kernel,
        (
            sds((group, width), BF16),
            sds((heads, nvis, nvis), BF16),
            sds((nvis, width), F32),
            sds((nvis, width), F32),
            sds((nvis, width), BF16),
            sds((nvis, 128), F32),
        ),
        ids,
        p_own,
        p_other,
        stats,
        stats_other,
    )
    embed_part = dot_nt(att, wpt) + xp_own + xp_other.astype(F32)

    def reduce_and_gather(part):
        received = exchange(part.astype(BF16).reshape(8, tok, dec_width), "mp")
        total = jnp.sum(received.astype(F32), axis=0).astype(BF16)
        gathered = exchange(jnp.broadcast_to(total, (8, tok, dec_width)), "mp").reshape(group, dec_width)
        return gathered, swap(gathered)

    emb_own, emb_other = reduce_and_gather(embed_part)

    w_dec = decoder_input.reshape(dec_width, 3 * dec_width)
    w_dec_t = w_dec.T
    mask_row = mask_token.reshape(1, dec_width)
    pos_vis, hidden, km_t, vm = call(
        mask_kernel,
        (
            sds((nvis, dec_width), F32),
            sds((1, npos), F32),
            sds((dec_width, npos), BF16),
            sds((npos, dec_width), BF16),
        ),
        ids,
        vis.reshape(nvis, 1),
        pos_all,
        mask_row,
        w_dec_t,
        w_dec,
    )
    groups = dec_width // 128
    rows = (128 // DHD) * pos_dev
    prediction, g_own, g_send = call(
        decoder_kernel,
        (
            sds((pos_dev, target.shape[2]), BF16),
            sds((group, dec_width), F32),
            sds((group, dec_width), BF16),
        ),
        ids,
        vis.reshape(1, nvis),
        emb_own,
        emb_other,
        pos_vis,
        hidden,
        km_t,
        vm,
        position_table,
        mask_row,
        w_dec_t,
        w_dec,
        decoder_output,
        pixel_weight,
        target[0],
        scratch=(pltpu.VMEM((groups, rows, npos), BF16), pltpu.VMEM((groups, rows, nvis), BF16)),
    )
    ge_own, ge_other = reduce_and_gather(g_own + swap(g_send).astype(F32))

    parts = call(
        encoder_back_kernel,
        sds((8, 2 * tok, half + 128), BF16),
        ids,
        ge_own,
        ge_other,
        wpt,
        e_enc,
        q_enc,
        k_enc,
        v_enc,
        aux,
        x_all,
        w_in,
        embed_weight,
        scratch=(pltpu.VMEM((nvis, 3 * width), BF16),),
    )

    def part(offset):
        return lax.dynamic_index_in_dim(parts, (column + offset) % 8, 0, False).astype(F32)

    right, left = part(4).astype(BF16), part(-3).astype(BF16)
    for step in range(3):
        moved_right, moved_left = shift(right, 1), shift(left, -1)
        right = (moved_right.astype(F32) + part(3 - step)).astype(BF16)
        if step < 2:
            left = (moved_left.astype(F32) + part(-2 + step)).astype(BF16)
    total = shift(right, 1).astype(F32) + moved_left.astype(F32) + part(0)
    patch_grad = call(
        final_kernel,
        sds((tok, model), BF16),
        ids,
        total[:tok],
        swap(total[tok:].astype(BF16)),
        x_own,
    )
    return (prediction[None], patch_grad[None])


def solution(mesh):
    group = ("section", "mp")
    in_specs = (
        P("dp", group, None),
        P("dp", group),
        P("section", None, "mp"),
        P("mp", "section"),
        P(group, None),
        P(),
        P(group, None),
        P(),
        P(),
        P(),
        P("dp", group, None),
    )
    out_specs = (P("dp", group, None), P("dp", group, None))
    return jax.shard_map(shards, mesh=mesh, in_specs=in_specs, out_specs=out_specs, check_vma=False)
```

```python
import math

import jax
import jax.numpy as jnp
from jax import lax
from jax.experimental import pallas as pl
from jax.experimental.pallas import tpu as pltpu
from jax.sharding import PartitionSpec as P

HD = 128
DHEADS = 16
DHD = 32
EPSILON = 1e-06
LOG2E = math.log2(math.e)
F32 = jnp.float32
BF16 = jnp.bfloat16
OFFSETS = (0, -1, 1, -2, 2, -3, 3, -4)


def dot(a, b):
    return lax.dot_general(a, b, (((1,), (0,)), ((), ())), preferred_element_type=F32)


def dot_nt(a, b):
    return lax.dot_general(a, b, (((1,), (1,)), ((), ())), preferred_element_type=F32)


def dot_tn(a, b):
    return lax.dot_general(a, b, (((0,), (0,)), ((), ())), preferred_element_type=F32)


def row_norm(values, axis=-1):
    centre = jnp.mean(values, axis=axis, keepdims=True)
    centered = values - centre
    inverse = lax.rsqrt(jnp.mean(centered * centered, axis=axis, keepdims=True) + EPSILON)
    return centered * inverse, inverse


def norm_back(normed, inverse, gradient, axis=-1):
    mean_grad = jnp.mean(gradient, axis=axis, keepdims=True)
    mean_dot = jnp.mean(gradient * normed, axis=axis, keepdims=True)
    return inverse * (gradient - mean_grad - normed * mean_dot)


def lanes(columns, rows):
    lane = lax.broadcasted_iota(jnp.int32, (rows, 128), 1)
    out = jnp.zeros((rows, 128), F32)
    for at, column in enumerate(columns):
        out = jnp.where(lane == at, column, out)
    return out


def call(kernel, out_shape, *args, scratch=(), far=(), limit=24):
    specs = [pl.BlockSpec(memory_space=pltpu.SMEM)]
    for at in range(1, len(args)):
        specs.append(pl.BlockSpec(memory_space=pl.ANY if at in far else pltpu.VMEM))
    return pl.pallas_call(
        kernel,
        out_shape=out_shape,
        in_specs=specs,
        out_specs=jax.tree.map(lambda _: pl.BlockSpec(memory_space=pltpu.VMEM), out_shape),
        scratch_shapes=list(scratch),
        compiler_params=pltpu.CompilerParams(vmem_limit_bytes=limit * 2**20),
    )(*args)


def sds(shape, dtype):
    return jax.ShapeDtypeStruct(shape, dtype)


def fetch(w, held, sems):
    copies = [pltpu.make_async_copy(w.at[at], held.at[at], sems.at[at]) for at in range(3)]
    for copy in copies:
        copy.start()
    return copies


def fold_kernel(ids, pieces, wo, out, out_low):
    slab = wo.shape[1] // 8
    total = dot_nt(pieces[0], wo[:, :slab])
    for at in range(1, 8):
        total = total + dot_nt(pieces[at], wo[:, at * slab : (at + 1) * slab])
    out[...] = total
    out_low[...] = total.astype(BF16)


def project_kernel(ids, *refs):
    chunks = refs[:8]
    w, we = refs[8:10]
    x_out, p_own, p_send, stats, xp_own, xp_send = refs[10:16]
    xc, held, sems = refs[16:]
    copies = fetch(w, held, sems)
    half = held.shape[1]
    width = held.shape[2]
    slab = half // 8
    tok = x_out.shape[2]
    group = 8 * tok
    m = ids[1]
    for chunk, offset in zip(chunks, OFFSETS):
        at = lax.rem(m + offset + 8, 8)
        value = chunk[...]
        x_out[0, at] = value[:tok]
        x_out[1, at] = value[tok:]
        wide = value.astype(F32)
        centre = jnp.mean(wide, axis=1, keepdims=True)
        centered = wide - centre
        spread = jnp.sum(centered * centered, axis=1, keepdims=True)
        low = centered.astype(BF16)
        both = lanes((centre, spread), 2 * tok)
        row = pl.multiple_of(at * tok, tok)
        xc[pl.ds(row, tok), :] = low[:tok]
        xc[pl.ds(row + group, tok), :] = low[tok:]
        stats[pl.ds(row, tok), :] = both[:tok]
        stats[pl.ds(row + group, tok), :] = both[tok:]
    xc[2 * group :, :] = jnp.ones((16, half), BF16)
    for at in range(3):
        copies[at].wait()
        product = dot(xc[...], held[at])
        p_own[:, at * width : (at + 1) * width] = product
        p_send[:, at * width : (at + 1) * width] = product.astype(BF16)
    column = pl.multiple_of(m * slab, 128)
    raw = jnp.concatenate(
        [x_out[0, :, :, pl.ds(column, slab)], x_out[1, :, :, pl.ds(column, slab)]]
    ).reshape(2 * group, slab)
    part = dot(raw, we[...])
    xp_own[...] = part[:group]
    xp_send[...] = part[group:].astype(BF16)


def attend_kernel(ids, p_own, p_other, st_own, st_other, att, e_out, q_out, k_out, v_out, aux):
    rows = st_own.shape[0]
    group = rows // 2
    width = p_own.shape[1] // 3
    heads = width // HD
    model = 2 * 8 * width
    stats_other = jnp.concatenate([st_other[group:, :], st_other[:group, :]])
    m_own, s_own = st_own[:, 0:1], st_own[:, 1:2]
    m_other, s_other = stats_other[:, 0:1], stats_other[:, 1:2]
    gap = (m_own - m_other) * 0.5
    centre = (m_own + m_other) * 0.5
    inverse = lax.rsqrt((s_own + s_other) / model + gap * gap + EPSILON)
    slope = p_own[rows : rows + 1, :] - p_other[rows : rows + 1, :].astype(F32)
    columns = [centre, inverse]
    inv_q, inv_k, inv_l = [], [], []
    factor = LOG2E * HD**-0.5

    def mixture(at):
        cols = slice(at * HD, (at + 1) * HD)
        other = jnp.concatenate([p_other[group:rows, cols], p_other[:group, cols]]).astype(F32)
        return inverse * (p_own[:rows, cols] + other + gap * slope[:, cols])

    for head in range(heads):
        cols = slice(head * HD, (head + 1) * HD)
        q_hat, q_inv = row_norm(mixture(head))
        k_hat, k_inv = row_norm(mixture(heads + head))
        v_low = mixture(2 * heads + head).astype(BF16)
        e = jnp.exp2(dot_nt(q_hat.astype(BF16), k_hat.astype(BF16)) * factor)
        l_inv = 1.0 / jnp.sum(e, axis=1, keepdims=True)
        e_low = e.astype(BF16)
        att[:, cols] = (dot(e_low[:group], v_low) * l_inv[:group]).astype(BF16)
        e_out[head] = e_low
        q_out[:, cols] = q_hat
        k_out[:, cols] = k_hat
        v_out[:, cols] = v_low
        inv_q.append(q_inv)
        inv_k.append(k_inv)
        inv_l.append(l_inv)
    aux[...] = lanes(columns + inv_l + inv_q + inv_k, rows)


def feature_parts(rows, gm, glayer, x_rows, centre, inverse, held, m, store):
    half, width = held.shape[1:]
    slab = half // 8
    total = jnp.zeros((rows, 1), F32)
    total_dot = jnp.zeros((rows, 1), F32)
    for block in range(8):
        cols = slice(block * slab, (block + 1) * slab)
        g = dot_nt(gm[:, :width], held[0, cols, :])
        g = g + dot_nt(gm[:, width : 2 * width], held[1, cols, :])
        g = g + dot_nt(gm[:, 2 * width :], held[2, cols, :])
        normed = (x_rows(cols).astype(F32) - centre) * inverse
        total = total + jnp.sum(g, axis=1, keepdims=True)
        total_dot = total_dot + jnp.sum(g * normed, axis=1, keepdims=True)
        mine = jnp.where(block == m, 1.0, 0.0)
        store(cols, (g * inverse + glayer * mine).astype(BF16))
    store(slice(half, half + 128), lanes((total, total_dot), rows).astype(BF16))


def encoder_back_kernel(
    ids, g_own, g_other, wpt, e_in, q_in, k_in, v_in, aux, x_in, w, we, first, gmix, glayer_out, few, held, sems
):
    copies = fetch(w, held, sems)
    rows = q_in.shape[0]
    width = q_in.shape[1]
    heads = width // HD
    tok = x_in.shape[2]
    group = 8 * tok
    m = ids[1]
    factor = HD**-0.5
    gemb = jnp.concatenate([g_own[...], g_other[...]])
    gatt = dot(gemb, wpt[...]).astype(BF16)
    for head in range(heads):
        cols = slice(head * HD, (head + 1) * HD)
        g_head = gatt[:, cols]
        q_hat, k_hat, v_low = q_in[:, cols], k_in[:, cols], v_in[:, cols]
        l_inv = aux[:, 2 + head : 3 + head]
        q_inv = aux[:, 2 + heads + head : 3 + heads + head]
        k_inv = aux[:, 2 + 2 * heads + head : 3 + 2 * heads + head]
        p = e_in[head].astype(F32) * l_inv
        gp = dot_nt(g_head, v_low)
        delta = jnp.sum(p * gp, axis=1, keepdims=True)
        gs = (p * (gp - delta)).astype(BF16)
        gq = dot(gs, k_hat.astype(BF16)) * factor
        gk = dot_tn(gs, q_hat.astype(BF16)) * factor
        gv = dot_tn(p.astype(BF16), g_head)
        gmix[:, head * HD : (head + 1) * HD] = norm_back(q_hat, q_inv, gq).astype(BF16)
        gmix[:, width + head * HD : width + (head + 1) * HD] = norm_back(k_hat, k_inv, gk).astype(BF16)
        gmix[:, 2 * width + head * HD : 2 * width + (head + 1) * HD] = gv.astype(BF16)
    glayer_out[...] = dot_nt(gemb, we[...])
    ats = [lax.rem(m + 4, 8), lax.rem(m + 5, 8)]
    blocks = [(rel, at) for at in ats for rel in range(2)]

    def rows_of(ref):
        return jnp.concatenate(
            [ref[pl.ds(pl.multiple_of(at * tok, tok) + rel * group, tok), :] for rel, at in blocks]
        )

    few[...] = rows_of(gmix)
    some = rows_of(aux)

    def x_rows(cols):
        return jnp.concatenate([x_in[rel, at, :, cols] for rel, at in blocks])

    def store(cols, value):
        first[:, cols] = value

    for copy in copies:
        copy.wait()
    feature_parts(4 * tok, few[...], rows_of(glayer_out), x_rows, some[:, 0:1], some[:, 1:2], held, m, store)


def feature_kernel(ids, gmix, glayer, aux, x_in, w, out, held, sems):
    copies = fetch(w, held, sems)
    tok = x_in.shape[2]
    rows = gmix.shape[0]

    def x_rows(cols):
        return x_in[:, :, :, cols].reshape(rows, cols.stop - cols.start)

    def store(cols, value):
        value = value.reshape(2, 8, tok, cols.stop - cols.start)
        out[:, :tok, cols] = value[0]
        out[:, tok:, cols] = value[1]

    for copy in copies:
        copy.wait()
    feature_parts(rows, gmix[...], glayer[...], x_rows, aux[:, 0:1], aux[:, 1:2], held, ids[1], store)


def final_kernel(ids, own, other, x_own, out):
    s = ids[0]
    half = x_own.shape[1] // 2
    model = x_own.shape[1]
    normed, inverse = row_norm(x_own[...].astype(F32))
    mine, theirs = own[...], other[...].astype(F32)
    total = (mine[:, half : half + 1] + theirs[:, half : half + 1]) / model
    total_dot = (mine[:, half + 1 : half + 2] + theirs[:, half + 1 : half + 2]) / model
    first = jnp.where(s == 0, mine[:, :half], theirs[:, :half])
    second = jnp.where(s == 0, theirs[:, :half], mine[:, :half])
    out[:, :half] = (first - inverse * (total + normed[:, :half] * total_dot)).astype(BF16)
    out[:, half:] = (second - inverse * (total + normed[:, half:] * total_dot)).astype(BF16)


def head_norm_t(values):
    width, n = values.shape
    hat, inverse = row_norm(values.reshape(DHEADS, DHD, n), axis=1)
    return hat.reshape(width, n), inverse


def head_back_t(hat, inverse, gradient):
    width, n = hat.shape
    back = norm_back(
        hat.reshape(DHEADS, DHD, n), inverse, gradient.reshape(DHEADS, DHD, n), axis=1
    )
    return back.reshape(width, n)


def mask_kernel(ids, table, mask, w, pos_vis, vis_row, hidden, k_t, v, wq_t, wk_t):
    members, pos_dev = table.shape[0], table.shape[1] - 16
    npos, width = members * pos_dev, table.shape[2]
    nvis = vis_row.shape[1]
    pos_all = table[:, :pos_dev, :].reshape(npos, width)
    codes = jnp.sum(table[:, pos_dev:, :].astype(F32), axis=0)
    row = codes[0:1, :nvis] * 32.0 + codes[1:2, :nvis]
    other = jnp.concatenate([row[:, nvis // 2 :], row[:, : nvis // 2]], axis=1)
    vis = jnp.where(ids[0] == 0, row, other).astype(jnp.int32)
    vis_row[...] = vis
    hot = jnp.where(lax.broadcasted_iota(jnp.int32, (npos, nvis), 0) == vis, 1.0, 0.0).astype(BF16)
    pos_vis[...] = dot_tn(hot, pos_all)
    hidden[...] = 1.0 - dot_nt(jnp.ones((16, nvis), BF16), hot)[0:1, :]
    hat, _ = row_norm(pos_all.astype(F32) + mask[...].astype(F32))
    low = hat.astype(BF16)
    wq_t[...] = w[0].T
    wk_t[...] = w[1].T
    key_hat, _ = head_norm_t(dot_nt(wk_t[...], low))
    k_t[...] = key_hat.astype(BF16)
    v[...] = dot(low, w[2]).astype(BF16)


def decoder_kernel(
    ids, vis_row, emb_own, emb_other, pos_vis, hidden, km_t, vm, pos_own, mask, wq_t, wk_t, w, w_out, w_pix, target,
    pred, g_own, g_other, em_ref, ev_ref,
):
    npos_dev, width = pos_own.shape
    nvis = pos_vis.shape[0]
    group = nvis // 2
    member = ids[2]
    groups = width // 128
    per = 128 // DHD
    rows = per * npos_dev
    factor = DHD**-0.5
    emb = jnp.concatenate([emb_own[...], emb_other[...]])
    vis_hat, vis_inv = row_norm(emb.astype(F32) + pos_vis[...])
    vis_low = vis_hat.astype(BF16)
    kv_hat, kv_inv = head_norm_t(dot_nt(wk_t[...], vis_low))
    kv_t = kv_hat.astype(BF16)
    vv = dot(vis_low, w[2]).astype(BF16)
    position = lax.broadcasted_iota(jnp.int32, (npos_dev, nvis), 0) + member * npos_dev
    hot = jnp.where(position == vis_row[...], 1.0, 0.0)
    seen = jnp.sum(hot, axis=1, keepdims=True)
    hot_low = hot.astype(BF16)
    filled = dot(hot_low, emb) + (1.0 - seen) * mask[...].astype(F32)
    stream = filled + pos_own[...].astype(F32)
    own_hat, own_inv = row_norm(stream)
    q_t, q_inv = head_norm_t(dot_nt(wq_t[...], own_hat.astype(BF16)))
    q_low = q_t.T.astype(BF16)
    head_mask = (
        lax.broadcasted_iota(jnp.int32, (rows, 128), 0) // npos_dev
        == lax.broadcasted_iota(jnp.int32, (rows, 128), 1) // DHD
    )

    def spread(values):
        return jnp.where(head_mask, jnp.concatenate([values] * per, axis=0), jnp.zeros((), values.dtype))

    def gather(values):
        return jnp.sum(jnp.where(head_mask, values, 0.0).reshape(per, npos_dev, 128), axis=0)

    attended, inv_l = [], []
    for at in range(groups):
        cols = slice(at * 128, (at + 1) * 128)
        q_wide = spread(q_low[:, cols])
        em = jnp.exp2(dot(q_wide, km_t[cols, :]) * (factor * LOG2E)) * hidden[...]
        ev = jnp.exp2(dot(q_wide, kv_t[cols, :]) * (factor * LOG2E))
        l_inv = 1.0 / (jnp.sum(em, axis=1, keepdims=True) + jnp.sum(ev, axis=1, keepdims=True))
        em_low, ev_low = em.astype(BF16), ev.astype(BF16)
        em_ref[at] = em_low
        ev_ref[at] = ev_low
        attended.append(gather((dot(em_low, vm[:, cols]) + dot(ev_low, vv[:, cols])) * l_inv))
        inv_l.append(l_inv)
    att = jnp.concatenate(attended, axis=1)
    second = stream + dot(att.astype(BF16), w_out[...])
    final_hat, final_inv = row_norm(second)
    full = dot(final_hat.astype(BF16), w_pix[...])
    pred[...] = full.astype(BF16)
    error = jnp.where(seen > 0, 0.0, full - target[...].astype(F32)).astype(BF16)
    g_second = norm_back(final_hat, final_inv, dot_nt(error, w_pix[...]))
    g_att = dot_nt(g_second.astype(BF16), w_out[...]).astype(BF16)
    product = g_att.astype(F32) * att
    gq, gk_t, gv = [], [], []
    for at in range(groups):
        cols = slice(at * 128, (at + 1) * 128)
        q_wide = spread(q_low[:, cols])
        g_wide = spread(g_att[:, cols])
        delta = jnp.sum(spread(product[:, cols]), axis=1, keepdims=True)
        l_inv = inv_l[at]
        pv = ev_ref[at].astype(F32) * l_inv
        gs_v = (pv * (dot_nt(g_wide, vv[:, cols]) - delta)).astype(BF16)
        pm = em_ref[at].astype(F32) * l_inv
        gs_m = (pm * (dot_nt(g_wide, vm[:, cols]) - delta)).astype(BF16)
        gq.append(gather(dot_nt(gs_m, km_t[cols, :]) + dot_nt(gs_v, kv_t[cols, :])) * factor)
        gk_t.append(dot_tn(q_wide, gs_v) * factor)
        gv.append(dot_tn(pv.astype(BF16), g_wide).astype(BF16))
    gq_back = head_back_t(q_t, q_inv, jnp.concatenate(gq, axis=1).T).T.astype(BF16)
    g_stream_own = g_second + norm_back(own_hat, own_inv, dot_nt(gq_back, w[0]))
    gk_back = head_back_t(kv_hat, kv_inv, jnp.concatenate(gk_t, axis=0)).T.astype(BF16)
    from_keys = dot_nt(gk_back, w[1]) + dot_nt(jnp.concatenate(gv, axis=1), w[2])
    part = norm_back(vis_hat, vis_inv, from_keys) + dot_tn(hot_low, g_stream_own.astype(BF16))
    g_own[...] = part[:group]
    g_other[...] = part[group:].astype(BF16)


def shards(
    patches,
    vis_index,
    input_weight,
    output_weight,
    embed_weight,
    mask_token,
    position_table,
    decoder_input,
    decoder_output,
    pixel_weight,
    target,
):
    section = lax.axis_index("section")
    column = lax.axis_index("mp")
    member = lax.axis_index(("section", "mp"))
    copies = lax.axis_size("dp")
    ids = jnp.stack([section, column, member]).astype(jnp.int32)
    x_own = patches[0]
    tok, model = x_own.shape
    half = model // 2
    slab, dec_width = embed_weight.shape
    width = output_weight.shape[0]
    heads = width // HD
    group = 8 * tok
    nvis = 2 * group
    pos_dev = position_table.shape[0]
    npos = 16 * pos_dev

    def swap(value):
        return lax.ppermute(value, "section", [(0, 1), (1, 0)])

    def shift(value, by):
        return lax.ppermute(value, "mp", [(i, (i + by) % 8) for i in range(8)])

    def exchange(value, axis):
        return lax.all_to_all(value, axis, 0, 0, tiled=True)

    spread = 4 if copies % 4 == 0 else 1
    dec_cols = dec_width // spread
    place = lax.axis_index("dp") % spread
    pieces = lax.all_gather(
        lax.dynamic_slice_in_dim(embed_weight, place * dec_cols, dec_cols, 1).T, "mp", axis=0, tiled=False
    )

    mine = lax.dynamic_slice_in_dim(x_own, section * half, half, 1)
    theirs = swap(lax.dynamic_slice_in_dim(x_own, (1 - section) * half, half, 1))
    chunk = jnp.concatenate([mine, theirs])
    chunks = {0: chunk}
    right = left = chunk
    for step in range(1, 5):
        right = shift(right, 1)
        chunks[-step] = right
        if step < 4:
            left = shift(left, -1)
            chunks[step] = left

    index, _, _ = lax.optimization_barrier((vis_index[0], chunks[-1], pieces))
    row = jnp.zeros((nvis,), jnp.int32)
    row = lax.dynamic_update_slice_in_dim(row, index, member * tok, 0)
    codes = jnp.pad(jnp.stack([row // 32, row % 32]), ((0, 14), (0, dec_width - nvis)))
    table = jnp.concatenate([position_table, codes.astype(BF16)])
    table = lax.all_gather(table, ("section", "mp"), axis=0, tiled=False)

    w_in = input_weight.transpose(1, 0, 2)
    held = (pltpu.VMEM(w_in.shape, BF16), pltpu.SemaphoreType.DMA((3,)))
    wp_part, wp_send = call(
        fold_kernel, (sds((dec_cols, width), F32), sds((dec_cols, width), BF16)), ids, pieces, output_weight
    )
    x_all, p_own, p_send, stats, xp_own, xp_send = call(
        project_kernel,
        (
            sds((2, 8, tok, half), BF16),
            sds((nvis + 16, 3 * width), F32),
            sds((nvis + 16, 3 * width), BF16),
            sds((nvis, 128), F32),
            sds((group, dec_width), F32),
            sds((group, dec_width), BF16),
        ),
        ids,
        *[chunks[offset] for offset in OFFSETS],
        w_in,
        embed_weight,
        scratch=(pltpu.VMEM((nvis + 16, half), BF16),) + held,
        far=(9,),
    )
    p_other = swap(p_send)
    stats_other = swap(stats)
    wp_piece = (wp_part + swap(wp_send).astype(F32)).astype(BF16)
    wpt = lax.all_to_all(
        jnp.broadcast_to(wp_piece, (spread, dec_cols, width)),
        "dp",
        0,
        0,
        tiled=True,
        axis_index_groups=[[y * spread + x for x in range(spread)] for y in range(copies // spread)],
    ).reshape(dec_width, width)
    xp_other = swap(xp_send)

    att, e_enc, q_enc, k_enc, v_enc, aux = call(
        attend_kernel,
        (
            sds((group, width), BF16),
            sds((heads, nvis, nvis), BF16),
            sds((nvis, width), F32),
            sds((nvis, width), F32),
            sds((nvis, width), BF16),
            sds((nvis, 128), F32),
        ),
        ids,
        p_own,
        p_other,
        stats,
        stats_other,
    )
    embed_part = dot_nt(att, wpt) + xp_own + xp_other.astype(F32)

    def reduce_and_gather(part):
        received = exchange(part.astype(BF16).reshape(8, tok, dec_width), "mp")
        total = jnp.sum(received.astype(F32), axis=0).astype(BF16)
        gathered = exchange(jnp.broadcast_to(total, (8, tok, dec_width)), "mp").reshape(group, dec_width)
        return gathered, swap(gathered)

    w_dec = decoder_input.transpose(1, 0, 2)
    mask_row = mask_token.reshape(1, dec_width)
    table, embed_part = lax.optimization_barrier((table, embed_part))
    pos_vis, vis_row, hidden, km_t, vm, wq_t, wk_t = call(
        mask_kernel,
        (
            sds((nvis, dec_width), F32),
            sds((1, nvis), jnp.int32),
            sds((1, npos), F32),
            sds((dec_width, npos), BF16),
            sds((npos, dec_width), BF16),
            sds((dec_width, dec_width), BF16),
            sds((dec_width, dec_width), BF16),
        ),
        ids,
        table,
        mask_row,
        w_dec,
    )
    emb_own, emb_other = reduce_and_gather(embed_part)

    groups = dec_width // 128
    rows = (128 // DHD) * pos_dev
    prediction, g_own, g_send = call(
        decoder_kernel,
        (
            sds((pos_dev, target.shape[2]), BF16),
            sds((group, dec_width), F32),
            sds((group, dec_width), BF16),
        ),
        ids,
        vis_row,
        emb_own,
        emb_other,
        pos_vis,
        hidden,
        km_t,
        vm,
        position_table,
        mask_row,
        wq_t,
        wk_t,
        w_dec,
        decoder_output,
        pixel_weight,
        target[0],
        scratch=(pltpu.VMEM((groups, rows, npos), BF16), pltpu.VMEM((groups, rows, nvis), BF16)),
    )
    ge_own, ge_other = reduce_and_gather(g_own + swap(g_send).astype(F32))

    first, gmix, glayer = call(
        encoder_back_kernel,
        (
            sds((4 * tok, half + 128), BF16),
            sds((nvis, 3 * width), BF16),
            sds((nvis, slab), F32),
        ),
        ids,
        ge_own,
        ge_other,
        wpt,
        e_enc,
        q_enc,
        k_enc,
        v_enc,
        aux,
        x_all,
        w_in,
        embed_weight,
        scratch=(pltpu.VMEM((4 * tok, 3 * width), BF16),) + held,
        far=(10,),
    )
    parts = call(
        feature_kernel,
        sds((8, 2 * tok, half + 128), BF16),
        ids,
        gmix,
        glayer,
        aux,
        x_all,
        w_in,
        scratch=held,
        far=(5,),
    )

    def part(offset):
        return lax.dynamic_index_in_dim(parts, (column + offset) % 8, 0, False).astype(F32)

    right, left = first[: 2 * tok], first[2 * tok :]
    for step in range(3):
        moved_right, moved_left = shift(right, 1), shift(left, -1)
        right = (moved_right.astype(F32) + part(3 - step)).astype(BF16)
        if step < 2:
            left = (moved_left.astype(F32) + part(-2 + step)).astype(BF16)
    total = shift(right, 1).astype(F32) + moved_left.astype(F32) + part(0)
    patch_grad = call(
        final_kernel,
        sds((tok, model), BF16),
        ids,
        total[:tok],
        swap(total[tok:].astype(BF16)),
        x_own,
    )
    return (prediction[None], patch_grad[None])


def solution(mesh):
    group = ("section", "mp")
    in_specs = (
        P("dp", group, None),
        P("dp", group),
        P("section", None, "mp"),
        P("mp", "section"),
        P(group, None),
        P(),
        P(group, None),
        P(),
        P(),
        P(),
        P("dp", group, None),
    )
    out_specs = (P("dp", group, None), P("dp", group, None))
    return jax.shard_map(shards, mesh=mesh, in_specs=in_specs, out_specs=out_specs, check_vma=False)
```

```python
import math

import jax
import jax.numpy as jnp
from jax import lax
from jax.experimental import pallas as pl
from jax.experimental.pallas import tpu as pltpu
from jax.sharding import PartitionSpec as P

HD = 128
DHEADS = 16
DHD = 32
EPSILON = 1e-06
LOG2E = math.log2(math.e)
F32 = jnp.float32
BF16 = jnp.bfloat16
OFFSETS = (0, -1, 1, -2, 2, -3, 3, -4)


def dot(a, b):
    return lax.dot_general(a, b, (((1,), (0,)), ((), ())), preferred_element_type=F32)


def dot_nt(a, b):
    return lax.dot_general(a, b, (((1,), (1,)), ((), ())), preferred_element_type=F32)


def dot_tn(a, b):
    return lax.dot_general(a, b, (((0,), (0,)), ((), ())), preferred_element_type=F32)


def row_norm(values, axis=-1):
    centre = jnp.mean(values, axis=axis, keepdims=True)
    centered = values - centre
    inverse = lax.rsqrt(jnp.mean(centered * centered, axis=axis, keepdims=True) + EPSILON)
    return centered * inverse, inverse


def norm_back(normed, inverse, gradient, axis=-1):
    mean_grad = jnp.mean(gradient, axis=axis, keepdims=True)
    mean_dot = jnp.mean(gradient * normed, axis=axis, keepdims=True)
    return inverse * (gradient - mean_grad - normed * mean_dot)


def lanes(columns, rows):
    lane = lax.broadcasted_iota(jnp.int32, (rows, 128), 1)
    out = jnp.zeros((rows, 128), F32)
    for at, column in enumerate(columns):
        out = jnp.where(lane == at, column, out)
    return out


def call(kernel, outs, *args, scratch=(), far=(), far_out=(), copies=0, limit=24):
    specs = [pl.BlockSpec(memory_space=pltpu.SMEM)]
    for at in range(1, len(args)):
        specs.append(pl.BlockSpec(memory_space=pltpu.HBM if at in far else pltpu.VMEM))
    out_specs = [
        pl.BlockSpec(memory_space=pltpu.HBM if at in far_out else pltpu.VMEM) for at in range(len(outs))
    ]
    scratch = [pltpu.VMEM(shape.shape, shape.dtype) for shape in scratch]
    if copies:
        scratch.append(pltpu.SemaphoreType.DMA((copies,)))
    return pl.pallas_call(
        kernel,
        out_shape=tuple(outs),
        in_specs=specs,
        out_specs=tuple(out_specs),
        scratch_shapes=scratch,
        compiler_params=pltpu.CompilerParams(vmem_limit_bytes=limit * 2**20),
    )(*args)


def start(sems, first, *pairs):
    copies = [
        pltpu.make_async_copy(source, target, sems.at[first + at]) for at, (source, target) in enumerate(pairs)
    ]
    for copy in copies:
        copy.start()
    return copies


def finish(copies):
    for copy in copies:
        copy.wait()


def sds(shape, dtype):
    return jax.ShapeDtypeStruct(shape, dtype)


def fold_kernel(ids, *refs):
    chunks, wo, out, wt = refs[:8], refs[8], refs[9], refs[10]
    half = wo.shape[1]
    slab = half // 8
    for chunk, offset in zip(chunks, OFFSETS):
        column = pl.multiple_of(lax.rem(ids[1] + offset + 8, 8) * slab, 128)
        for piece in range(wt.shape[0] // 32):
            wt[piece * 32 : piece * 32 + 32, pl.ds(column, slab)] = chunk[
                :, half + piece * slab : half + (piece + 1) * slab
            ]
    total = dot_nt(wt[...], wo[...]).astype(BF16)
    for at in range(out.shape[0]):
        out[at] = total


def split3(values):
    first = values.astype(BF16).astype(F32)
    second = (values - first).astype(BF16).astype(F32)
    return [first, second, values - first - second]


def project_kernel(ids, *refs):
    chunks = refs[:8]
    w, we = refs[8:10]
    x_out, p_own, p_send, xp_own, xp_send = refs[10:15]
    xs, xc, held, xp, sems = refs[15:]
    loads = start(sems, 0, *[(w.at[at], held.at[at]) for at in range(3)])
    half, width = held.shape[1:]
    slab = half // 8
    tok = xs.shape[2]
    group = 8 * tok
    m = ids[1]
    for chunk, offset in zip(chunks, OFFSETS):
        at = lax.rem(m + offset + 8, 8)
        value = chunk[:, :half]
        xs[0, at] = value[:tok]
        xs[1, at] = value[tok:]
        wide = value.astype(F32)
        centre = jnp.mean(wide, axis=1, keepdims=True)
        centered = wide - centre
        spread = jnp.sum(centered * centered, axis=1, keepdims=True)
        low = centered.astype(BF16)
        own = lanes((centre, spread), 2 * tok)
        send = lanes(split3(centre) + split3(spread), 2 * tok).astype(BF16)
        row = pl.multiple_of(at * tok, tok)
        for rel in range(2):
            part = slice(rel * tok, (rel + 1) * tok)
            xc[pl.ds(row + rel * group, tok), :] = low[part]
            p_own[pl.ds(row + rel * group, tok), 3 * width :] = own[part]
            p_send[pl.ds(row + rel * group, tok), 3 * width :] = send[part]
    stores = start(sems, 3, (xs, x_out))
    xc[2 * group :, :] = jnp.ones((16, half), BF16)
    p_own[2 * group :, 3 * width :] = jnp.zeros((16, 128), F32)
    p_send[2 * group :, 3 * width :] = jnp.zeros((16, 128), BF16)
    for at in range(3):
        loads[at].wait()
        product = dot(xc[...], held[at])
        p_own[:, at * width : (at + 1) * width] = product
        p_send[:, at * width : (at + 1) * width] = product.astype(BF16)
    column = pl.multiple_of(m * slab, 128)
    raw = jnp.concatenate([xs[0, :, :, pl.ds(column, slab)], xs[1, :, :, pl.ds(column, slab)]])
    part = dot(raw.reshape(2 * group, slab), we[...])
    xp[...] = part[:group]
    stores += start(sems, 4, (xp, xp_own))
    xp_send[...] = part[group:].astype(BF16)
    finish(stores)


def attend_kernel(ids, p_own, p_other, att, *refs):
    saved = refs[:5]
    e_out, q_out, k_out, v_out, aux = refs[5:10]
    sems = refs[10]
    rows = p_own.shape[0] - 16
    group = rows // 2
    width = (p_own.shape[1] - 128) // 3
    heads = width // HD
    model = 2 * 8 * width
    stats = p_other[:rows, 3 * width :].astype(F32)
    stats = jnp.concatenate([stats[group:, :], stats[:group, :]])
    m_own, s_own = p_own[:rows, 3 * width : 3 * width + 1], p_own[:rows, 3 * width + 1 : 3 * width + 2]
    m_other = stats[:, 0:1] + stats[:, 1:2] + stats[:, 2:3]
    s_other = stats[:, 3:4] + stats[:, 4:5] + stats[:, 5:6]
    gap = (m_own - m_other) * 0.5
    centre = (m_own + m_other) * 0.5
    inverse = lax.rsqrt((s_own + s_other) / model + gap * gap + EPSILON)
    slope = p_own[rows : rows + 1, : 3 * width] - p_other[rows : rows + 1, : 3 * width].astype(F32)
    inv_q, inv_k, inv_l = [], [], []
    factor = LOG2E * HD**-0.5
    stores = []

    def mixture(at):
        cols = slice(at * HD, (at + 1) * HD)
        other = jnp.concatenate([p_other[group:rows, cols], p_other[:group, cols]]).astype(F32)
        return inverse * (p_own[:rows, cols] + other + gap * slope[:, cols])

    for head in range(heads):
        cols = slice(head * HD, (head + 1) * HD)
        q_hat, q_inv = row_norm(mixture(head))
        k_hat, k_inv = row_norm(mixture(heads + head))
        v_low = mixture(2 * heads + head).astype(BF16)
        e = jnp.exp2(dot_nt(q_hat.astype(BF16), k_hat.astype(BF16)) * factor)
        l_inv = 1.0 / jnp.sum(e, axis=1, keepdims=True)
        e_low = e.astype(BF16)
        e_out[head] = e_low
        stores += start(sems, head, (e_out.at[head], saved[0].at[head]))
        att[:, cols] = (dot(e_low[:group], v_low) * l_inv[:group]).astype(BF16)
        q_out[:, cols] = q_hat
        k_out[:, cols] = k_hat
        v_out[:, cols] = v_low
        inv_q.append(q_inv)
        inv_k.append(k_inv)
        inv_l.append(l_inv)
    aux[...] = lanes([centre, inverse] + inv_l + inv_q + inv_k, rows)
    stores += start(sems, heads, (q_out, saved[1]), (k_out, saved[2]), (v_out, saved[3]), (aux, saved[4]))
    finish(stores)


def embed_kernel(ids, att, wpt_own, wpt_other, xp_own, xp_other, out, wpt, wpt_held, xp, sems):
    load = start(sems, 0, (xp_own, xp))
    total = (wpt_own[...].astype(F32) + wpt_other[...].astype(F32)).astype(BF16)
    wpt_held[...] = total
    store = start(sems, 1, (wpt_held, wpt))
    part = dot_nt(att[...], total) + xp_other[...].astype(F32)
    finish(load)
    out[...] = (part + xp[...]).astype(BF16).reshape(out.shape)
    finish(store)


def sum_kernel(ids, parts, out):
    total = jnp.sum(parts[...].astype(F32), axis=0).astype(BF16)
    for at in range(out.shape[0]):
        out[at] = total


def feature_parts(rows, gm, glayer, x_rows, centre, inverse, held, m, store):
    half, width = held.shape[1:]
    slab = half // 8
    total = jnp.zeros((rows, 1), F32)
    total_dot = jnp.zeros((rows, 1), F32)
    for block in range(8):
        cols = slice(block * slab, (block + 1) * slab)
        g = dot_nt(gm[:, :width], held[0, cols, :])
        g = g + dot_nt(gm[:, width : 2 * width], held[1, cols, :])
        g = g + dot_nt(gm[:, 2 * width :], held[2, cols, :])
        normed = (x_rows(cols).astype(F32) - centre) * inverse
        total = total + jnp.sum(g, axis=1, keepdims=True)
        total_dot = total_dot + jnp.sum(g * normed, axis=1, keepdims=True)
        mine = jnp.where(block == m, 1.0, 0.0)
        store(cols, (g * inverse + glayer * mine).astype(BF16))
    store(slice(half, half + 128), lanes((total, total_dot), rows).astype(BF16))


def encoder_back_kernel(ids, g_own, g_other, we, *refs):
    sources = refs[:7]
    w = refs[7]
    right, left, gmix_out, glayer_out = refs[8:12]
    wpt, e_in, q_in, k_in, v_in, aux, x_in, held, gmix, glayer, few, sems = refs[12:]
    loads = start(sems, 0, *zip(sources, (wpt, e_in, q_in, k_in, v_in, aux, x_in)))
    w_loads = start(sems, 7, *[(w.at[at], held.at[at]) for at in range(3)])
    rows, width = q_in.shape
    heads = width // HD
    tok = x_in.shape[2]
    group = 8 * tok
    m = ids[1]
    factor = HD**-0.5
    gemb = jnp.concatenate([g_own[...], g_other[...]])
    glayer[...] = dot_nt(gemb, we[...])
    stores = start(sems, 10, (glayer, glayer_out))
    finish(loads)
    gatt = dot(gemb, wpt[...]).astype(BF16)
    for head in range(heads):
        cols = slice(head * HD, (head + 1) * HD)
        g_head = gatt[:, cols]
        q_hat, k_hat, v_low = q_in[:, cols], k_in[:, cols], v_in[:, cols]
        l_inv = aux[:, 2 + head : 3 + head]
        q_inv = aux[:, 2 + heads + head : 3 + heads + head]
        k_inv = aux[:, 2 + 2 * heads + head : 3 + 2 * heads + head]
        p = e_in[head].astype(F32) * l_inv
        gp = dot_nt(g_head, v_low)
        delta = jnp.sum(p * gp, axis=1, keepdims=True)
        gs = (p * (gp - delta)).astype(BF16)
        gq = dot(gs, k_hat.astype(BF16)) * factor
        gk = dot_tn(gs, q_hat.astype(BF16)) * factor
        gv = dot_tn(p.astype(BF16), g_head)
        gmix[:, head * HD : (head + 1) * HD] = norm_back(q_hat, q_inv, gq).astype(BF16)
        gmix[:, width + head * HD : width + (head + 1) * HD] = norm_back(k_hat, k_inv, gk).astype(BF16)
        gmix[:, 2 * width + head * HD : 2 * width + (head + 1) * HD] = gv.astype(BF16)
    stores += start(sems, 11, (gmix, gmix_out))
    ats = [lax.rem(m + 4, 8), lax.rem(m + 5, 8)]
    blocks = [(rel, at) for at in ats for rel in range(2)]

    def rows_of(ref):
        return jnp.concatenate(
            [ref[pl.ds(pl.multiple_of(at * tok, tok) + rel * group, tok), :] for rel, at in blocks]
        )

    few[...] = rows_of(gmix)
    some = rows_of(aux)

    def x_rows(cols):
        return jnp.concatenate([x_in[rel, at, :, cols] for rel, at in blocks])

    def store(cols, value):
        right[:, cols] = value[: 2 * tok]
        left[:, cols] = value[2 * tok :]

    finish(w_loads)
    feature_parts(4 * tok, few[...], rows_of(glayer), x_rows, some[:, 0:1], some[:, 1:2], held, m, store)
    finish(stores)


def feature_kernel(ids, *refs):
    sources, w, out = refs[:4], refs[4], refs[5]
    gmix, glayer, aux, x_in, held, sems = refs[6:]
    loads = start(sems, 0, *zip(sources, (gmix, glayer, aux, x_in)))
    loads += start(sems, 4, *[(w.at[at], held.at[at]) for at in range(3)])
    tok = x_in.shape[2]
    rows = gmix.shape[0]

    def x_rows(cols):
        return x_in[:, :, :, cols].reshape(rows, cols.stop - cols.start)

    def store(cols, value):
        value = value.reshape(2, 8, tok, cols.stop - cols.start)
        out[:, :tok, cols] = value[0]
        out[:, tok:, cols] = value[1]

    finish(loads)
    feature_parts(rows, gmix[...], glayer[...], x_rows, aux[:, 0:1], aux[:, 1:2], held, ids[1], store)


def final_kernel(ids, own, other, x_own, out):
    s = ids[0]
    half = x_own.shape[1] // 2
    model = x_own.shape[1]
    normed, inverse = row_norm(x_own[...].astype(F32))
    mine, theirs = own[...], other[...].astype(F32)
    total = (mine[:, half : half + 1] + theirs[:, half : half + 1]) / model
    total_dot = (mine[:, half + 1 : half + 2] + theirs[:, half + 1 : half + 2]) / model
    first = jnp.where(s == 0, mine[:, :half], theirs[:, :half])
    second = jnp.where(s == 0, theirs[:, :half], mine[:, :half])
    out[:, :half] = (first - inverse * (total + normed[:, :half] * total_dot)).astype(BF16)
    out[:, half:] = (second - inverse * (total + normed[:, half:] * total_dot)).astype(BF16)


def head_norm_t(values):
    width, n = values.shape
    hat, inverse = row_norm(values.reshape(DHEADS, DHD, n), axis=1)
    return hat.reshape(width, n), inverse


def head_back_t(hat, inverse, gradient):
    width, n = hat.shape
    back = norm_back(
        hat.reshape(DHEADS, DHD, n), inverse, gradient.reshape(DHEADS, DHD, n), axis=1
    )
    return back.reshape(width, n)


def mask_kernel(ids, table_in, mask, w, pos_vis, vis_row, hidden, k_t, v, wq_t, wk_t, table, sems):
    load = start(sems, 0, (table_in, table))
    wq_t[...] = w[0].T
    wk_t[...] = w[1].T
    finish(load)
    members, pos_dev = table.shape[0], table.shape[1] - 16
    npos, width = members * pos_dev, table.shape[2]
    nvis = vis_row.shape[1]
    pos_all = table[:, :pos_dev, :].reshape(npos, width)
    codes = jnp.sum(table[:, pos_dev:, :].astype(F32), axis=0)
    row = codes[0:1, :nvis] * 32.0 + codes[1:2, :nvis]
    other = jnp.concatenate([row[:, nvis // 2 :], row[:, : nvis // 2]], axis=1)
    vis = jnp.where(ids[0] == 0, row, other).astype(jnp.int32)
    vis_row[...] = vis
    hot = jnp.where(lax.broadcasted_iota(jnp.int32, (npos, nvis), 0) == vis, 1.0, 0.0).astype(BF16)
    pos_vis[...] = dot_tn(hot, pos_all)
    hidden[...] = 1.0 - dot_nt(jnp.ones((16, nvis), BF16), hot)[0:1, :]
    hat, _ = row_norm(pos_all.astype(F32) + mask[...].astype(F32))
    low = hat.astype(BF16)
    key_hat, _ = head_norm_t(dot_nt(wk_t[...], low))
    k_t[...] = key_hat.astype(BF16)
    v[...] = dot(low, w[2]).astype(BF16)


def decoder_kernel(
    ids, vis_row, emb_own, emb_other, pos_vis, hidden, km_t, vm, pos_own, mask, wq_t, wk_t, w, w_out, w_pix, target,
    pred, g_own, g_other, em_ref, ev_ref,
):
    npos_dev, width = pos_own.shape
    nvis = pos_vis.shape[0]
    group = nvis // 2
    member = ids[2]
    groups = width // 128
    per = 128 // DHD
    rows = per * npos_dev
    factor = DHD**-0.5
    emb = jnp.concatenate([emb_own[...], emb_other[...]])
    vis_hat, vis_inv = row_norm(emb.astype(F32) + pos_vis[...])
    vis_low = vis_hat.astype(BF16)
    kv_hat, kv_inv = head_norm_t(dot_nt(wk_t[...], vis_low))
    kv_t = kv_hat.astype(BF16)
    vv = dot(vis_low, w[2]).astype(BF16)
    position = lax.broadcasted_iota(jnp.int32, (npos_dev, nvis), 0) + member * npos_dev
    hot = jnp.where(position == vis_row[...], 1.0, 0.0)
    seen = jnp.sum(hot, axis=1, keepdims=True)
    hot_low = hot.astype(BF16)
    filled = dot(hot_low, emb) + (1.0 - seen) * mask[...].astype(F32)
    stream = filled + pos_own[...].astype(F32)
    own_hat, own_inv = row_norm(stream)
    q_t, q_inv = head_norm_t(dot_nt(wq_t[...], own_hat.astype(BF16)))
    q_low = q_t.T.astype(BF16)
    head_mask = (
        lax.broadcasted_iota(jnp.int32, (rows, 128), 0) // npos_dev
        == lax.broadcasted_iota(jnp.int32, (rows, 128), 1) // DHD
    )

    def spread(values):
        return jnp.where(head_mask, jnp.concatenate([values] * per, axis=0), jnp.zeros((), values.dtype))

    def gather(values):
        return jnp.sum(jnp.where(head_mask, values, 0.0).reshape(per, npos_dev, 128), axis=0)

    attended, inv_l = [], []
    for at in range(groups):
        cols = slice(at * 128, (at + 1) * 128)
        q_wide = spread(q_low[:, cols])
        em = jnp.exp2(dot(q_wide, km_t[cols, :]) * (factor * LOG2E)) * hidden[...]
        ev = jnp.exp2(dot(q_wide, kv_t[cols, :]) * (factor * LOG2E))
        l_inv = 1.0 / (jnp.sum(em, axis=1, keepdims=True) + jnp.sum(ev, axis=1, keepdims=True))
        em_low, ev_low = em.astype(BF16), ev.astype(BF16)
        em_ref[at] = em_low
        ev_ref[at] = ev_low
        attended.append(gather((dot(em_low, vm[:, cols]) + dot(ev_low, vv[:, cols])) * l_inv))
        inv_l.append(l_inv)
    att = jnp.concatenate(attended, axis=1)
    second = stream + dot(att.astype(BF16), w_out[...])
    final_hat, final_inv = row_norm(second)
    full = dot(final_hat.astype(BF16), w_pix[...])
    pred[...] = full.astype(BF16)
    error = jnp.where(seen > 0, 0.0, full - target[...].astype(F32)).astype(BF16)
    g_second = norm_back(final_hat, final_inv, dot_nt(error, w_pix[...]))
    g_att = dot_nt(g_second.astype(BF16), w_out[...]).astype(BF16)
    product = g_att.astype(F32) * att
    gq, gk_t, gv = [], [], []
    for at in range(groups):
        cols = slice(at * 128, (at + 1) * 128)
        q_wide = spread(q_low[:, cols])
        g_wide = spread(g_att[:, cols])
        delta = jnp.sum(spread(product[:, cols]), axis=1, keepdims=True)
        l_inv = inv_l[at]
        pv = ev_ref[at].astype(F32) * l_inv
        gs_v = (pv * (dot_nt(g_wide, vv[:, cols]) - delta)).astype(BF16)
        pm = em_ref[at].astype(F32) * l_inv
        gs_m = (pm * (dot_nt(g_wide, vm[:, cols]) - delta)).astype(BF16)
        gq.append(gather(dot_nt(gs_m, km_t[cols, :]) + dot_nt(gs_v, kv_t[cols, :])) * factor)
        gk_t.append(dot_tn(q_wide, gs_v) * factor)
        gv.append(dot_tn(pv.astype(BF16), g_wide).astype(BF16))
    gq_back = head_back_t(q_t, q_inv, jnp.concatenate(gq, axis=1).T).T.astype(BF16)
    g_stream_own = g_second + norm_back(own_hat, own_inv, dot_nt(gq_back, w[0]))
    gk_back = head_back_t(kv_hat, kv_inv, jnp.concatenate(gk_t, axis=0)).T.astype(BF16)
    from_keys = dot_nt(gk_back, w[1]) + dot_nt(jnp.concatenate(gv, axis=1), w[2])
    part = norm_back(vis_hat, vis_inv, from_keys) + dot_tn(hot_low, g_stream_own.astype(BF16))
    g_own[...] = part[:group]
    g_other[...] = part[group:].astype(BF16)


def shards(
    patches,
    vis_index,
    input_weight,
    output_weight,
    embed_weight,
    mask_token,
    position_table,
    decoder_input,
    decoder_output,
    pixel_weight,
    target,
):
    section = lax.axis_index("section")
    column = lax.axis_index("mp")
    member = lax.axis_index(("section", "mp"))
    copies = lax.axis_size("dp")
    ids = jnp.stack([section, column, member]).astype(jnp.int32)
    x_own = patches[0]
    tok, model = x_own.shape
    half = model // 2
    slab, dec_width = embed_weight.shape
    width = output_weight.shape[0]
    heads = width // HD
    group = 8 * tok
    nvis = 2 * group
    pos_dev = position_table.shape[0]
    npos = 16 * pos_dev

    def swap(value):
        return lax.ppermute(value, "section", [(0, 1), (1, 0)])

    def shift(value, by):
        return lax.ppermute(value, "mp", [(i, (i + by) % 8) for i in range(8)])

    def exchange(value, axis):
        return lax.all_to_all(value, axis, 0, 0, tiled=True)

    mine = lax.dynamic_slice_in_dim(x_own, section * half, half, 1)
    theirs = swap(lax.dynamic_slice_in_dim(x_own, (1 - section) * half, half, 1))
    dec_cols = dec_width // copies
    we_t = lax.dynamic_slice_in_dim(embed_weight, lax.axis_index("dp") * dec_cols, dec_cols, 1).T
    we_t = we_t.reshape(dec_cols // 32, 32, slab).transpose(1, 0, 2).reshape(32, -1)
    chunk = jnp.concatenate([jnp.concatenate([mine, theirs]), we_t], axis=1)
    chunks = {0: chunk}
    right = left = chunk
    for step in range(1, 5):
        right = shift(right, 1)
        chunks[-step] = right
        if step < 4:
            left = shift(left, -1)
            chunks[step] = left

    index, _ = lax.optimization_barrier((vis_index[0], chunks[-1]))
    row = jnp.zeros((nvis,), jnp.int32)
    row = lax.dynamic_update_slice_in_dim(row, index, member * tok, 0)
    codes = jnp.pad(jnp.stack([row // 32, row % 32]), ((0, 14), (0, dec_width - nvis)))
    table = jnp.concatenate([position_table, codes.astype(BF16)])
    table = lax.all_gather(table, ("section", "mp"), axis=0, tiled=False)

    w_in = input_weight.transpose(1, 0, 2)
    held = sds(w_in.shape, BF16)
    ordered = [chunks[offset] for offset in OFFSETS]
    (wp_part,) = call(
        fold_kernel,
        [sds((copies, dec_cols, width), BF16)],
        ids,
        *ordered,
        output_weight,
        scratch=[sds((dec_cols, half), BF16)],
    )
    wpt_own = exchange(wp_part, "dp").reshape(dec_width, width)
    ids_late, _ = lax.optimization_barrier((ids, wp_part))
    x_all, p_own, p_send, xp_own, xp_send = call(
        project_kernel,
        [
            sds((2, 8, tok, half), BF16),
            sds((nvis + 16, 3 * width + 128), F32),
            sds((nvis + 16, 3 * width + 128), BF16),
            sds((group, dec_width), F32),
            sds((group, dec_width), BF16),
        ],
        ids_late,
        *ordered,
        w_in,
        embed_weight,
        scratch=[
            sds((2, 8, tok, half), BF16),
            sds((nvis + 16, half), BF16),
            held,
            sds((group, dec_width), F32),
        ],
        far=(9,),
        far_out=(0, 3),
        copies=5,
        limit=28,
    )
    p_other = swap(p_send)
    wpt_other = swap(wpt_own)
    xp_other = swap(xp_send)
    saved = [
        sds((heads, nvis, nvis), BF16),
        sds((nvis, width), F32),
        sds((nvis, width), F32),
        sds((nvis, width), BF16),
        sds((nvis, 128), F32),
    ]
    att, e_enc, q_enc, k_enc, v_enc, aux = call(
        attend_kernel,
        [sds((group, width), BF16)] + saved,
        ids,
        p_own,
        p_other,
        scratch=saved,
        far_out=(1, 2, 3, 4, 5),
        copies=heads + 4,
    )
    embed_part, wpt = call(
        embed_kernel,
        [sds((8, tok, dec_width), BF16), sds((dec_width, width), BF16)],
        ids,
        att,
        wpt_own,
        wpt_other,
        xp_own,
        xp_other,
        scratch=[sds((dec_width, width), BF16), sds((group, dec_width), F32)],
        far=(4,),
        far_out=(1,),
        copies=2,
    )

    def reduce_and_gather(part):
        (total,) = call(sum_kernel, [sds((8, tok, dec_width), BF16)], ids, exchange(part, "mp"))
        gathered = exchange(total, "mp").reshape(group, dec_width)
        return gathered, swap(gathered)

    w_dec = decoder_input.transpose(1, 0, 2)
    mask_row = mask_token.reshape(1, dec_width)
    table, embed_part = lax.optimization_barrier((table, embed_part))
    pos_vis, vis_row, hidden, km_t, vm, wq_t, wk_t = call(
        mask_kernel,
        [
            sds((nvis, dec_width), F32),
            sds((1, nvis), jnp.int32),
            sds((1, npos), F32),
            sds((dec_width, npos), BF16),
            sds((npos, dec_width), BF16),
            sds((dec_width, dec_width), BF16),
            sds((dec_width, dec_width), BF16),
        ],
        ids,
        table,
        mask_row,
        w_dec,
        scratch=[sds(table.shape, BF16)],
        far=(1,),
        copies=1,
    )
    emb_own, emb_other = reduce_and_gather(embed_part)

    groups = dec_width // 128
    rows = (128 // DHD) * pos_dev
    prediction, g_own, g_send = call(
        decoder_kernel,
        [
            sds((pos_dev, target.shape[2]), BF16),
            sds((group, dec_width), F32),
            sds((group, dec_width), BF16),
        ],
        ids,
        vis_row,
        emb_own,
        emb_other,
        pos_vis,
        hidden,
        km_t,
        vm,
        position_table,
        mask_row,
        wq_t,
        wk_t,
        w_dec,
        decoder_output,
        pixel_weight,
        target[0],
        scratch=[sds((groups, rows, npos), BF16), sds((groups, rows, nvis), BF16)],
    )
    g_part = (g_own + swap(g_send).astype(F32)).astype(BF16)
    ge_own, ge_other = reduce_and_gather(g_part.reshape(8, tok, dec_width))

    right, left, gmix, glayer = call(
        encoder_back_kernel,
        [
            sds((2 * tok, half + 128), BF16),
            sds((2 * tok, half + 128), BF16),
            sds((nvis, 3 * width), BF16),
            sds((nvis, slab), F32),
        ],
        ids,
        ge_own,
        ge_other,
        embed_weight,
        wpt,
        e_enc,
        q_enc,
        k_enc,
        v_enc,
        aux,
        x_all,
        w_in,
        scratch=[sds((dec_width, width), BF16)]
        + saved
        + [sds(x_all.shape, BF16), held, sds((nvis, 3 * width), BF16), sds((nvis, slab), F32)]
        + [sds((4 * tok, 3 * width), BF16)],
        far=tuple(range(4, 12)),
        far_out=(2, 3),
        copies=12,
    )
    (parts,) = call(
        feature_kernel,
        [sds((8, 2 * tok, half + 128), BF16)],
        ids,
        gmix,
        glayer,
        aux,
        x_all,
        w_in,
        scratch=[
            sds((nvis, 3 * width), BF16),
            sds((nvis, slab), F32),
            sds((nvis, 128), F32),
            sds(x_all.shape, BF16),
            held,
        ],
        far=(1, 2, 3, 4, 5),
        copies=7,
    )

    def part(offset):
        return lax.dynamic_index_in_dim(parts, (column + offset) % 8, 0, False).astype(F32)

    for step in range(3):
        moved_right, moved_left = shift(right, 1), shift(left, -1)
        right = (moved_right.astype(F32) + part(3 - step)).astype(BF16)
        if step < 2:
            left = (moved_left.astype(F32) + part(-2 + step)).astype(BF16)
    total = shift(right, 1).astype(F32) + moved_left.astype(F32) + part(0)
    (patch_grad,) = call(
        final_kernel,
        [sds((tok, model), BF16)],
        ids,
        total[:tok],
        swap(total[tok:].astype(BF16)),
        x_own,
    )
    return (prediction[None], patch_grad[None])


def solution(mesh):
    group = ("section", "mp")
    in_specs = (
        P("dp", group, None),
        P("dp", group),
        P("section", None, "mp"),
        P("mp", "section"),
        P(group, None),
        P(),
        P(group, None),
        P(),
        P(),
        P(),
        P("dp", group, None),
    )
    out_specs = (P("dp", group, None), P("dp", group, None))
    return jax.shard_map(shards, mesh=mesh, in_specs=in_specs, out_specs=out_specs, check_vma=False)
```

```python
import math

import jax
import jax.numpy as jnp
from jax import lax
from jax.experimental import pallas as pl
from jax.experimental.pallas import tpu as pltpu
from jax.sharding import PartitionSpec as P

HD = 128
DHEADS = 16
DHD = 32
EPSILON = 1e-06
LOG2E = math.log2(math.e)
F32 = jnp.float32
BF16 = jnp.bfloat16
OFFSETS = (0, -1, 1, -2, 2, -3, 3, -4)


def dot(a, b):
    return lax.dot_general(a, b, (((1,), (0,)), ((), ())), preferred_element_type=F32)


def dot_nt(a, b):
    return lax.dot_general(a, b, (((1,), (1,)), ((), ())), preferred_element_type=F32)


def dot_tn(a, b):
    return lax.dot_general(a, b, (((0,), (0,)), ((), ())), preferred_element_type=F32)


def row_norm(values, axis=-1):
    centre = jnp.mean(values, axis=axis, keepdims=True)
    centered = values - centre
    inverse = lax.rsqrt(jnp.mean(centered * centered, axis=axis, keepdims=True) + EPSILON)
    return centered * inverse, inverse


def norm_back(normed, inverse, gradient, axis=-1):
    mean_grad = jnp.mean(gradient, axis=axis, keepdims=True)
    mean_dot = jnp.mean(gradient * normed, axis=axis, keepdims=True)
    return inverse * (gradient - mean_grad - normed * mean_dot)


def lanes(columns, rows):
    lane = lax.broadcasted_iota(jnp.int32, (rows, 128), 1)
    out = jnp.zeros((rows, 128), F32)
    for at, column in enumerate(columns):
        out = jnp.where(lane == at, column, out)
    return out


def call(kernel, outs, *args, scratch=(), far=(), far_out=(), copies=0, limit=58):
    specs = [pl.BlockSpec(memory_space=pltpu.SMEM)]
    for at in range(1, len(args)):
        specs.append(pl.BlockSpec(memory_space=pl.ANY if at in far else pltpu.VMEM))
    out_specs = [
        pl.BlockSpec(memory_space=pl.ANY if at in far_out else pltpu.VMEM) for at in range(len(outs))
    ]
    scratch = [pltpu.VMEM(shape.shape, shape.dtype) for shape in scratch]
    if copies:
        scratch.append(pltpu.SemaphoreType.DMA((copies,)))
    return pl.pallas_call(
        kernel,
        out_shape=tuple(outs),
        in_specs=specs,
        out_specs=tuple(out_specs),
        scratch_shapes=scratch,
        compiler_params=pltpu.CompilerParams(vmem_limit_bytes=limit * 2**20),
    )(*args)


def start(sems, first, *pairs):
    copies = [
        pltpu.make_async_copy(source, target, sems.at[first + at]) for at, (source, target) in enumerate(pairs)
    ]
    for copy in copies:
        copy.start()
    return copies


def finish(copies):
    for copy in copies:
        copy.wait()


def sds(shape, dtype):
    return jax.ShapeDtypeStruct(shape, dtype)


def fold_kernel(ids, *refs):
    sources, wo_in, out = refs[:8], refs[8], refs[9]
    wt, wo, sems = refs[10:]
    half = wo.shape[1]
    slab = half // 8
    pieces = wt.shape[0] // 32
    loads = start(sems, 0, (wo_in, wo))
    for index, (source, offset) in enumerate(zip(sources, OFFSETS)):
        column = pl.multiple_of(lax.rem(ids[1] + offset + 8, 8) * slab, 128)
        base = source.shape[1] - pieces * slab
        for piece in range(pieces):
            target = wt.at[pl.ds(piece * 32, 32), pl.ds(column, slab)]
            source_part = source.at[:, pl.ds(base + piece * slab, slab)]
            loads += start(sems, 1 + index * pieces + piece, (source_part, target))
    finish(loads)
    total = dot_nt(wt[...], wo[...]).astype(BF16)
    for at in range(out.shape[0]):
        out[at] = total


def split3(values):
    first = values.astype(BF16).astype(F32)
    second = (values - first).astype(BF16).astype(F32)
    return [first, second, values - first - second]


def project_kernel(ids, *refs):
    chunks = refs[:8]
    w, we = refs[8:10]
    x_out, p_own, p_send, xp_own, xp_send = refs[10:15]
    xs, xc, held, xp, held_chunks, sems = refs[15:]
    half, width = held.shape[1:]
    arrivals = start(
        sems, 5, *[(chunk.at[:, pl.ds(0, half)], held_chunks.at[at]) for at, chunk in enumerate(chunks)]
    )
    loads = start(sems, 0, *[(w.at[at], held.at[at]) for at in range(3)])
    slab = half // 8
    tok = xs.shape[2]
    group = 8 * tok
    m = ids[1]
    for index, offset in enumerate(OFFSETS):
        at = lax.rem(m + offset + 8, 8)
        arrivals[index].wait()
        value = held_chunks[index]
        xs[0, at] = value[:tok]
        xs[1, at] = value[tok:]
        wide = value.astype(F32)
        centre = jnp.mean(wide, axis=1, keepdims=True)
        centered = wide - centre
        spread = jnp.sum(centered * centered, axis=1, keepdims=True)
        low = centered.astype(BF16)
        own = lanes((centre, spread), 2 * tok)
        send = lanes(split3(centre) + split3(spread), 2 * tok).astype(BF16)
        row = pl.multiple_of(at * tok, tok)
        for rel in range(2):
            part = slice(rel * tok, (rel + 1) * tok)
            xc[pl.ds(row + rel * group, tok), :] = low[part]
            p_own[pl.ds(row + rel * group, tok), 3 * width :] = own[part]
            p_send[pl.ds(row + rel * group, tok), 3 * width :] = send[part]
    stores = start(sems, 3, (xs, x_out))
    xc[2 * group :, :] = jnp.ones((16, half), BF16)
    p_own[2 * group :, 3 * width :] = jnp.zeros((16, 128), F32)
    p_send[2 * group :, 3 * width :] = jnp.zeros((16, 128), BF16)
    for at in range(3):
        loads[at].wait()
        product = dot(xc[...], held[at])
        p_own[:, at * width : (at + 1) * width] = product
        p_send[:, at * width : (at + 1) * width] = product.astype(BF16)
    column = pl.multiple_of(m * slab, 128)
    raw = jnp.concatenate([xs[0, :, :, pl.ds(column, slab)], xs[1, :, :, pl.ds(column, slab)]])
    part = dot(raw.reshape(2 * group, slab), we[...])
    xp[...] = part[:group]
    stores += start(sems, 4, (xp, xp_own))
    xp_send[...] = part[group:].astype(BF16)
    finish(stores)


def attend_kernel(ids, p_own, p_other, att, *refs):
    saved = refs[:5]
    e_out, q_out, k_out, v_out, aux = refs[5:10]
    sems = refs[10]
    rows = p_own.shape[0] - 16
    group = rows // 2
    width = (p_own.shape[1] - 128) // 3
    heads = width // HD
    model = 2 * 8 * width
    stats = p_other[:rows, 3 * width :].astype(F32)
    stats = jnp.concatenate([stats[group:, :], stats[:group, :]])
    m_own, s_own = p_own[:rows, 3 * width : 3 * width + 1], p_own[:rows, 3 * width + 1 : 3 * width + 2]
    m_other = stats[:, 0:1] + stats[:, 1:2] + stats[:, 2:3]
    s_other = stats[:, 3:4] + stats[:, 4:5] + stats[:, 5:6]
    gap = (m_own - m_other) * 0.5
    centre = (m_own + m_other) * 0.5
    inverse = lax.rsqrt((s_own + s_other) / model + gap * gap + EPSILON)
    slope = p_own[rows : rows + 1, : 3 * width] - p_other[rows : rows + 1, : 3 * width].astype(F32)
    inv_q, inv_k, inv_l = [], [], []
    factor = LOG2E * HD**-0.5
    stores = []

    def mixture(at):
        cols = slice(at * HD, (at + 1) * HD)
        other = jnp.concatenate([p_other[group:rows, cols], p_other[:group, cols]]).astype(F32)
        return inverse * (p_own[:rows, cols] + other + gap * slope[:, cols])

    for head in range(heads):
        cols = slice(head * HD, (head + 1) * HD)
        q_hat, q_inv = row_norm(mixture(head))
        k_hat, k_inv = row_norm(mixture(heads + head))
        v_low = mixture(2 * heads + head).astype(BF16)
        e = jnp.exp2(dot_nt(q_hat.astype(BF16), k_hat.astype(BF16)) * factor)
        l_inv = 1.0 / jnp.sum(e, axis=1, keepdims=True)
        e_low = e.astype(BF16)
        e_out[head] = e_low
        stores += start(sems, head, (e_out.at[head], saved[0].at[head]))
        att[:, cols] = (dot(e_low[:group], v_low) * l_inv[:group]).astype(BF16)
        q_out[:, cols] = q_hat
        k_out[:, cols] = k_hat
        v_out[:, cols] = v_low
        inv_q.append(q_inv)
        inv_k.append(k_inv)
        inv_l.append(l_inv)
    aux[...] = lanes([centre, inverse] + inv_l + inv_q + inv_k, rows)
    stores += start(sems, heads, (q_out, saved[1]), (k_out, saved[2]), (v_out, saved[3]), (aux, saved[4]))
    finish(stores)


def embed_kernel(ids, att, wpt_own, wpt_other, xp_own, xp_other, out, wpt, wpt_held, xp, sems):
    load = start(sems, 0, (xp_own, xp))
    total = (wpt_own[...].astype(F32) + wpt_other[...].astype(F32)).astype(BF16)
    wpt_held[...] = total
    store = start(sems, 1, (wpt_held, wpt))
    part = dot_nt(att[...], total) + xp_other[...].astype(F32)
    finish(load)
    out[...] = (part + xp[...]).astype(BF16).reshape(out.shape)
    finish(store)


def sum_kernel(ids, parts, out):
    total = jnp.sum(parts[...].astype(F32), axis=0).astype(BF16)
    for at in range(out.shape[0]):
        out[at] = total


def feature_parts(rows, gm, glayer, x_rows, centre, inverse, held, m, store):
    half, width = held.shape[1:]
    slab = half // 8
    total = jnp.zeros((rows, 1), F32)
    total_dot = jnp.zeros((rows, 1), F32)
    for block in range(8):
        cols = slice(block * slab, (block + 1) * slab)
        g = dot_nt(gm[:, :width], held[0, cols, :])
        g = g + dot_nt(gm[:, width : 2 * width], held[1, cols, :])
        g = g + dot_nt(gm[:, 2 * width :], held[2, cols, :])
        normed = (x_rows(cols).astype(F32) - centre) * inverse
        total = total + jnp.sum(g, axis=1, keepdims=True)
        total_dot = total_dot + jnp.sum(g * normed, axis=1, keepdims=True)
        mine = jnp.where(block == m, 1.0, 0.0)
        store(cols, (g * inverse + glayer * mine).astype(BF16))
    store(slice(half, half + 128), lanes((total, total_dot), rows).astype(BF16))


def encoder_back_kernel(ids, g_own, g_other, we, *refs):
    sources = refs[:7]
    w = refs[7]
    right, left, gmix_out, glayer_out = refs[8:12]
    wpt, e_in, q_in, k_in, v_in, aux, x_in, held, gmix, glayer, few, sems = refs[12:]
    loads = start(sems, 0, *zip(sources, (wpt, e_in, q_in, k_in, v_in, aux, x_in)))
    w_loads = start(sems, 7, *[(w.at[at], held.at[at]) for at in range(3)])
    rows, width = q_in.shape
    heads = width // HD
    tok = x_in.shape[2]
    group = 8 * tok
    m = ids[1]
    factor = HD**-0.5
    gemb = jnp.concatenate([g_own[...], g_other[...]])
    glayer[...] = dot_nt(gemb, we[...])
    stores = start(sems, 10, (glayer, glayer_out))
    finish(loads)
    gatt = dot(gemb, wpt[...]).astype(BF16)
    for head in range(heads):
        cols = slice(head * HD, (head + 1) * HD)
        g_head = gatt[:, cols]
        q_hat, k_hat, v_low = q_in[:, cols], k_in[:, cols], v_in[:, cols]
        l_inv = aux[:, 2 + head : 3 + head]
        q_inv = aux[:, 2 + heads + head : 3 + heads + head]
        k_inv = aux[:, 2 + 2 * heads + head : 3 + 2 * heads + head]
        p = e_in[head].astype(F32) * l_inv
        gp = dot_nt(g_head, v_low)
        delta = jnp.sum(p * gp, axis=1, keepdims=True)
        gs = (p * (gp - delta)).astype(BF16)
        gq = dot(gs, k_hat.astype(BF16)) * factor
        gk = dot_tn(gs, q_hat.astype(BF16)) * factor
        gv = dot_tn(p.astype(BF16), g_head)
        gmix[:, head * HD : (head + 1) * HD] = norm_back(q_hat, q_inv, gq).astype(BF16)
        gmix[:, width + head * HD : width + (head + 1) * HD] = norm_back(k_hat, k_inv, gk).astype(BF16)
        gmix[:, 2 * width + head * HD : 2 * width + (head + 1) * HD] = gv.astype(BF16)
    stores += start(sems, 11, (gmix, gmix_out))
    ats = [lax.rem(m + 4, 8), lax.rem(m + 5, 8)]
    blocks = [(rel, at) for at in ats for rel in range(2)]

    def rows_of(ref):
        return jnp.concatenate(
            [ref[pl.ds(pl.multiple_of(at * tok, tok) + rel * group, tok), :] for rel, at in blocks]
        )

    few[...] = rows_of(gmix)
    some = rows_of(aux)

    def x_rows(cols):
        return jnp.concatenate([x_in[rel, at, :, cols] for rel, at in blocks])

    def store(cols, value):
        right[:, cols] = value[: 2 * tok]
        left[:, cols] = value[2 * tok :]

    finish(w_loads)
    feature_parts(4 * tok, few[...], rows_of(glayer), x_rows, some[:, 0:1], some[:, 1:2], held, m, store)
    finish(stores)


def feature_kernel(ids, *refs):
    sources, w, out = refs[:4], refs[4], refs[5]
    gmix, glayer, aux, x_in, held, sems = refs[6:]
    loads = start(sems, 0, *zip(sources, (gmix, glayer, aux, x_in)))
    loads += start(sems, 4, *[(w.at[at], held.at[at]) for at in range(3)])
    tok = x_in.shape[2]
    rows = gmix.shape[0]

    def x_rows(cols):
        return x_in[:, :, :, cols].reshape(rows, cols.stop - cols.start)

    def store(cols, value):
        value = value.reshape(2, 8, tok, cols.stop - cols.start)
        out[:, :tok, cols] = value[0]
        out[:, tok:, cols] = value[1]

    finish(loads)
    feature_parts(rows, gmix[...], glayer[...], x_rows, aux[:, 0:1], aux[:, 1:2], held, ids[1], store)


def final_kernel(ids, own, other, x_own, out):
    s = ids[0]
    half = x_own.shape[1] // 2
    model = x_own.shape[1]
    normed, inverse = row_norm(x_own[...].astype(F32))
    mine, theirs = own[...], other[...].astype(F32)
    total = (mine[:, half : half + 1] + theirs[:, half : half + 1]) / model
    total_dot = (mine[:, half + 1 : half + 2] + theirs[:, half + 1 : half + 2]) / model
    first = jnp.where(s == 0, mine[:, :half], theirs[:, :half])
    second = jnp.where(s == 0, theirs[:, :half], mine[:, :half])
    out[:, :half] = (first - inverse * (total + normed[:, :half] * total_dot)).astype(BF16)
    out[:, half:] = (second - inverse * (total + normed[:, half:] * total_dot)).astype(BF16)


def head_norm_t(values):
    width, n = values.shape
    hat, inverse = row_norm(values.reshape(DHEADS, DHD, n), axis=1)
    return hat.reshape(width, n), inverse


def head_back_t(hat, inverse, gradient):
    width, n = hat.shape
    back = norm_back(
        hat.reshape(DHEADS, DHD, n), inverse, gradient.reshape(DHEADS, DHD, n), axis=1
    )
    return back.reshape(width, n)


def mask_kernel(ids, table_in, mask, w_in, pos_vis, vis_row, hidden, k_t, v, wq_t, wk_t, table, w, sems):
    loads = start(sems, 0, (w_in, w), (table_in, table))
    loads[0].wait()
    wq_t[...] = w[0].T
    wk_t[...] = w[1].T
    loads[1].wait()
    members, pos_dev = table.shape[0], table.shape[1] - 16
    npos, width = members * pos_dev, table.shape[2]
    nvis = vis_row.shape[1]
    pos_all = table[:, :pos_dev, :].reshape(npos, width)
    codes = jnp.sum(table[:, pos_dev:, :].astype(F32), axis=0)
    row = codes[0:1, :nvis] * 32.0 + codes[1:2, :nvis]
    other = jnp.concatenate([row[:, nvis // 2 :], row[:, : nvis // 2]], axis=1)
    vis = jnp.where(ids[0] == 0, row, other).astype(jnp.int32)
    vis_row[...] = vis
    hot = jnp.where(lax.broadcasted_iota(jnp.int32, (npos, nvis), 0) == vis, 1.0, 0.0).astype(BF16)
    pos_vis[...] = dot_tn(hot, pos_all)
    hidden[...] = 1.0 - dot_nt(jnp.ones((16, nvis), BF16), hot)[0:1, :]
    hat, _ = row_norm(pos_all.astype(F32) + mask[...].astype(F32))
    low = hat.astype(BF16)
    key_hat, _ = head_norm_t(dot_nt(wk_t[...], low))
    k_t[...] = key_hat.astype(BF16)
    v[...] = dot(low, w[2]).astype(BF16)


def decoder_kernel(ids, vis_row, emb_own, emb_other, hidden, mask, *refs):
    sources = refs[:10]
    pred, g_own, g_other, em_ref, ev_ref = refs[10:15]
    wk_t, w, pos_vis, wq_t, pos_own, km_t, vm, w_out, w_pix, target, sems = refs[15:]
    loads = start(sems, 0, *zip(sources, (wk_t, w, pos_vis, wq_t, pos_own, km_t, vm, w_out, w_pix, target)))
    npos_dev, width = pos_own.shape
    nvis = pos_vis.shape[0]
    group = nvis // 2
    member = ids[2]
    groups = width // 128
    per = 128 // DHD
    rows = per * npos_dev
    factor = DHD**-0.5
    emb = jnp.concatenate([emb_own[...], emb_other[...]])
    finish(loads[:3])
    vis_hat, vis_inv = row_norm(emb.astype(F32) + pos_vis[...])
    vis_low = vis_hat.astype(BF16)
    kv_hat, kv_inv = head_norm_t(dot_nt(wk_t[...], vis_low))
    kv_t = kv_hat.astype(BF16)
    vv = dot(vis_low, w[2]).astype(BF16)
    finish(loads[3:5])
    position = lax.broadcasted_iota(jnp.int32, (npos_dev, nvis), 0) + member * npos_dev
    hot = jnp.where(position == vis_row[...], 1.0, 0.0)
    seen = jnp.sum(hot, axis=1, keepdims=True)
    hot_low = hot.astype(BF16)
    filled = dot(hot_low, emb) + (1.0 - seen) * mask[...].astype(F32)
    stream = filled + pos_own[...].astype(F32)
    own_hat, own_inv = row_norm(stream)
    q_t, q_inv = head_norm_t(dot_nt(wq_t[...], own_hat.astype(BF16)))
    q_low = q_t.T.astype(BF16)
    head_mask = (
        lax.broadcasted_iota(jnp.int32, (rows, 128), 0) // npos_dev
        == lax.broadcasted_iota(jnp.int32, (rows, 128), 1) // DHD
    )

    def spread(values):
        return jnp.where(head_mask, jnp.concatenate([values] * per, axis=0), jnp.zeros((), values.dtype))

    def gather(values):
        return jnp.sum(jnp.where(head_mask, values, 0.0).reshape(per, npos_dev, 128), axis=0)

    finish(loads[5:7])
    attended, inv_l = [], []
    for at in range(groups):
        cols = slice(at * 128, (at + 1) * 128)
        q_wide = spread(q_low[:, cols])
        em = jnp.exp2(dot(q_wide, km_t[cols, :]) * (factor * LOG2E)) * hidden[...]
        ev = jnp.exp2(dot(q_wide, kv_t[cols, :]) * (factor * LOG2E))
        l_inv = 1.0 / (jnp.sum(em, axis=1, keepdims=True) + jnp.sum(ev, axis=1, keepdims=True))
        em_low, ev_low = em.astype(BF16), ev.astype(BF16)
        em_ref[at] = em_low
        ev_ref[at] = ev_low
        attended.append(gather((dot(em_low, vm[:, cols]) + dot(ev_low, vv[:, cols])) * l_inv))
        inv_l.append(l_inv)
    att = jnp.concatenate(attended, axis=1)
    finish(loads[7:])
    second = stream + dot(att.astype(BF16), w_out[...])
    final_hat, final_inv = row_norm(second)
    full = dot(final_hat.astype(BF16), w_pix[...])
    pred[...] = full.astype(BF16)
    error = jnp.where(seen > 0, 0.0, full - target[...].astype(F32)).astype(BF16)
    g_second = norm_back(final_hat, final_inv, dot_nt(error, w_pix[...]))
    g_att = dot_nt(g_second.astype(BF16), w_out[...]).astype(BF16)
    product = g_att.astype(F32) * att
    gq, gk_t, gv = [], [], []
    for at in range(groups):
        cols = slice(at * 128, (at + 1) * 128)
        q_wide = spread(q_low[:, cols])
        g_wide = spread(g_att[:, cols])
        delta = jnp.sum(spread(product[:, cols]), axis=1, keepdims=True)
        l_inv = inv_l[at]
        pv = ev_ref[at].astype(F32) * l_inv
        gs_v = (pv * (dot_nt(g_wide, vv[:, cols]) - delta)).astype(BF16)
        pm = em_ref[at].astype(F32) * l_inv
        gs_m = (pm * (dot_nt(g_wide, vm[:, cols]) - delta)).astype(BF16)
        gq.append(gather(dot_nt(gs_m, km_t[cols, :]) + dot_nt(gs_v, kv_t[cols, :])) * factor)
        gk_t.append(dot_tn(q_wide, gs_v) * factor)
        gv.append(dot_tn(pv.astype(BF16), g_wide).astype(BF16))
    gq_back = head_back_t(q_t, q_inv, jnp.concatenate(gq, axis=1).T).T.astype(BF16)
    g_stream_own = g_second + norm_back(own_hat, own_inv, dot_nt(gq_back, w[0]))
    gk_back = head_back_t(kv_hat, kv_inv, jnp.concatenate(gk_t, axis=0)).T.astype(BF16)
    from_keys = dot_nt(gk_back, w[1]) + dot_nt(jnp.concatenate(gv, axis=1), w[2])
    part = norm_back(vis_hat, vis_inv, from_keys) + dot_tn(hot_low, g_stream_own.astype(BF16))
    g_own[...] = part[:group]
    g_other[...] = part[group:].astype(BF16)


def shards(
    patches,
    vis_index,
    input_weight,
    output_weight,
    embed_weight,
    mask_token,
    position_table,
    decoder_input,
    decoder_output,
    pixel_weight,
    target,
):
    section = lax.axis_index("section")
    column = lax.axis_index("mp")
    member = lax.axis_index(("section", "mp"))
    copies = lax.axis_size("dp")
    ids = jnp.stack([section, column, member]).astype(jnp.int32)
    x_own = patches[0]
    tok, model = x_own.shape
    half = model // 2
    slab, dec_width = embed_weight.shape
    width = output_weight.shape[0]
    heads = width // HD
    group = 8 * tok
    nvis = 2 * group
    pos_dev = position_table.shape[0]
    npos = 16 * pos_dev

    def swap(value):
        return lax.ppermute(value, "section", [(0, 1), (1, 0)])

    def shift(value, by):
        return lax.ppermute(value, "mp", [(i, (i + by) % 8) for i in range(8)])

    def exchange(value, axis):
        return lax.all_to_all(value, axis, 0, 0, tiled=True)

    mine = lax.dynamic_slice_in_dim(x_own, section * half, half, 1)
    theirs = swap(lax.dynamic_slice_in_dim(x_own, (1 - section) * half, half, 1))
    dec_cols = dec_width // copies
    we_t = lax.dynamic_slice_in_dim(embed_weight, lax.axis_index("dp") * dec_cols, dec_cols, 1).T
    we_t = we_t.reshape(dec_cols // 32, 32, slab).transpose(1, 0, 2).reshape(32, -1)
    we_right, we_left = shift(we_t, 1), shift(we_t, -1)
    chunk = jnp.concatenate([mine, theirs])
    right = jnp.concatenate([chunk, we_right], axis=1)
    left = jnp.concatenate([chunk, we_left], axis=1)
    chunks, columns = {0: chunk}, {0: we_t, -1: we_right, 1: we_left}
    for step in range(1, 5):
        right = shift(right, 1)
        if step < 4:
            left = shift(left, -1)
            right, left = lax.optimization_barrier((right, left))
            chunks[step] = left
            columns[step + 1] = left
        chunks[-step] = right
        columns[-step - 1] = right

    index, _ = lax.optimization_barrier((vis_index[0], chunks[-4]))
    row = jnp.zeros((nvis,), jnp.int32)
    row = lax.dynamic_update_slice_in_dim(row, index, member * tok, 0)
    codes = jnp.pad(jnp.stack([row // 32, row % 32]), ((0, 14), (0, dec_width - nvis)))
    table = jnp.concatenate([position_table, codes.astype(BF16)])
    table = lax.all_gather(table, ("section", "mp"), axis=0, tiled=False)

    w_in = input_weight.transpose(1, 0, 2)
    held = sds(w_in.shape, BF16)
    ordered = [chunks[offset] for offset in OFFSETS]
    (wp_part,) = call(
        fold_kernel,
        [sds((copies, dec_cols, width), BF16)],
        ids,
        *[columns[offset] for offset in OFFSETS],
        output_weight,
        scratch=[sds((dec_cols, half), BF16), sds(output_weight.shape, BF16)],
        far=tuple(range(1, 10)),
        copies=1 + 8 * (dec_cols // 32),
    )
    wpt_own = exchange(wp_part, "dp").reshape(dec_width, width)
    ids_late, _ = lax.optimization_barrier((ids, wp_part))
    x_all, p_own, p_send, xp_own, xp_send = call(
        project_kernel,
        [
            sds((2, 8, tok, half), BF16),
            sds((nvis + 16, 3 * width + 128), F32),
            sds((nvis + 16, 3 * width + 128), BF16),
            sds((group, dec_width), F32),
            sds((group, dec_width), BF16),
        ],
        ids_late,
        *ordered,
        w_in,
        embed_weight,
        scratch=[
            sds((2, 8, tok, half), BF16),
            sds((nvis + 16, half), BF16),
            held,
            sds((group, dec_width), F32),
            sds((8, 2 * tok, half), BF16),
        ],
        far=tuple(range(1, 10)),
        far_out=(0, 3),
        copies=13,
    )
    p_other = swap(p_send)
    wpt_other = swap(wpt_own)
    xp_other = swap(xp_send)
    saved = [
        sds((heads, nvis, nvis), BF16),
        sds((nvis, width), F32),
        sds((nvis, width), F32),
        sds((nvis, width), BF16),
        sds((nvis, 128), F32),
    ]
    att, e_enc, q_enc, k_enc, v_enc, aux = call(
        attend_kernel,
        [sds((group, width), BF16)] + saved,
        ids,
        p_own,
        p_other,
        scratch=saved,
        far_out=(1, 2, 3, 4, 5),
        copies=heads + 4,
    )
    embed_part, wpt = call(
        embed_kernel,
        [sds((8, tok, dec_width), BF16), sds((dec_width, width), BF16)],
        ids,
        att,
        wpt_own,
        wpt_other,
        xp_own,
        xp_other,
        scratch=[sds((dec_width, width), BF16), sds((group, dec_width), F32)],
        far=(4,),
        far_out=(1,),
        copies=2,
    )

    def reduce_and_gather(part, beside=None):
        (total,) = call(sum_kernel, [sds((8, tok, dec_width), BF16)], ids, exchange(part, "mp"))
        gathered = exchange(total, "mp").reshape(group, dec_width)
        if beside is not None:
            gathered, _ = lax.optimization_barrier((gathered, beside))
        return gathered, swap(gathered)

    w_dec = decoder_input.transpose(1, 0, 2)
    mask_row = mask_token.reshape(1, dec_width)
    table, embed_part = lax.optimization_barrier((table, embed_part))
    pos_vis, vis_row, hidden, km_t, vm, wq_t, wk_t = call(
        mask_kernel,
        [
            sds((nvis, dec_width), F32),
            sds((1, nvis), jnp.int32),
            sds((1, npos), F32),
            sds((dec_width, npos), BF16),
            sds((npos, dec_width), BF16),
            sds((dec_width, dec_width), BF16),
            sds((dec_width, dec_width), BF16),
        ],
        ids,
        table,
        mask_row,
        w_dec,
        scratch=[sds(table.shape, BF16), sds(w_dec.shape, BF16)],
        far=(1, 3),
        copies=2,
    )
    emb_own, emb_other = reduce_and_gather(embed_part, hidden)

    groups = dec_width // 128
    rows = (128 // DHD) * pos_dev
    prediction, g_own, g_send = call(
        decoder_kernel,
        [
            sds((pos_dev, target.shape[2]), BF16),
            sds((group, dec_width), F32),
            sds((group, dec_width), BF16),
        ],
        ids,
        vis_row,
        emb_own,
        emb_other,
        hidden,
        mask_row,
        wk_t,
        w_dec,
        pos_vis,
        wq_t,
        position_table,
        km_t,
        vm,
        decoder_output,
        pixel_weight,
        target[0],
        scratch=[sds((groups, rows, npos), BF16), sds((groups, rows, nvis), BF16)]
        + [sds(wk_t.shape, BF16), sds(w_dec.shape, BF16), sds(pos_vis.shape, F32), sds(wq_t.shape, BF16)]
        + [sds(position_table.shape, BF16), sds(km_t.shape, BF16), sds(vm.shape, BF16)]
        + [sds(decoder_output.shape, BF16), sds(pixel_weight.shape, BF16), sds(target.shape[1:], BF16)],
        far=tuple(range(6, 16)),
        copies=10,
    )
    g_part = (g_own + swap(g_send).astype(F32)).astype(BF16)
    ge_own, ge_other = reduce_and_gather(g_part.reshape(8, tok, dec_width))

    right, left, gmix, glayer = call(
        encoder_back_kernel,
        [
            sds((2 * tok, half + 128), BF16),
            sds((2 * tok, half + 128), BF16),
            sds((nvis, 3 * width), BF16),
            sds((nvis, slab), F32),
        ],
        ids,
        ge_own,
        ge_other,
        embed_weight,
        wpt,
        e_enc,
        q_enc,
        k_enc,
        v_enc,
        aux,
        x_all,
        w_in,
        scratch=[sds((dec_width, width), BF16)]
        + saved
        + [sds(x_all.shape, BF16), held, sds((nvis, 3 * width), BF16), sds((nvis, slab), F32)]
        + [sds((4 * tok, 3 * width), BF16)],
        far=tuple(range(4, 12)),
        far_out=(2, 3),
        copies=12,
    )
    (parts,) = call(
        feature_kernel,
        [sds((8, 2 * tok, half + 128), BF16)],
        ids,
        gmix,
        glayer,
        aux,
        x_all,
        w_in,
        scratch=[
            sds((nvis, 3 * width), BF16),
            sds((nvis, slab), F32),
            sds((nvis, 128), F32),
            sds(x_all.shape, BF16),
            held,
        ],
        far=(1, 2, 3, 4, 5),
        copies=7,
    )

    def part(offset):
        return lax.dynamic_index_in_dim(parts, (column + offset) % 8, 0, False).astype(F32)

    for step in range(3):
        moved_right, moved_left = shift(right, 1), shift(left, -1)
        right = (moved_right.astype(F32) + part(3 - step)).astype(BF16)
        if step < 2:
            left = (moved_left.astype(F32) + part(-2 + step)).astype(BF16)
    total = shift(right, 1).astype(F32) + moved_left.astype(F32) + part(0)
    (patch_grad,) = call(
        final_kernel,
        [sds((tok, model), BF16)],
        ids,
        total[:tok],
        swap(total[tok:].astype(BF16)),
        x_own,
    )
    return (prediction[None], patch_grad[None])


def solution(mesh):
    group = ("section", "mp")
    in_specs = (
        P("dp", group, None),
        P("dp", group),
        P("section", None, "mp"),
        P("mp", "section"),
        P(group, None),
        P(),
        P(group, None),
        P(),
        P(),
        P(),
        P("dp", group, None),
    )
    out_specs = (P("dp", group, None), P("dp", group, None))
    return jax.shard_map(shards, mesh=mesh, in_specs=in_specs, out_specs=out_specs, check_vma=False)
```

```python
import math

import jax
import jax.numpy as jnp
from jax import lax
from jax.experimental import pallas as pl
from jax.experimental.pallas import tpu as pltpu
from jax.sharding import PartitionSpec as P

HD = 128
DHEADS = 16
DHD = 32
EPSILON = 1e-06
LOG2E = math.log2(math.e)
F32 = jnp.float32
BF16 = jnp.bfloat16
OFFSETS = (0, -1, 1, -2, 2, -3, 3, -4)


def dot(a, b):
    return lax.dot_general(a, b, (((1,), (0,)), ((), ())), preferred_element_type=F32)


def dot_nt(a, b):
    return lax.dot_general(a, b, (((1,), (1,)), ((), ())), preferred_element_type=F32)


def dot_tn(a, b):
    return lax.dot_general(a, b, (((0,), (0,)), ((), ())), preferred_element_type=F32)


def row_norm(values, axis=-1):
    centre = jnp.mean(values, axis=axis, keepdims=True)
    centered = values - centre
    inverse = lax.rsqrt(jnp.mean(centered * centered, axis=axis, keepdims=True) + EPSILON)
    return centered * inverse, inverse


def norm_back(normed, inverse, gradient, axis=-1):
    mean_grad = jnp.mean(gradient, axis=axis, keepdims=True)
    mean_dot = jnp.mean(gradient * normed, axis=axis, keepdims=True)
    return inverse * (gradient - mean_grad - normed * mean_dot)


def lanes(columns, rows):
    lane = lax.broadcasted_iota(jnp.int32, (rows, 128), 1)
    out = jnp.zeros((rows, 128), F32)
    for at, column in enumerate(columns):
        out = jnp.where(lane == at, column, out)
    return out


def call(kernel, outs, *args, scratch=(), far=(), far_out=(), copies=0, limit=58):
    specs = [pl.BlockSpec(memory_space=pltpu.SMEM)]
    for at in range(1, len(args)):
        specs.append(pl.BlockSpec(memory_space=pl.ANY if at in far else pltpu.VMEM))
    out_specs = [
        pl.BlockSpec(memory_space=pl.ANY if at in far_out else pltpu.VMEM) for at in range(len(outs))
    ]
    scratch = [pltpu.VMEM(shape.shape, shape.dtype) for shape in scratch]
    if copies:
        scratch.append(pltpu.SemaphoreType.DMA((copies,)))
    return pl.pallas_call(
        kernel,
        out_shape=tuple(outs),
        in_specs=specs,
        out_specs=tuple(out_specs),
        scratch_shapes=scratch,
        compiler_params=pltpu.CompilerParams(vmem_limit_bytes=limit * 2**20),
    )(*args)


def start(sems, first, *pairs):
    copies = [
        pltpu.make_async_copy(source, target, sems.at[first + at]) for at, (source, target) in enumerate(pairs)
    ]
    for copy in copies:
        copy.start()
    return copies


def finish(copies):
    for copy in copies:
        copy.wait()


def sds(shape, dtype):
    return jax.ShapeDtypeStruct(shape, dtype)


def fold_kernel(ids, *refs):
    sources, wo_in, out = refs[:8], refs[8], refs[9]
    wt, wo, sems = refs[10:]
    half = wo.shape[1]
    slab = half // 8
    pieces = wt.shape[0] // 32
    loads = start(sems, 0, (wo_in, wo))
    for index, (source, offset) in enumerate(zip(sources, OFFSETS)):
        column = pl.multiple_of(lax.rem(ids[1] + offset + 8, 8) * slab, 128)
        base = source.shape[1] - pieces * slab
        for piece in range(pieces):
            target = wt.at[pl.ds(piece * 32, 32), pl.ds(column, slab)]
            source_part = source.at[:, pl.ds(base + piece * slab, slab)]
            loads += start(sems, 1 + index * pieces + piece, (source_part, target))
    finish(loads)
    total = dot_nt(wt[...], wo[...]).astype(BF16)
    for at in range(out.shape[0]):
        out[at] = total


def split3(values):
    first = values.astype(BF16).astype(F32)
    second = (values - first).astype(BF16).astype(F32)
    return [first, second, values - first - second]


def project_kernel(ids, *refs):
    chunks = refs[:8]
    w, we = refs[8:10]
    x_out, p_out, xp_own, xp_send = refs[10:14]
    xs, xc, held, xp, held_chunks, p_send, sems = refs[14:]
    half, width = held.shape[1:]
    arrivals = start(
        sems, 6, *[(chunk.at[:, pl.ds(0, half)], held_chunks.at[at]) for at, chunk in enumerate(chunks)]
    )
    loads = start(sems, 0, *[(w.at[at], held.at[at]) for at in range(3)])
    slab = half // 8
    tok = xs.shape[2]
    group = 8 * tok
    m = ids[1]
    for index, offset in enumerate(OFFSETS):
        at = lax.rem(m + offset + 8, 8)
        arrivals[index].wait()
        value = held_chunks[index]
        xs[0, at] = value[:tok]
        xs[1, at] = value[tok:]
        wide = value.astype(F32)
        centre = jnp.mean(wide, axis=1, keepdims=True)
        centered = wide - centre
        spread = jnp.sum(centered * centered, axis=1, keepdims=True)
        low = centered.astype(BF16)
        send = lanes(split3(centre) + split3(spread), 2 * tok).astype(BF16)
        row = pl.multiple_of(at * tok, tok)
        for rel in range(2):
            part = slice(rel * tok, (rel + 1) * tok)
            xc[pl.ds(row + rel * group, tok), :] = low[part]
            p_send[pl.ds(row + rel * group, tok), 3 * width :] = send[part]
    xc[2 * group :, :] = jnp.ones((16, half), BF16)
    p_send[2 * group :, 3 * width :] = jnp.zeros((16, 128), BF16)
    for at in range(3):
        loads[at].wait()
        p_send[:, at * width : (at + 1) * width] = dot(xc[...], held[at]).astype(BF16)
    stores = start(sems, 3, (p_send, p_out), (xs, x_out))
    column = pl.multiple_of(m * slab, 128)
    raw = jnp.concatenate([xs[0, :, :, pl.ds(column, slab)], xs[1, :, :, pl.ds(column, slab)]])
    part = dot(raw.reshape(2 * group, slab), we[...])
    xp[...] = part[:group]
    stores += start(sems, 5, (xp, xp_own))
    xp_send[...] = part[group:].astype(BF16)
    finish(stores)


def attend_kernel(ids, p_own, p_other, att, *refs):
    saved = refs[:5]
    e_out, q_out, k_out, v_out, aux = refs[5:10]
    sems = refs[10]
    rows = p_own.shape[0] - 16
    group = rows // 2
    width = (p_own.shape[1] - 128) // 3
    heads = width // HD
    model = 2 * 8 * width

    def moments(p):
        stats = p[:rows, 3 * width :].astype(F32)
        parts = [stats[:, at : at + 1] for at in range(6)]
        return parts[0] + parts[1] + parts[2], parts[3] + parts[4] + parts[5]

    def exchanged(values):
        return jnp.concatenate([values[group:], values[:group]])

    m_own, s_own = moments(p_own)
    m_other, s_other = [exchanged(value) for value in moments(p_other)]
    gap = (m_own - m_other) * 0.5
    centre = (m_own + m_other) * 0.5
    inverse = lax.rsqrt((s_own + s_other) / model + gap * gap + EPSILON)
    slope = p_own[rows : rows + 1, : 3 * width].astype(F32) - p_other[rows : rows + 1, : 3 * width].astype(F32)
    inv_q, inv_k, inv_l = [], [], []
    factor = LOG2E * HD**-0.5
    stores = []

    def mixture(at):
        cols = slice(at * HD, (at + 1) * HD)
        other = exchanged(p_other[:rows, cols]).astype(F32)
        return inverse * (p_own[:rows, cols].astype(F32) + other + gap * slope[:, cols])

    for head in range(heads):
        cols = slice(head * HD, (head + 1) * HD)
        q_hat, q_inv = row_norm(mixture(head))
        k_hat, k_inv = row_norm(mixture(heads + head))
        v_low = mixture(2 * heads + head).astype(BF16)
        q_low, k_low = q_hat.astype(BF16), k_hat.astype(BF16)
        e = jnp.exp2(dot_nt(q_low, k_low) * factor)
        l_inv = 1.0 / jnp.sum(e, axis=1, keepdims=True)
        e_low = e.astype(BF16)
        e_out[head] = e_low
        stores += start(sems, head, (e_out.at[head], saved[0].at[head]))
        att[:, cols] = (dot(e_low[:group], v_low) * l_inv[:group]).astype(BF16)
        q_out[:, cols] = q_low
        k_out[:, cols] = k_low
        v_out[:, cols] = v_low
        inv_q.append(q_inv)
        inv_k.append(k_inv)
        inv_l.append(l_inv)
    aux[...] = lanes([centre, inverse] + inv_l + inv_q + inv_k, rows)
    stores += start(sems, heads, (q_out, saved[1]), (k_out, saved[2]), (v_out, saved[3]), (aux, saved[4]))
    finish(stores)


def embed_kernel(ids, att, wpt_own, wpt_other, xp_own, xp_other, out, wpt, wpt_held, xp, sems):
    load = start(sems, 0, (xp_own, xp))
    total = (wpt_own[...].astype(F32) + wpt_other[...].astype(F32)).astype(BF16)
    wpt_held[...] = total
    store = start(sems, 1, (wpt_held, wpt))
    part = dot_nt(att[...], total) + xp_other[...].astype(F32)
    finish(load)
    out[...] = (part + xp[...]).astype(BF16).reshape(out.shape)
    finish(store)


def sum_kernel(ids, parts, out):
    total = jnp.sum(parts[...].astype(F32), axis=0).astype(BF16)
    for at in range(out.shape[0]):
        out[at] = total


def encoder_back_kernel(ids, g_own, g_other, we, *refs):
    sources = refs[:7]
    w = refs[7]
    right, left, parts_out = refs[8:11]
    wpt, e_in, q_in, k_in, v_in, aux, x_in, held, gmix, out, sems = refs[11:]
    loads = start(sems, 0, *zip(sources[:6], (wpt, e_in, q_in, k_in, v_in, aux)))
    w_loads = start(sems, 6, *[(w.at[at], held.at[at]) for at in range(3)])
    w_loads += start(sems, 9, (sources[6], x_in))
    rows, width = q_in.shape
    heads = width // HD
    half = held.shape[1]
    slab = half // 8
    tok = x_in.shape[2]
    m = ids[1]
    factor = HD**-0.5
    gemb = jnp.concatenate([g_own[...], g_other[...]])
    glayer = dot_nt(gemb, we[...])
    loads[0].wait()
    gatt = dot(gemb, wpt[...]).astype(BF16)
    finish(loads[1:])
    for head in range(heads):
        cols = slice(head * HD, (head + 1) * HD)
        g_head = gatt[:, cols]
        q_low, k_low, v_low = q_in[:, cols], k_in[:, cols], v_in[:, cols]
        l_inv = aux[:, 2 + head : 3 + head]
        q_inv = aux[:, 2 + heads + head : 3 + heads + head]
        k_inv = aux[:, 2 + 2 * heads + head : 3 + 2 * heads + head]
        p = e_in[head].astype(F32) * l_inv
        gp = dot_nt(g_head, v_low)
        delta = jnp.sum(p * gp, axis=1, keepdims=True)
        gs = (p * (gp - delta)).astype(BF16)
        gq = dot(gs, k_low) * factor
        gk = dot_tn(gs, q_low) * factor
        gv = dot_tn(p.astype(BF16), g_head)
        gmix[:, cols] = norm_back(q_low.astype(F32), q_inv, gq).astype(BF16)
        gmix[:, width + head * HD : width + (head + 1) * HD] = norm_back(k_low.astype(F32), k_inv, gk).astype(BF16)
        gmix[:, 2 * width + head * HD : 2 * width + (head + 1) * HD] = gv.astype(BF16)
    finish(w_loads)
    centre, inverse = aux[:, 0:1], aux[:, 1:2]
    total = jnp.zeros((rows, 1), F32)
    total_dot = jnp.zeros((rows, 1), F32)
    for block in range(8):
        cols = slice(block * slab, (block + 1) * slab)
        g = dot_nt(gmix[:, :width], held[0, cols, :])
        g = g + dot_nt(gmix[:, width : 2 * width], held[1, cols, :])
        g = g + dot_nt(gmix[:, 2 * width :], held[2, cols, :])
        normed = (x_in[:, :, :, cols].reshape(rows, slab).astype(F32) - centre) * inverse
        total = total + jnp.sum(g, axis=1, keepdims=True)
        total_dot = total_dot + jnp.sum(g * normed, axis=1, keepdims=True)
        mine = jnp.where(block == m, 1.0, 0.0)
        value = (g * inverse + glayer * mine).astype(BF16).reshape(2, 8, tok, slab)
        out[:, :tok, cols] = value[0]
        out[:, tok:, cols] = value[1]
    sums = lanes((total, total_dot), rows).astype(BF16).reshape(2, 8, tok, 128)
    out[:, :tok, half:] = sums[0]
    out[:, tok:, half:] = sums[1]
    store = start(sems, 10, (out, parts_out))
    right[...] = out[lax.rem(m + 4, 8)]
    left[...] = out[lax.rem(m + 5, 8)]
    finish(store)


def final_kernel(ids, both, other, x_own, out):
    s = ids[0]
    tok = x_own.shape[0]
    half = x_own.shape[1] // 2
    model = x_own.shape[1]
    normed, inverse = row_norm(x_own[...].astype(F32))
    mine, theirs = both[:tok, :], other[...].astype(F32)
    total = (mine[:, half : half + 1] + theirs[:, half : half + 1]) / model
    total_dot = (mine[:, half + 1 : half + 2] + theirs[:, half + 1 : half + 2]) / model
    first = jnp.where(s == 0, mine[:, :half], theirs[:, :half])
    second = jnp.where(s == 0, theirs[:, :half], mine[:, :half])
    out[:, :half] = (first - inverse * (total + normed[:, :half] * total_dot)).astype(BF16)
    out[:, half:] = (second - inverse * (total + normed[:, half:] * total_dot)).astype(BF16)


def head_norm_t(values):
    width, n = values.shape
    hat, inverse = row_norm(values.reshape(DHEADS, DHD, n), axis=1)
    return hat.reshape(width, n), inverse


def head_back_t(hat, inverse, gradient):
    width, n = hat.shape
    back = norm_back(
        hat.reshape(DHEADS, DHD, n), inverse, gradient.reshape(DHEADS, DHD, n), axis=1
    )
    return back.reshape(width, n)


def mask_kernel(ids, table_in, mask, w_in, w_out_in, w_pix_in, target_in, pos_own_in, *refs):
    pos_vis, vis_row, hidden, k_t, v, wq_t, wk_t, w, w_out, w_pix, target, pos_own, table, sems = refs
    loads = start(
        sems,
        0,
        (w_in, w),
        (table_in, table),
        (w_out_in, w_out),
        (w_pix_in, w_pix),
        (target_in, target),
        (pos_own_in, pos_own),
    )
    loads[0].wait()
    wq_t[...] = w[0].T
    wk_t[...] = w[1].T
    loads[1].wait()
    members, pos_dev = table.shape[0], table.shape[1] - 16
    npos, width = members * pos_dev, table.shape[2]
    nvis = vis_row.shape[1]
    pos_all = table[:, :pos_dev, :].reshape(npos, width)
    codes = jnp.sum(table[:, pos_dev:, :].astype(F32), axis=0)
    row = codes[0:1, :nvis] * 32.0 + codes[1:2, :nvis]
    other = jnp.concatenate([row[:, nvis // 2 :], row[:, : nvis // 2]], axis=1)
    vis = jnp.where(ids[0] == 0, row, other).astype(jnp.int32)
    vis_row[...] = vis
    hot = jnp.where(lax.broadcasted_iota(jnp.int32, (npos, nvis), 0) == vis, 1.0, 0.0).astype(BF16)
    pos_vis[...] = dot_tn(hot, pos_all)
    hidden[...] = 1.0 - dot_nt(jnp.ones((16, nvis), BF16), hot)[0:1, :]
    hat, _ = row_norm(pos_all.astype(F32) + mask[...].astype(F32))
    low = hat.astype(BF16)
    key_hat, _ = head_norm_t(dot_nt(wk_t[...], low))
    k_t[...] = key_hat.astype(BF16)
    v[...] = dot(low, w[2]).astype(BF16)
    finish(loads[2:])


def decoder_kernel(
    ids, emb_own, emb_other, mask, pos_vis, vis_row, hidden, km_t, vm, wq_t, wk_t, w, w_out, w_pix, target, pos_own,
    pred, g_own, g_other, em_ref, ev_ref,
):
    npos_dev, width = pos_own.shape
    nvis = pos_vis.shape[0]
    group = nvis // 2
    member = ids[2]
    groups = width // 128
    per = 128 // DHD
    rows = per * npos_dev
    factor = DHD**-0.5
    emb = jnp.concatenate([emb_own[...], emb_other[...]])
    vis_hat, vis_inv = row_norm(emb.astype(F32) + pos_vis[...])
    vis_low = vis_hat.astype(BF16)
    kv_hat, kv_inv = head_norm_t(dot_nt(wk_t[...], vis_low))
    kv_t = kv_hat.astype(BF16)
    vv = dot(vis_low, w[2]).astype(BF16)
    position = lax.broadcasted_iota(jnp.int32, (npos_dev, nvis), 0) + member * npos_dev
    hot = jnp.where(position == vis_row[...], 1.0, 0.0)
    seen = jnp.sum(hot, axis=1, keepdims=True)
    hot_low = hot.astype(BF16)
    filled = dot(hot_low, emb) + (1.0 - seen) * mask[...].astype(F32)
    stream = filled + pos_own[...].astype(F32)
    own_hat, own_inv = row_norm(stream)
    q_t, q_inv = head_norm_t(dot_nt(wq_t[...], own_hat.astype(BF16)))
    q_low = q_t.T.astype(BF16)
    head_mask = (
        lax.broadcasted_iota(jnp.int32, (rows, 128), 0) // npos_dev
        == lax.broadcasted_iota(jnp.int32, (rows, 128), 1) // DHD
    )

    def spread(values):
        return jnp.where(head_mask, jnp.concatenate([values] * per, axis=0), jnp.zeros((), values.dtype))

    def gather(values):
        return jnp.sum(jnp.where(head_mask, values, 0.0).reshape(per, npos_dev, 128), axis=0)

    attended, inv_l = [], []
    for at in range(groups):
        cols = slice(at * 128, (at + 1) * 128)
        q_wide = spread(q_low[:, cols])
        em = jnp.exp2(dot(q_wide, km_t[cols, :]) * (factor * LOG2E)) * hidden[...]
        ev = jnp.exp2(dot(q_wide, kv_t[cols, :]) * (factor * LOG2E))
        l_inv = 1.0 / (jnp.sum(em, axis=1, keepdims=True) + jnp.sum(ev, axis=1, keepdims=True))
        em_low, ev_low = em.astype(BF16), ev.astype(BF16)
        em_ref[at] = em_low
        ev_ref[at] = ev_low
        attended.append(gather((dot(em_low, vm[:, cols]) + dot(ev_low, vv[:, cols])) * l_inv))
        inv_l.append(l_inv)
    att = jnp.concatenate(attended, axis=1)
    second = stream + dot(att.astype(BF16), w_out[...])
    final_hat, final_inv = row_norm(second)
    full = dot(final_hat.astype(BF16), w_pix[...])
    pred[...] = full.astype(BF16)
    error = jnp.where(seen > 0, 0.0, full - target[...].astype(F32)).astype(BF16)
    g_second = norm_back(final_hat, final_inv, dot_nt(error, w_pix[...]))
    g_att = dot_nt(g_second.astype(BF16), w_out[...]).astype(BF16)
    product = g_att.astype(F32) * att
    gq, gk_t, gv = [], [], []
    for at in range(groups):
        cols = slice(at * 128, (at + 1) * 128)
        q_wide = spread(q_low[:, cols])
        g_wide = spread(g_att[:, cols])
        delta = jnp.sum(spread(product[:, cols]), axis=1, keepdims=True)
        l_inv = inv_l[at]
        pv = ev_ref[at].astype(F32) * l_inv
        gs_v = (pv * (dot_nt(g_wide, vv[:, cols]) - delta)).astype(BF16)
        pm = em_ref[at].astype(F32) * l_inv
        gs_m = (pm * (dot_nt(g_wide, vm[:, cols]) - delta)).astype(BF16)
        gq.append(gather(dot_nt(gs_m, km_t[cols, :]) + dot_nt(gs_v, kv_t[cols, :])) * factor)
        gk_t.append(dot_tn(q_wide, gs_v) * factor)
        gv.append(dot_tn(pv.astype(BF16), g_wide).astype(BF16))
    gq_back = head_back_t(q_t, q_inv, jnp.concatenate(gq, axis=1).T).T.astype(BF16)
    g_stream_own = g_second + norm_back(own_hat, own_inv, dot_nt(gq_back, w[0]))
    gk_back = head_back_t(kv_hat, kv_inv, jnp.concatenate(gk_t, axis=0)).T.astype(BF16)
    from_keys = dot_nt(gk_back, w[1]) + dot_nt(jnp.concatenate(gv, axis=1), w[2])
    part = norm_back(vis_hat, vis_inv, from_keys) + dot_tn(hot_low, g_stream_own.astype(BF16))
    g_own[...] = part[:group]
    g_other[...] = part[group:].astype(BF16)


def shards(
    patches,
    vis_index,
    input_weight,
    output_weight,
    embed_weight,
    mask_token,
    position_table,
    decoder_input,
    decoder_output,
    pixel_weight,
    target,
):
    section = lax.axis_index("section")
    column = lax.axis_index("mp")
    member = lax.axis_index(("section", "mp"))
    copies = lax.axis_size("dp")
    ids = jnp.stack([section, column, member]).astype(jnp.int32)
    x_own = patches[0]
    tok, model = x_own.shape
    half = model // 2
    slab, dec_width = embed_weight.shape
    width = output_weight.shape[0]
    heads = width // HD
    group = 8 * tok
    nvis = 2 * group
    pos_dev = position_table.shape[0]
    npos = 16 * pos_dev

    def swap(value):
        return lax.ppermute(value, "section", [(0, 1), (1, 0)])

    def shift(value, by):
        return lax.ppermute(value, "mp", [(i, (i + by) % 8) for i in range(8)])

    def exchange(value, axis):
        return lax.all_to_all(value, axis, 0, 0, tiled=True)

    mine = lax.dynamic_slice_in_dim(x_own, section * half, half, 1)
    theirs = swap(lax.dynamic_slice_in_dim(x_own, (1 - section) * half, half, 1))
    dec_cols = dec_width // copies
    we_t = lax.dynamic_slice_in_dim(embed_weight, lax.axis_index("dp") * dec_cols, dec_cols, 1).T
    we_t = we_t.reshape(dec_cols // 32, 32, slab).transpose(1, 0, 2).reshape(32, -1)
    we_right, we_left = shift(we_t, 1), shift(we_t, -1)
    chunk = jnp.concatenate([mine, theirs])
    right = jnp.concatenate([chunk, we_right], axis=1)
    left = jnp.concatenate([chunk, we_left], axis=1)
    chunks, columns = {0: right}, {0: we_t, -1: we_right, 1: we_left}
    for step in range(1, 5):
        right = shift(right, 1)
        if step < 4:
            left = shift(left, -1)
            right, left = lax.optimization_barrier((right, left))
            chunks[step] = left
            columns[step + 1] = left
        chunks[-step] = right
        columns[-step - 1] = right

    row = jnp.zeros((nvis,), jnp.int32)
    row = lax.dynamic_update_slice_in_dim(row, vis_index[0], member * tok, 0)
    codes = jnp.pad(jnp.stack([row // 32, row % 32]), ((0, 14), (0, dec_width - nvis)))
    table = jnp.concatenate([position_table, codes.astype(BF16)])
    table, _ = lax.optimization_barrier((table, chunks[-3]))
    table = lax.all_gather(table, ("section", "mp"), axis=0, tiled=False)

    w_in = input_weight.transpose(1, 0, 2)
    held = sds(w_in.shape, BF16)
    ordered = [chunks[offset] for offset in OFFSETS]
    (wp_part,) = call(
        fold_kernel,
        [sds((copies, dec_cols, width), BF16)],
        ids,
        *[columns[offset] for offset in OFFSETS],
        output_weight,
        scratch=[sds((dec_cols, half), BF16), sds(output_weight.shape, BF16)],
        far=tuple(range(1, 10)),
        copies=1 + 8 * (dec_cols // 32),
    )
    wpt_own = exchange(wp_part, "dp").reshape(dec_width, width)
    ids_late, _ = lax.optimization_barrier((ids, wp_part))
    x_all, p_own, xp_own, xp_send = call(
        project_kernel,
        [
            sds((2, 8, tok, half), BF16),
            sds((nvis + 16, 3 * width + 128), BF16),
            sds((group, dec_width), F32),
            sds((group, dec_width), BF16),
        ],
        ids_late,
        *ordered,
        w_in,
        embed_weight,
        scratch=[
            sds((2, 8, tok, half), BF16),
            sds((nvis + 16, half), BF16),
            held,
            sds((group, dec_width), F32),
            sds((8, 2 * tok, half), BF16),
            sds((nvis + 16, 3 * width + 128), BF16),
        ],
        far=tuple(range(1, 10)),
        far_out=(0, 1, 2),
        copies=14,
    )
    p_other = swap(p_own)
    wpt_other = swap(wpt_own)
    xp_other = swap(xp_send)
    saved = [
        sds((heads, nvis, nvis), BF16),
        sds((nvis, width), BF16),
        sds((nvis, width), BF16),
        sds((nvis, width), BF16),
        sds((nvis, 128), F32),
    ]
    att, e_enc, q_enc, k_enc, v_enc, aux = call(
        attend_kernel,
        [sds((group, width), BF16)] + saved,
        ids,
        p_own,
        p_other,
        scratch=saved,
        far_out=(1, 2, 3, 4, 5),
        copies=heads + 4,
    )
    embed_part, wpt = call(
        embed_kernel,
        [sds((8, tok, dec_width), BF16), sds((dec_width, width), BF16)],
        ids,
        att,
        wpt_own,
        wpt_other,
        xp_own,
        xp_other,
        scratch=[sds((dec_width, width), BF16), sds((group, dec_width), F32)],
        far=(4,),
        far_out=(1,),
        copies=2,
        limit=24,
    )

    w_dec = decoder_input.transpose(1, 0, 2)
    mask_row = mask_token.reshape(1, dec_width)
    (embed_sum,) = call(sum_kernel, [sds((8, tok, dec_width), BF16)], ids, exchange(embed_part, "mp"), limit=16)
    table, _ = lax.optimization_barrier((table, embed_sum))
    weights = (w_dec, decoder_output, pixel_weight, target[0], position_table)
    prepared = call(
        mask_kernel,
        [
            sds((nvis, dec_width), F32),
            sds((1, nvis), jnp.int32),
            sds((1, npos), F32),
            sds((dec_width, npos), BF16),
            sds((npos, dec_width), BF16),
            sds((dec_width, dec_width), BF16),
            sds((dec_width, dec_width), BF16),
        ]
        + [sds(weight.shape, BF16) for weight in weights],
        ids,
        table,
        mask_row,
        *weights,
        scratch=[sds(table.shape, BF16)],
        far=(1, 3, 4, 5, 6, 7),
        copies=6,
        limit=32,
    )
    emb_own = exchange(embed_sum, "mp").reshape(group, dec_width)
    emb_own, _ = lax.optimization_barrier((emb_own, prepared[2]))
    emb_other = swap(emb_own)

    groups = dec_width // 128
    rows = (128 // DHD) * pos_dev
    prediction, g_own, g_send = call(
        decoder_kernel,
        [
            sds((pos_dev, target.shape[2]), BF16),
            sds((group, dec_width), F32),
            sds((group, dec_width), BF16),
        ],
        ids,
        emb_own,
        emb_other,
        mask_row,
        *prepared,
        scratch=[sds((groups, rows, npos), BF16), sds((groups, rows, nvis), BF16)],
        limit=32,
    )
    g_part = (g_own + swap(g_send).astype(F32)).astype(BF16).reshape(8, tok, dec_width)
    (g_sum,) = call(sum_kernel, [sds((8, tok, dec_width), BF16)], ids, exchange(g_part, "mp"), limit=16)
    ge_own = exchange(g_sum, "mp").reshape(group, dec_width)
    ge_other = swap(ge_own)

    right, left, parts = call(
        encoder_back_kernel,
        [
            sds((2 * tok, half + 128), BF16),
            sds((2 * tok, half + 128), BF16),
            sds((8, 2 * tok, half + 128), BF16),
        ],
        ids,
        ge_own,
        ge_other,
        embed_weight,
        wpt,
        e_enc,
        q_enc,
        k_enc,
        v_enc,
        aux,
        x_all,
        w_in,
        scratch=[sds((dec_width, width), BF16)]
        + saved
        + [sds(x_all.shape, BF16), held, sds((nvis, 3 * width), BF16), sds((8, 2 * tok, half + 128), BF16)],
        far=tuple(range(4, 12)),
        far_out=(2,),
        copies=11,
    )

    def part(offset):
        return lax.dynamic_index_in_dim(parts, (column + offset) % 8, 0, False).astype(F32)

    for step in range(3):
        right, left = lax.optimization_barrier((shift(right, 1), shift(left, -1)))
        right = (right.astype(F32) + part(3 - step)).astype(BF16)
        if step < 2:
            left = (left.astype(F32) + part(-2 + step)).astype(BF16)
    total = shift(right, 1).astype(F32) + left.astype(F32) + part(0)
    (patch_grad,) = call(
        final_kernel,
        [sds((tok, model), BF16)],
        ids,
        total,
        swap(total[tok:].astype(BF16)),
        x_own,
        limit=16,
    )
    return (prediction[None], patch_grad[None])


def solution(mesh):
    group = ("section", "mp")
    in_specs = (
        P("dp", group, None),
        P("dp", group),
        P("section", None, "mp"),
        P("mp", "section"),
        P(group, None),
        P(),
        P(group, None),
        P(),
        P(),
        P(),
        P("dp", group, None),
    )
    out_specs = (P("dp", group, None), P("dp", group, None))
    return jax.shard_map(shards, mesh=mesh, in_specs=in_specs, out_specs=out_specs, check_vma=False)
```

```python
import math

import jax
import jax.numpy as jnp
from jax import lax
from jax.experimental import pallas as pl
from jax.experimental.pallas import tpu as pltpu
from jax.sharding import PartitionSpec as P

HD = 128
DHEADS = 16
DHD = 32
EPSILON = 1e-06
LOG2E = math.log2(math.e)
F32 = jnp.float32
BF16 = jnp.bfloat16
OFFSETS = (0, -1, 1, -2, 2, -3, 3, -4)


def dot(a, b):
    return lax.dot_general(a, b, (((1,), (0,)), ((), ())), preferred_element_type=F32)


def dot_nt(a, b):
    return lax.dot_general(a, b, (((1,), (1,)), ((), ())), preferred_element_type=F32)


def dot_tn(a, b):
    return lax.dot_general(a, b, (((0,), (0,)), ((), ())), preferred_element_type=F32)


def row_norm(values, axis=-1):
    centre = jnp.mean(values, axis=axis, keepdims=True)
    centered = values - centre
    inverse = lax.rsqrt(jnp.mean(centered * centered, axis=axis, keepdims=True) + EPSILON)
    return centered * inverse, inverse


def norm_back(normed, inverse, gradient, axis=-1):
    mean_grad = jnp.mean(gradient, axis=axis, keepdims=True)
    mean_dot = jnp.mean(gradient * normed, axis=axis, keepdims=True)
    return inverse * (gradient - mean_grad - normed * mean_dot)


def lanes(columns, rows):
    lane = lax.broadcasted_iota(jnp.int32, (rows, 128), 1)
    out = jnp.zeros((rows, 128), F32)
    for at, column in enumerate(columns):
        out = jnp.where(lane == at, column, out)
    return out


def call(kernel, outs, *args, scratch=(), far=(), far_out=(), copies=0, limit=58):
    specs = [pl.BlockSpec(memory_space=pltpu.SMEM)]
    for at in range(1, len(args)):
        specs.append(pl.BlockSpec(memory_space=pl.ANY if at in far else pltpu.VMEM))
    out_specs = [
        pl.BlockSpec(memory_space=pl.ANY if at in far_out else pltpu.VMEM) for at in range(len(outs))
    ]
    scratch = [pltpu.VMEM(shape.shape, shape.dtype) for shape in scratch]
    if copies:
        scratch.append(pltpu.SemaphoreType.DMA((copies,)))
    return pl.pallas_call(
        kernel,
        out_shape=tuple(outs),
        in_specs=specs,
        out_specs=tuple(out_specs),
        scratch_shapes=scratch,
        compiler_params=pltpu.CompilerParams(vmem_limit_bytes=limit * 2**20),
    )(*args)


def start(sems, first, *pairs):
    copies = [
        pltpu.make_async_copy(source, target, sems.at[first + at]) for at, (source, target) in enumerate(pairs)
    ]
    for copy in copies:
        copy.start()
    return copies


def finish(copies):
    for copy in copies:
        copy.wait()


def sds(shape, dtype):
    return jax.ShapeDtypeStruct(shape, dtype)


def fold_kernel(ids, *refs):
    sources, wo_in, out = refs[:8], refs[8], refs[9]
    wt, wo, sems = refs[10:]
    half = wo.shape[1]
    slab = half // 8
    pieces = wt.shape[0] // 32
    loads = start(sems, 0, (wo_in, wo))
    for index, (source, offset) in enumerate(zip(sources, OFFSETS)):
        column = pl.multiple_of(lax.rem(ids[1] + offset + 8, 8) * slab, 128)
        base = source.shape[1] - pieces * slab
        for piece in range(pieces):
            target = wt.at[pl.ds(piece * 32, 32), pl.ds(column, slab)]
            source_part = source.at[:, pl.ds(base + piece * slab, slab)]
            loads += start(sems, 1 + index * pieces + piece, (source_part, target))
    finish(loads)
    out[...] = dot_nt(wt[...], wo[...]).astype(BF16)


def split3(values):
    first = values.astype(BF16).astype(F32)
    second = (values - first).astype(BF16).astype(F32)
    return [first, second, values - first - second]


def project_kernel(ids, *refs):
    chunks = refs[:8]
    w, we, wp_own, wp_other = refs[8:12]
    x_out, p_out, xp_own, xp_send, wp_out = refs[12:17]
    xs, xc, held, xp, held_chunks, p_send, sems = refs[17:]
    half, width = held.shape[1:]
    arrivals = start(
        sems, 6, *[(chunk.at[:, pl.ds(0, half)], held_chunks.at[at]) for at, chunk in enumerate(chunks)]
    )
    loads = start(sems, 0, *[(w.at[at], held.at[at]) for at in range(3)])
    slab = half // 8
    tok = xs.shape[2]
    group = 8 * tok
    m = ids[1]
    for index, offset in enumerate(OFFSETS):
        at = lax.rem(m + offset + 8, 8)
        arrivals[index].wait()
        value = held_chunks[index]
        xs[0, at] = value[:tok]
        xs[1, at] = value[tok:]
        wide = value.astype(F32)
        centre = jnp.mean(wide, axis=1, keepdims=True)
        centered = wide - centre
        spread = jnp.sum(centered * centered, axis=1, keepdims=True)
        low = centered.astype(BF16)
        send = lanes(split3(centre) + split3(spread), 2 * tok).astype(BF16)
        row = pl.multiple_of(at * tok, tok)
        for rel in range(2):
            part = slice(rel * tok, (rel + 1) * tok)
            xc[pl.ds(row + rel * group, tok), :] = low[part]
            p_send[pl.ds(row + rel * group, tok), 3 * width :] = send[part]
    wp = (wp_own[...].astype(F32) + wp_other[...].astype(F32)).astype(BF16)
    for at in range(wp_out.shape[0]):
        wp_out[at] = wp
    xc[2 * group :, :] = jnp.ones((16, half), BF16)
    p_send[2 * group :, 3 * width :] = jnp.zeros((16, 128), BF16)
    stores = []
    for at in range(3):
        loads[at].wait()
        p_send[:, at * width : (at + 1) * width] = dot(xc[...], held[at]).astype(BF16)
        cols = pl.ds(at * width, width if at < 2 else width + 128)
        stores += start(sems, 14 + at, (p_send.at[:, cols], p_out.at[:, cols]))
    stores += start(sems, 3, (xs, x_out))
    column = pl.multiple_of(m * slab, 128)
    raw = jnp.concatenate([xs[0, :, :, pl.ds(column, slab)], xs[1, :, :, pl.ds(column, slab)]])
    part = dot(raw.reshape(2 * group, slab), we[...])
    xp[...] = part[:group]
    stores += start(sems, 5, (xp, xp_own))
    xp_send[...] = part[group:].astype(BF16)
    finish(stores)


def attend_kernel(ids, p_own, p_other, att, *refs):
    saved = refs[:5]
    e_out, q_out, k_out, v_out, aux = refs[5:10]
    sems = refs[10]
    rows = p_own.shape[0] - 16
    group = rows // 2
    width = (p_own.shape[1] - 128) // 3
    heads = width // HD
    model = 2 * 8 * width

    def moments(p):
        stats = p[:rows, 3 * width :].astype(F32)
        parts = [stats[:, at : at + 1] for at in range(6)]
        return parts[0] + parts[1] + parts[2], parts[3] + parts[4] + parts[5]

    def exchanged(values):
        return jnp.concatenate([values[group:], values[:group]])

    m_own, s_own = moments(p_own)
    m_other, s_other = [exchanged(value) for value in moments(p_other)]
    gap = (m_own - m_other) * 0.5
    centre = (m_own + m_other) * 0.5
    inverse = lax.rsqrt((s_own + s_other) / model + gap * gap + EPSILON)
    slope = p_own[rows : rows + 1, : 3 * width].astype(F32) - p_other[rows : rows + 1, : 3 * width].astype(F32)
    inv_q, inv_k, inv_l = [], [], []
    factor = LOG2E * HD**-0.5
    stores = []

    def mixture(at):
        cols = slice(at * HD, (at + 1) * HD)
        other = exchanged(p_other[:rows, cols]).astype(F32)
        return inverse * (p_own[:rows, cols].astype(F32) + other + gap * slope[:, cols])

    for head in range(heads):
        cols = slice(head * HD, (head + 1) * HD)
        q_hat, q_inv = row_norm(mixture(head))
        k_hat, k_inv = row_norm(mixture(heads + head))
        v_low = mixture(2 * heads + head).astype(BF16)
        q_low, k_low = q_hat.astype(BF16), k_hat.astype(BF16)
        e = jnp.exp2(dot_nt(q_low, k_low) * factor)
        l_inv = 1.0 / jnp.sum(e, axis=1, keepdims=True)
        e_low = e.astype(BF16)
        e_out[head] = e_low
        stores += start(sems, head, (e_out.at[head], saved[0].at[head]))
        att[:, cols] = (dot(e_low[:group], v_low) * l_inv[:group]).astype(BF16)
        q_out[:, cols] = q_low
        k_out[:, cols] = k_low
        v_out[:, cols] = v_low
        inv_q.append(q_inv)
        inv_k.append(k_inv)
        inv_l.append(l_inv)
    aux[...] = lanes([centre, inverse] + inv_l + inv_q + inv_k, rows)
    stores += start(sems, heads, (q_out, saved[1]), (k_out, saved[2]), (v_out, saved[3]), (aux, saved[4]))
    finish(stores)


def embed_kernel(ids, att, wpt, xp_own, xp_other, out):
    part = dot_nt(att[...], wpt[...]) + xp_own[...] + xp_other[...].astype(F32)
    out[...] = part.astype(BF16).reshape(out.shape)


def sum_kernel(ids, parts, out):
    total = jnp.sum(parts[...].astype(F32), axis=0).astype(BF16)
    for at in range(out.shape[0]):
        out[at] = total


def encoder_back_kernel(ids, g_own, g_other, we, *refs):
    sources = refs[:7]
    w = refs[7]
    right, left, parts_out = refs[8:11]
    wpt, e_in, q_in, k_in, v_in, aux, x_in, held, gmix, out, sems = refs[11:]
    loads = start(sems, 0, *zip(sources[:6], (wpt, e_in, q_in, k_in, v_in, aux)))
    w_loads = start(sems, 6, *[(w.at[at], held.at[at]) for at in range(3)])
    w_loads += start(sems, 9, (sources[6], x_in))
    rows, width = q_in.shape
    heads = width // HD
    half = held.shape[1]
    slab = half // 8
    tok = x_in.shape[2]
    m = ids[1]
    factor = HD**-0.5
    gemb = jnp.concatenate([g_own[...], g_other[...]])
    glayer = dot_nt(gemb, we[...])
    loads[0].wait()
    gatt = dot(gemb, wpt[...]).astype(BF16)
    finish(loads[1:])
    for head in range(heads):
        cols = slice(head * HD, (head + 1) * HD)
        g_head = gatt[:, cols]
        q_low, k_low, v_low = q_in[:, cols], k_in[:, cols], v_in[:, cols]
        l_inv = aux[:, 2 + head : 3 + head]
        q_inv = aux[:, 2 + heads + head : 3 + heads + head]
        k_inv = aux[:, 2 + 2 * heads + head : 3 + 2 * heads + head]
        p = e_in[head].astype(F32) * l_inv
        gp = dot_nt(g_head, v_low)
        delta = jnp.sum(p * gp, axis=1, keepdims=True)
        gs = (p * (gp - delta)).astype(BF16)
        gq = dot(gs, k_low) * factor
        gk = dot_tn(gs, q_low) * factor
        gv = dot_tn(p.astype(BF16), g_head)
        gmix[:, cols] = norm_back(q_low.astype(F32), q_inv, gq).astype(BF16)
        gmix[:, width + head * HD : width + (head + 1) * HD] = norm_back(k_low.astype(F32), k_inv, gk).astype(BF16)
        gmix[:, 2 * width + head * HD : 2 * width + (head + 1) * HD] = gv.astype(BF16)
    finish(w_loads)
    centre, inverse = aux[:, 0:1], aux[:, 1:2]
    total = jnp.zeros((rows, 1), F32)
    total_dot = jnp.zeros((rows, 1), F32)
    for block in range(8):
        cols = slice(block * slab, (block + 1) * slab)
        g = dot_nt(gmix[:, :width], held[0, cols, :])
        g = g + dot_nt(gmix[:, width : 2 * width], held[1, cols, :])
        g = g + dot_nt(gmix[:, 2 * width :], held[2, cols, :])
        normed = (x_in[:, :, :, cols].reshape(rows, slab).astype(F32) - centre) * inverse
        total = total + jnp.sum(g, axis=1, keepdims=True)
        total_dot = total_dot + jnp.sum(g * normed, axis=1, keepdims=True)
        mine = jnp.where(block == m, 1.0, 0.0)
        value = (g * inverse + glayer * mine).astype(BF16).reshape(2, 8, tok, slab)
        out[:, :tok, cols] = value[0]
        out[:, tok:, cols] = value[1]
    sums = lanes((total, total_dot), rows).astype(BF16).reshape(2, 8, tok, 128)
    out[:, :tok, half:] = sums[0]
    out[:, tok:, half:] = sums[1]
    store = start(sems, 10, (out, parts_out))
    right[...] = out[lax.rem(m + 4, 8), :tok]
    left[...] = out[lax.rem(m + 4, 8), tok:]
    finish(store)


def final_kernel(ids, x_own, own_right, own_left, other_here, other_right, other_left, parts, out, own_here, sems):
    s = ids[0]
    tok, model = x_own.shape
    half = model // 2
    load = start(sems, 0, (parts.at[ids[1], pl.ds(0, tok)], own_here))
    normed, inverse = row_norm(x_own[...].astype(F32))
    theirs = other_here[...].astype(F32) + other_right[...].astype(F32) + other_left[...].astype(F32)
    finish(load)
    mine = own_here[...].astype(F32) + own_right[...].astype(F32) + own_left[...].astype(F32)
    total = (mine[:, half : half + 1] + theirs[:, half : half + 1]) / model
    total_dot = (mine[:, half + 1 : half + 2] + theirs[:, half + 1 : half + 2]) / model
    first = jnp.where(s == 0, mine[:, :half], theirs[:, :half])
    second = jnp.where(s == 0, theirs[:, :half], mine[:, :half])
    out[:, :half] = (first - inverse * (total + normed[:, :half] * total_dot)).astype(BF16)
    out[:, half:] = (second - inverse * (total + normed[:, half:] * total_dot)).astype(BF16)


def head_norm_t(values):
    width, n = values.shape
    hat, inverse = row_norm(values.reshape(DHEADS, DHD, n), axis=1)
    return hat.reshape(width, n), inverse


def head_back_t(hat, inverse, gradient):
    width, n = hat.shape
    back = norm_back(
        hat.reshape(DHEADS, DHD, n), inverse, gradient.reshape(DHEADS, DHD, n), axis=1
    )
    return back.reshape(width, n)


def mask_kernel(ids, table_in, mask, w_in, pos_vis, vis_row, hidden, k_t, v, wq_t, wk_t, table, w, sems):
    loads = start(sems, 0, (w_in, w), (table_in, table))
    loads[0].wait()
    wq_t[...] = w[0].T
    wk_t[...] = w[1].T
    loads[1].wait()
    members, pos_dev = table.shape[0], table.shape[1] - 16
    npos, width = members * pos_dev, table.shape[2]
    nvis = vis_row.shape[1]
    pos_all = table[:, :pos_dev, :].reshape(npos, width)
    codes = jnp.sum(table[:, pos_dev:, :].astype(F32), axis=0)
    row = codes[0:1, :nvis] * 32.0 + codes[1:2, :nvis]
    other = jnp.concatenate([row[:, nvis // 2 :], row[:, : nvis // 2]], axis=1)
    vis = jnp.where(ids[0] == 0, row, other).astype(jnp.int32)
    vis_row[...] = vis
    hot = jnp.where(lax.broadcasted_iota(jnp.int32, (npos, nvis), 0) == vis, 1.0, 0.0).astype(BF16)
    pos_vis[...] = dot_tn(hot, pos_all).astype(BF16)
    hidden[...] = 1.0 - dot_nt(jnp.ones((16, nvis), BF16), hot)[0:1, :]
    hat, _ = row_norm(pos_all.astype(F32) + mask[...].astype(F32))
    low = hat.astype(BF16)
    key_hat, _ = head_norm_t(dot_nt(wk_t[...], low))
    k_t[...] = key_hat.astype(BF16)
    v[...] = dot(low, w[2]).astype(BF16)


def decoder_kernel(ids, emb_own, emb_other, mask, vis_row, hidden, *refs):
    wk_t_in, w_in, pos_vis_in, pos_own_in, wq_t_in, km_t_in, vm_in, w_out_in, w_pix_in, target_in = refs[:10]
    pred, g_own, g_other, em_ref, ev_ref = refs[10:15]
    wk_t, w, pos_vis, pos_own, wq_t, km_t, vm, w_out, w_pix, target, sems = refs[15:]
    loads = start(
        sems,
        0,
        (pos_vis_in, pos_vis),
        (wk_t_in, wk_t),
        (w_in.at[2], w.at[2]),
        (pos_own_in, pos_own),
        (wq_t_in, wq_t),
        (km_t_in, km_t),
        (vm_in, vm),
        (w_out_in, w_out),
        (w_pix_in, w_pix),
        (target_in, target),
        (w_in.at[0], w.at[0]),
        (w_in.at[1], w.at[1]),
    )
    npos_dev, width = pos_own.shape
    nvis = pos_vis.shape[0]
    group = nvis // 2
    member = ids[2]
    groups = width // 128
    per = 128 // DHD
    rows = per * npos_dev
    factor = DHD**-0.5
    emb = jnp.concatenate([emb_own[...], emb_other[...]])
    loads[0].wait()
    vis_hat, vis_inv = row_norm(emb.astype(F32) + pos_vis[...].astype(F32))
    vis_low = vis_hat.astype(BF16)
    finish(loads[1:3])
    kv_hat, kv_inv = head_norm_t(dot_nt(wk_t[...], vis_low))
    kv_t = kv_hat.astype(BF16)
    vv = dot(vis_low, w[2]).astype(BF16)
    position = lax.broadcasted_iota(jnp.int32, (npos_dev, nvis), 0) + member * npos_dev
    hot = jnp.where(position == vis_row[...], 1.0, 0.0)
    seen = jnp.sum(hot, axis=1, keepdims=True)
    hot_low = hot.astype(BF16)
    filled = dot(hot_low, emb) + (1.0 - seen) * mask[...].astype(F32)
    finish(loads[3:5])
    stream = filled + pos_own[...].astype(F32)
    own_hat, own_inv = row_norm(stream)
    q_t, q_inv = head_norm_t(dot_nt(wq_t[...], own_hat.astype(BF16)))
    q_low = q_t.T.astype(BF16)
    head_mask = (
        lax.broadcasted_iota(jnp.int32, (rows, 128), 0) // npos_dev
        == lax.broadcasted_iota(jnp.int32, (rows, 128), 1) // DHD
    )

    def spread(values):
        return jnp.where(head_mask, jnp.concatenate([values] * per, axis=0), jnp.zeros((), values.dtype))

    def gather(values):
        return jnp.sum(jnp.where(head_mask, values, 0.0).reshape(per, npos_dev, 128), axis=0)

    finish(loads[5:7])
    attended, inv_l = [], []
    for at in range(groups):
        cols = slice(at * 128, (at + 1) * 128)
        q_wide = spread(q_low[:, cols])
        em = jnp.exp2(dot(q_wide, km_t[cols, :]) * (factor * LOG2E)) * hidden[...]
        ev = jnp.exp2(dot(q_wide, kv_t[cols, :]) * (factor * LOG2E))
        l_inv = 1.0 / (jnp.sum(em, axis=1, keepdims=True) + jnp.sum(ev, axis=1, keepdims=True))
        em_low, ev_low = em.astype(BF16), ev.astype(BF16)
        em_ref[at] = em_low
        ev_ref[at] = ev_low
        attended.append(gather((dot(em_low, vm[:, cols]) + dot(ev_low, vv[:, cols])) * l_inv))
        inv_l.append(l_inv)
    att = jnp.concatenate(attended, axis=1)
    finish(loads[7:])
    second = stream + dot(att.astype(BF16), w_out[...])
    final_hat, final_inv = row_norm(second)
    full = dot(final_hat.astype(BF16), w_pix[...])
    pred[...] = full.astype(BF16)
    error = jnp.where(seen > 0, 0.0, full - target[...].astype(F32)).astype(BF16)
    g_second = norm_back(final_hat, final_inv, dot_nt(error, w_pix[...]))
    g_att = dot_nt(g_second.astype(BF16), w_out[...]).astype(BF16)
    product = g_att.astype(F32) * att
    gq, gk_t, gv = [], [], []
    for at in range(groups):
        cols = slice(at * 128, (at + 1) * 128)
        q_wide = spread(q_low[:, cols])
        g_wide = spread(g_att[:, cols])
        delta = jnp.sum(spread(product[:, cols]), axis=1, keepdims=True)
        l_inv = inv_l[at]
        pv = ev_ref[at].astype(F32) * l_inv
        gs_v = (pv * (dot_nt(g_wide, vv[:, cols]) - delta)).astype(BF16)
        pm = em_ref[at].astype(F32) * l_inv
        gs_m = (pm * (dot_nt(g_wide, vm[:, cols]) - delta)).astype(BF16)
        gq.append(gather(dot_nt(gs_m, km_t[cols, :]) + dot_nt(gs_v, kv_t[cols, :])) * factor)
        gk_t.append(dot_tn(q_wide, gs_v) * factor)
        gv.append(dot_tn(pv.astype(BF16), g_wide).astype(BF16))
    gq_back = head_back_t(q_t, q_inv, jnp.concatenate(gq, axis=1).T).T.astype(BF16)
    g_stream_own = g_second + norm_back(own_hat, own_inv, dot_nt(gq_back, w[0]))
    gk_back = head_back_t(kv_hat, kv_inv, jnp.concatenate(gk_t, axis=0)).T.astype(BF16)
    from_keys = dot_nt(gk_back, w[1]) + dot_nt(jnp.concatenate(gv, axis=1), w[2])
    part = norm_back(vis_hat, vis_inv, from_keys) + dot_tn(hot_low, g_stream_own.astype(BF16))
    g_own[...] = part[:group]
    g_other[...] = part[group:].astype(BF16)


def shards(
    patches,
    vis_index,
    input_weight,
    output_weight,
    embed_weight,
    mask_token,
    position_table,
    decoder_input,
    decoder_output,
    pixel_weight,
    target,
):
    section = lax.axis_index("section")
    column = lax.axis_index("mp")
    member = lax.axis_index(("section", "mp"))
    copies = lax.axis_size("dp")
    ids = jnp.stack([section, column, member]).astype(jnp.int32)
    x_own = patches[0]
    tok, model = x_own.shape
    half = model // 2
    slab, dec_width = embed_weight.shape
    width = output_weight.shape[0]
    heads = width // HD
    group = 8 * tok
    nvis = 2 * group
    pos_dev = position_table.shape[0]
    npos = 16 * pos_dev

    def swap(value):
        return lax.ppermute(value, "section", [(0, 1), (1, 0)])

    def shift(value, by):
        return lax.ppermute(value, "mp", [(i, (i + by) % 8) for i in range(8)])

    def exchange(value, axis):
        return lax.all_to_all(value, axis, 0, 0, tiled=True)

    mine = lax.dynamic_slice_in_dim(x_own, section * half, half, 1)
    theirs = swap(lax.dynamic_slice_in_dim(x_own, (1 - section) * half, half, 1))
    dec_cols = dec_width // copies
    we_t = lax.dynamic_slice_in_dim(embed_weight, lax.axis_index("dp") * dec_cols, dec_cols, 1).T
    we_t = we_t.reshape(dec_cols // 32, 32, slab).transpose(1, 0, 2).reshape(32, -1)
    we_right, we_left = shift(we_t, 1), shift(we_t, -1)
    chunk = jnp.concatenate([mine, theirs])
    right = jnp.concatenate([chunk, we_right], axis=1)
    left = jnp.concatenate([chunk, we_left], axis=1)
    chunks, columns = {0: right}, {0: we_t, -1: we_right, 1: we_left}
    for step in range(1, 5):
        right = shift(right, 1)
        if step < 4:
            left = shift(left, -1)
            right, left = lax.optimization_barrier((right, left))
            chunks[step] = left
            columns[step + 1] = left
        chunks[-step] = right
        columns[-step - 1] = right

    row = jnp.zeros((nvis,), jnp.int32)
    row = lax.dynamic_update_slice_in_dim(row, vis_index[0], member * tok, 0)
    codes = jnp.pad(jnp.stack([row // 32, row % 32]), ((0, 14), (0, dec_width - nvis)))
    table = jnp.concatenate([position_table, codes.astype(BF16)])
    table, _ = lax.optimization_barrier((table, chunks[-3]))
    table = lax.all_gather(table, ("section", "mp"), axis=0, tiled=False)

    w_in = input_weight.transpose(1, 0, 2)
    held = sds(w_in.shape, BF16)
    ordered = [chunks[offset] for offset in OFFSETS]
    (wp_low,) = call(
        fold_kernel,
        [sds((dec_cols, width), BF16)],
        ids,
        *[columns[offset] for offset in OFFSETS],
        output_weight,
        scratch=[sds((dec_cols, half), BF16), sds(output_weight.shape, BF16)],
        far=tuple(range(1, 10)),
        copies=1 + 8 * (dec_cols // 32),
    )
    x_all, p_own, xp_own, xp_send, wp_parts = call(
        project_kernel,
        [
            sds((2, 8, tok, half), BF16),
            sds((nvis + 16, 3 * width + 128), BF16),
            sds((group, dec_width), F32),
            sds((group, dec_width), BF16),
            sds((copies, dec_cols, width), BF16),
        ],
        ids,
        *ordered,
        w_in,
        embed_weight,
        wp_low,
        swap(wp_low),
        scratch=[
            sds((2, 8, tok, half), BF16),
            sds((nvis + 16, half), BF16),
            held,
            sds((group, dec_width), F32),
            sds((8, 2 * tok, half), BF16),
            sds((nvis + 16, 3 * width + 128), BF16),
        ],
        far=tuple(range(1, 10)),
        far_out=(0, 1, 2),
        copies=17,
    )
    p_other = swap(p_own)
    xp_other = swap(xp_send)
    wp_parts, _ = lax.optimization_barrier((wp_parts, xp_other))
    wpt = exchange(wp_parts, "dp").reshape(dec_width, width)
    saved = [
        sds((heads, nvis, nvis), BF16),
        sds((nvis, width), BF16),
        sds((nvis, width), BF16),
        sds((nvis, width), BF16),
        sds((nvis, 128), F32),
    ]
    att, e_enc, q_enc, k_enc, v_enc, aux = call(
        attend_kernel,
        [sds((group, width), BF16)] + saved,
        ids,
        p_own,
        p_other,
        scratch=saved,
        far_out=(1, 2, 3, 4, 5),
        copies=heads + 4,
    )
    (embed_part,) = call(
        embed_kernel, [sds((8, tok, dec_width), BF16)], ids, att, wpt, xp_own, xp_other
    )

    w_dec = decoder_input.transpose(1, 0, 2)
    mask_row = mask_token.reshape(1, dec_width)
    (embed_sum,) = call(sum_kernel, [sds((8, tok, dec_width), BF16)], ids, exchange(embed_part, "mp"), limit=16)
    table, _ = lax.optimization_barrier((table, embed_sum))
    pos_vis, vis_row, hidden, km_t, vm, wq_t, wk_t = call(
        mask_kernel,
        [
            sds((nvis, dec_width), BF16),
            sds((1, nvis), jnp.int32),
            sds((1, npos), F32),
            sds((dec_width, npos), BF16),
            sds((npos, dec_width), BF16),
            sds((dec_width, dec_width), BF16),
            sds((dec_width, dec_width), BF16),
        ],
        ids,
        table,
        mask_row,
        w_dec,
        scratch=[sds(table.shape, BF16), sds(w_dec.shape, BF16)],
        far=(1, 3),
        copies=2,
    )
    emb_own = exchange(embed_sum, "mp").reshape(group, dec_width)
    emb_own, _ = lax.optimization_barrier((emb_own, hidden))
    emb_other = swap(emb_own)

    groups = dec_width // 128
    rows = (128 // DHD) * pos_dev
    prediction, g_own, g_send = call(
        decoder_kernel,
        [
            sds((pos_dev, target.shape[2]), BF16),
            sds((group, dec_width), F32),
            sds((group, dec_width), BF16),
        ],
        ids,
        emb_own,
        emb_other,
        mask_row,
        vis_row,
        hidden,
        wk_t,
        w_dec,
        pos_vis,
        position_table,
        wq_t,
        km_t,
        vm,
        decoder_output,
        pixel_weight,
        target[0],
        scratch=[sds((groups, rows, npos), BF16), sds((groups, rows, nvis), BF16)]
        + [sds(wk_t.shape, BF16), sds(w_dec.shape, BF16), sds(pos_vis.shape, BF16)]
        + [sds(position_table.shape, BF16), sds(wq_t.shape, BF16), sds(km_t.shape, BF16), sds(vm.shape, BF16)]
        + [sds(decoder_output.shape, BF16), sds(pixel_weight.shape, BF16), sds(target.shape[1:], BF16)],
        far=tuple(range(6, 16)),
        copies=12,
    )
    g_part = (g_own + swap(g_send).astype(F32)).astype(BF16).reshape(8, tok, dec_width)
    (g_sum,) = call(sum_kernel, [sds((8, tok, dec_width), BF16)], ids, exchange(g_part, "mp"), limit=16)
    ge_own = exchange(g_sum, "mp").reshape(group, dec_width)
    ge_other = swap(ge_own)

    right, left, parts = call(
        encoder_back_kernel,
        [
            sds((tok, half + 128), BF16),
            sds((tok, half + 128), BF16),
            sds((8, 2 * tok, half + 128), BF16),
        ],
        ids,
        ge_own,
        ge_other,
        embed_weight,
        wpt,
        e_enc,
        q_enc,
        k_enc,
        v_enc,
        aux,
        x_all,
        w_in,
        scratch=[sds((dec_width, width), BF16)]
        + saved
        + [sds(x_all.shape, BF16), held, sds((nvis, 3 * width), BF16), sds((8, 2 * tok, half + 128), BF16)],
        far=tuple(range(4, 12)),
        far_out=(2,),
        copies=11,
    )

    def part(offset):
        return lax.dynamic_index_in_dim(parts, (column + offset) % 8, 0, False).astype(F32)

    def cross(value, by):
        pairs = [(s * 8 + i, (1 - s) * 8 + (i + by) % 8) for s in range(2) for i in range(8)]
        return lax.ppermute(value, ("section", "mp"), pairs)

    other_here = swap(part(0)[tok:].astype(BF16))
    right, left = lax.optimization_barrier((shift(right, 1), shift(left, -1)))
    ahead, behind = part(3), part(-3)
    right = jnp.concatenate([right.astype(F32) + ahead[:tok], ahead[tok:]]).astype(BF16)
    left = jnp.concatenate([behind[:tok], left.astype(F32) + behind[tok:]]).astype(BF16)
    for offset in (2, 1):
        right, left = lax.optimization_barrier((shift(right, 1), shift(left, -1)))
        right = (right.astype(F32) + part(offset)).astype(BF16)
        left = (left.astype(F32) + part(-offset)).astype(BF16)
    (patch_grad,) = call(
        final_kernel,
        [sds((tok, model), BF16)],
        ids,
        x_own,
        shift(right[:tok], 1),
        shift(left[:tok], -1),
        other_here,
        cross(right[tok:], 1),
        cross(left[tok:], -1),
        parts,
        scratch=[sds((tok, half + 128), BF16)],
        far=(7,),
        copies=1,
    )
    return (prediction[None], patch_grad[None])


def solution(mesh):
    group = ("section", "mp")
    in_specs = (
        P("dp", group, None),
        P("dp", group),
        P("section", None, "mp"),
        P("mp", "section"),
        P(group, None),
        P(),
        P(group, None),
        P(),
        P(),
        P(),
        P("dp", group, None),
    )
    out_specs = (P("dp", group, None), P("dp", group, None))
    return jax.shard_map(shards, mesh=mesh, in_specs=in_specs, out_specs=out_specs, check_vma=False)
```

```python
import math

import jax
import jax.numpy as jnp
from jax import lax
from jax.experimental import pallas as pl
from jax.experimental.pallas import tpu as pltpu
from jax.sharding import PartitionSpec as P

HD = 128
DHEADS = 16
DHD = 32
EPSILON = 1e-06
LOG2E = math.log2(math.e)
F32 = jnp.float32
BF16 = jnp.bfloat16
OFFSETS = (0, -1, 1, -2, 2, -3, 3, -4)


def dot(a, b):
    return lax.dot_general(a, b, (((1,), (0,)), ((), ())), preferred_element_type=F32)


def dot_nt(a, b):
    return lax.dot_general(a, b, (((1,), (1,)), ((), ())), preferred_element_type=F32)


def dot_tn(a, b):
    return lax.dot_general(a, b, (((0,), (0,)), ((), ())), preferred_element_type=F32)


def row_norm(values, axis=-1):
    centre = jnp.mean(values, axis=axis, keepdims=True)
    centered = values - centre
    inverse = lax.rsqrt(jnp.mean(centered * centered, axis=axis, keepdims=True) + EPSILON)
    return centered * inverse, inverse


def norm_back(normed, inverse, gradient, axis=-1):
    mean_grad = jnp.mean(gradient, axis=axis, keepdims=True)
    mean_dot = jnp.mean(gradient * normed, axis=axis, keepdims=True)
    return inverse * (gradient - mean_grad - normed * mean_dot)


def lanes(columns, rows):
    lane = lax.broadcasted_iota(jnp.int32, (rows, 128), 1)
    out = jnp.zeros((rows, 128), F32)
    for at, column in enumerate(columns):
        out = jnp.where(lane == at, column, out)
    return out


def call(kernel, outs, *args, scratch=(), far=(), far_out=(), copies=0, limit=58):
    specs = [pl.BlockSpec(memory_space=pltpu.SMEM)]
    for at in range(1, len(args)):
        specs.append(pl.BlockSpec(memory_space=pl.ANY if at in far else pltpu.VMEM))
    out_specs = [
        pl.BlockSpec(memory_space=pl.ANY if at in far_out else pltpu.VMEM) for at in range(len(outs))
    ]
    scratch = [pltpu.VMEM(shape.shape, shape.dtype) for shape in scratch]
    if copies:
        scratch.append(pltpu.SemaphoreType.DMA((copies,)))
    return pl.pallas_call(
        kernel,
        out_shape=tuple(outs),
        in_specs=specs,
        out_specs=tuple(out_specs),
        scratch_shapes=scratch,
        compiler_params=pltpu.CompilerParams(vmem_limit_bytes=limit * 2**20),
    )(*args)


def start(sems, first, *pairs):
    copies = [
        pltpu.make_async_copy(source, target, sems.at[first + at]) for at, (source, target) in enumerate(pairs)
    ]
    for copy in copies:
        copy.start()
    return copies


def finish(copies):
    for copy in copies:
        copy.wait()


def sds(shape, dtype):
    return jax.ShapeDtypeStruct(shape, dtype)


def weight_copies(w, held, pieces):
    _, rows, width = w.shape
    size = rows // pieces
    return [
        (w.at[at, pl.ds(piece * size, size)], held.at[pl.ds(piece * size, size), pl.ds(at * width, width)])
        for piece in range(pieces)
        for at in range(3)
    ]


def split3(values):
    first = values.astype(BF16).astype(F32)
    second = (values - first).astype(BF16).astype(F32)
    return [first, second, values - first - second]


def centre_rows(value):
    wide = value.astype(F32)
    centre = jnp.mean(wide, axis=1, keepdims=True)
    centered = wide - centre
    spread = jnp.sum(centered * centered, axis=1, keepdims=True)
    return centered.astype(BF16), lanes(split3(centre) + split3(spread), value.shape[0]).astype(BF16)


def place_rows(rows, at, target, cols=slice(None)):
    tok = rows.shape[0] // 2
    row = pl.multiple_of(at * tok, tok)
    target[pl.ds(row, tok), cols] = rows[:tok]
    target[pl.ds(row + 8 * tok, tok), cols] = rows[tok:]


def project_kernel(ids, we, *refs):
    chunks, columns, wo_in, w = refs[:7], refs[7:15], refs[15], refs[16]
    p_out, xp_out, wp_out = refs[17:20]
    held_chunks, xc, held, wt, wo, sems = refs[20:]
    half, width3 = held.shape
    slab = half // 8
    rows2 = held_chunks.shape[1]
    m = ids[1]
    pieces = wt.shape[0] // 32
    arrivals = start(
        sems, 0, *[(chunk.at[:, pl.ds(0, half)], held_chunks.at[at]) for at, chunk in enumerate(chunks)]
    )
    loads = []
    for index, (source, offset) in enumerate(zip(columns, OFFSETS)):
        column = pl.multiple_of(lax.rem(m + offset + 8, 8) * slab, 128)
        base = source.shape[1] - pieces * slab
        for piece in range(pieces):
            target = wt.at[pl.ds(piece * 32, 32), pl.ds(column, slab)]
            source_part = source.at[:, pl.ds(base + piece * slab, slab)]
            loads += start(sems, 14 + index * pieces + piece, (source_part, target))
    loads += start(sems, 7, (wo_in, wo))
    w_loads = start(sems, 8, *weight_copies(w, held, 2))
    own_column = pl.multiple_of(m * slab, 128)
    stats = []
    for index, offset in enumerate(OFFSETS[:7]):
        arrivals[index].wait()
        low, moments = centre_rows(held_chunks[index])
        xc[index * rows2 : (index + 1) * rows2, :] = low
        stats.append(moments)
    xc[7 * rows2 :, :] = jnp.ones((16, half), BF16)
    raw = held_chunks[:, :, pl.ds(own_column, slab)].reshape(7 * rows2, slab)
    xp = dot(raw, we[...])
    finish(loads)
    wp_out[...] = dot_nt(wt[...], wo[...]).astype(BF16)
    finish(w_loads[:3])
    product = dot(xc[:, : half // 2], held[: half // 2, :])
    finish(w_loads[3:])
    product = (product + dot(xc[:, half // 2 :], held[half // 2 :, :])).astype(BF16)
    for index, offset in enumerate(OFFSETS[:7]):
        at = lax.rem(m + offset + 8, 8)
        part = slice(index * rows2, (index + 1) * rows2)
        place_rows(product[part], at, p_out, slice(0, width3))
        place_rows(stats[index], at, p_out, slice(width3, width3 + 128))
        place_rows(xp[part], at, xp_out)
    last = lax.rem(m + OFFSETS[7] + 8, 8)
    place_rows(jnp.zeros((rows2, width3 + 128), BF16), last, p_out)
    place_rows(jnp.zeros((rows2, xp.shape[1]), F32), last, xp_out)
    p_out[8 * rows2 :, :width3] = product[7 * rows2 :]
    p_out[8 * rows2 :, width3:] = jnp.zeros((16, 128), BF16)


def project_last_kernel(ids, we, p_in, xp_in, chunk, w, p_out, xp_own, xp_send, held_chunk, held, sems):
    half, width3 = held.shape
    slab = half // 8
    rows2 = held_chunk.shape[0]
    m = ids[1]
    arrival = start(sems, 0, (chunk.at[:, pl.ds(0, half)], held_chunk))
    w_loads = start(sems, 1, *weight_copies(w, held, 4))
    p_out[...] = p_in[...]
    finish(arrival)
    at = lax.rem(m + OFFSETS[7] + 8, 8)
    low, moments = centre_rows(held_chunk[...])
    xp = dot(held_chunk[:, pl.ds(pl.multiple_of(m * slab, 128), slab)], we[...])
    group = 4 * rows2
    tok = rows2 // 2
    xp_own[...] = xp_in[:group, :]
    xp_send[...] = xp_in[group:, :].astype(BF16)
    row = pl.multiple_of(at * tok, tok)
    xp_own[pl.ds(row, tok), :] = xp[:tok]
    xp_send[pl.ds(row, tok), :] = xp[tok:].astype(BF16)
    place_rows(moments, at, p_out, slice(width3, width3 + 128))
    quarter = half // 4
    product = jnp.zeros((rows2, width3), F32)
    for piece in range(4):
        finish(w_loads[piece * 3 : piece * 3 + 3])
        part = slice(piece * quarter, (piece + 1) * quarter)
        product = product + dot(low[:, part], held[part, :])
    place_rows(product.astype(BF16), at, p_out, slice(0, width3))


def spread_kernel(ids, own, other, out):
    total = (own[...].astype(F32) + other[...].astype(F32)).astype(BF16)
    for at in range(out.shape[0]):
        out[at] = total


def attend_kernel(ids, p_own, p_other, att, *refs):
    saved = refs[:5]
    e_out, q_out, k_out, v_out, aux = refs[5:10]
    sems = refs[10]
    rows = p_own.shape[0] - 16
    group = rows // 2
    width = (p_own.shape[1] - 128) // 3
    heads = width // HD
    model = 2 * 8 * width

    def moments(p):
        stats = p[:rows, 3 * width :].astype(F32)
        parts = [stats[:, at : at + 1] for at in range(6)]
        return parts[0] + parts[1] + parts[2], parts[3] + parts[4] + parts[5]

    def exchanged(values):
        return jnp.concatenate([values[group:], values[:group]])

    m_own, s_own = moments(p_own)
    m_other, s_other = [exchanged(value) for value in moments(p_other)]
    gap = (m_own - m_other) * 0.5
    centre = (m_own + m_other) * 0.5
    inverse = lax.rsqrt((s_own + s_other) / model + gap * gap + EPSILON)
    slope = p_own[rows : rows + 1, : 3 * width].astype(F32) - p_other[rows : rows + 1, : 3 * width].astype(F32)
    inv_q, inv_k, inv_l = [], [], []
    factor = LOG2E * HD**-0.5
    stores = []

    def mixture(at):
        cols = slice(at * HD, (at + 1) * HD)
        other = exchanged(p_other[:rows, cols]).astype(F32)
        return inverse * (p_own[:rows, cols].astype(F32) + other + gap * slope[:, cols])

    for head in range(heads):
        cols = slice(head * HD, (head + 1) * HD)
        q_hat, q_inv = row_norm(mixture(head))
        k_hat, k_inv = row_norm(mixture(heads + head))
        v_low = mixture(2 * heads + head).astype(BF16)
        q_low, k_low = q_hat.astype(BF16), k_hat.astype(BF16)
        e = jnp.exp2(dot_nt(q_low, k_low) * factor)
        l_inv = 1.0 / jnp.sum(e, axis=1, keepdims=True)
        e_low = e.astype(BF16)
        e_out[head] = e_low
        stores += start(sems, head, (e_out.at[head], saved[0].at[head]))
        att[:, cols] = (dot(e_low[:group], v_low) * l_inv[:group]).astype(BF16)
        q_out[:, cols] = q_low
        k_out[:, cols] = k_low
        v_out[:, cols] = v_low
        inv_q.append(q_inv)
        inv_k.append(k_inv)
        inv_l.append(l_inv)
    aux[...] = lanes([centre, inverse] + inv_l + inv_q + inv_k, rows)
    stores += start(sems, heads, (q_out, saved[1]), (k_out, saved[2]), (v_out, saved[3]), (aux, saved[4]))
    finish(stores)


def embed_kernel(ids, att, wpt, xp_own, xp_other, out):
    part = dot_nt(att[...], wpt[...]) + xp_own[...] + xp_other[...].astype(F32)
    out[...] = part.astype(BF16).reshape(out.shape)


def sum_kernel(ids, parts, out):
    total = jnp.sum(parts[...].astype(F32), axis=0).astype(BF16)
    for at in range(out.shape[0]):
        out[at] = total


def encoder_back_kernel(ids, g_own, g_other, we, *refs):
    sources, w, chunks = refs[:6], refs[6], refs[7:15]
    right, left, parts_out = refs[15:18]
    wpt, e_in, q_in, k_in, v_in, aux, x_in, held, gmix, out, sems = refs[18:]
    rows, width = q_in.shape
    heads = width // HD
    half = held.shape[0]
    slab = half // 8
    tok = x_in.shape[2]
    m = ids[1]
    loads = start(sems, 0, *zip(sources, (wpt, e_in, q_in, k_in, v_in, aux)))
    w_loads = start(sems, 6, *weight_copies(w, held, 1))
    for index, offset in enumerate(OFFSETS):
        at = lax.rem(m + offset + 8, 8)
        for rel in range(2):
            rows_of = chunks[index].at[pl.ds(rel * tok, tok), pl.ds(0, half)]
            w_loads += start(sems, 10 + 2 * index + rel, (rows_of, x_in.at[rel, at]))
    factor = HD**-0.5
    gemb = jnp.concatenate([g_own[...], g_other[...]])
    glayer = dot_nt(gemb, we[...])
    loads[0].wait()
    gatt = dot(gemb, wpt[...]).astype(BF16)
    finish(loads[1:])
    for head in range(heads):
        cols = slice(head * HD, (head + 1) * HD)
        g_head = gatt[:, cols]
        q_low, k_low, v_low = q_in[:, cols], k_in[:, cols], v_in[:, cols]
        l_inv = aux[:, 2 + head : 3 + head]
        q_inv = aux[:, 2 + heads + head : 3 + heads + head]
        k_inv = aux[:, 2 + 2 * heads + head : 3 + 2 * heads + head]
        p = e_in[head].astype(F32) * l_inv
        gp = dot_nt(g_head, v_low)
        delta = jnp.sum(p * gp, axis=1, keepdims=True)
        gs = (p * (gp - delta)).astype(BF16)
        gq = dot(gs, k_low) * factor
        gk = dot_tn(gs, q_low) * factor
        gv = dot_tn(p.astype(BF16), g_head)
        gmix[:, cols] = norm_back(q_low.astype(F32), q_inv, gq).astype(BF16)
        gmix[:, width + head * HD : width + (head + 1) * HD] = norm_back(k_low.astype(F32), k_inv, gk).astype(BF16)
        gmix[:, 2 * width + head * HD : 2 * width + (head + 1) * HD] = gv.astype(BF16)
    finish(w_loads)
    centre, inverse = aux[:, 0:1], aux[:, 1:2]
    total = jnp.zeros((rows, 1), F32)
    total_dot = jnp.zeros((rows, 1), F32)
    for block in range(4):
        cols = slice(2 * block * slab, 2 * (block + 1) * slab)
        g = dot_nt(gmix[...], held[cols, :])
        normed = (x_in[:, :, :, cols].reshape(rows, 2 * slab).astype(F32) - centre) * inverse
        total = total + jnp.sum(g, axis=1, keepdims=True)
        total_dot = total_dot + jnp.sum(g * normed, axis=1, keepdims=True)
        mine = [glayer * jnp.where(2 * block + at == m, 1.0, 0.0) for at in range(2)]
        value = (g * inverse + jnp.concatenate(mine, axis=1)).astype(BF16).reshape(2, 8, tok, 2 * slab)
        out[:, :tok, cols] = value[0]
        out[:, tok:, cols] = value[1]
    sums = lanes((total, total_dot), rows).astype(BF16).reshape(2, 8, tok, 128)
    out[:, :tok, half:] = sums[0]
    out[:, tok:, half:] = sums[1]
    store = start(sems, 9, (out, parts_out))
    right[...] = out[lax.rem(m + 4, 8), :tok]
    left[...] = out[lax.rem(m + 4, 8), tok:]
    finish(store)


def final_kernel(ids, x_own, both, other, out):
    s = ids[0]
    tok, model = x_own.shape
    half = model // 2
    normed, inverse = row_norm(x_own[...].astype(F32))
    mine, theirs = both[:tok, :], other[...].astype(F32)
    total = (mine[:, half : half + 1] + theirs[:, half : half + 1]) / model
    total_dot = (mine[:, half + 1 : half + 2] + theirs[:, half + 1 : half + 2]) / model
    first = jnp.where(s == 0, mine[:, :half], theirs[:, :half])
    second = jnp.where(s == 0, theirs[:, :half], mine[:, :half])
    out[:, :half] = (first - inverse * (total + normed[:, :half] * total_dot)).astype(BF16)
    out[:, half:] = (second - inverse * (total + normed[:, half:] * total_dot)).astype(BF16)


def head_norm_t(values):
    width, n = values.shape
    hat, inverse = row_norm(values.reshape(DHEADS, DHD, n), axis=1)
    return hat.reshape(width, n), inverse


def head_back_t(hat, inverse, gradient):
    width, n = hat.shape
    back = norm_back(
        hat.reshape(DHEADS, DHD, n), inverse, gradient.reshape(DHEADS, DHD, n), axis=1
    )
    return back.reshape(width, n)


def mask_kernel(ids, table_in, mask, w_in, pos_vis, vis_row, hidden, k_t, v, wq_t, wk_t, table, w, sems):
    loads = start(sems, 0, (w_in, w), (table_in, table))
    loads[0].wait()
    wq_t[...] = w[0].T
    wk_t[...] = w[1].T
    loads[1].wait()
    members, pos_dev = table.shape[0], table.shape[1] - 16
    npos, width = members * pos_dev, table.shape[2]
    nvis = vis_row.shape[1]
    pos_all = table[:, :pos_dev, :].reshape(npos, width)
    codes = jnp.sum(table[:, pos_dev:, :].astype(F32), axis=0)
    row = codes[0:1, :nvis] * 32.0 + codes[1:2, :nvis]
    other = jnp.concatenate([row[:, nvis // 2 :], row[:, : nvis // 2]], axis=1)
    vis = jnp.where(ids[0] == 0, row, other).astype(jnp.int32)
    vis_row[...] = vis
    hot = jnp.where(lax.broadcasted_iota(jnp.int32, (npos, nvis), 0) == vis, 1.0, 0.0).astype(BF16)
    pos_vis[...] = dot_tn(hot, pos_all).astype(BF16)
    hidden[...] = 1.0 - dot_nt(jnp.ones((16, nvis), BF16), hot)[0:1, :]
    hat, _ = row_norm(pos_all.astype(F32) + mask[...].astype(F32))
    low = hat.astype(BF16)
    key_hat, _ = head_norm_t(dot_nt(wk_t[...], low))
    k_t[...] = key_hat.astype(BF16)
    v[...] = dot(low, w[2]).astype(BF16)


def decoder_kernel(ids, emb_own, emb_other, mask, vis_row, hidden, *refs):
    wk_t_in, w_in, pos_vis_in, pos_own_in, wq_t_in, km_t_in, vm_in, w_out_in, w_pix_in, target_in = refs[:10]
    pred, g_own, g_other, em_ref, ev_ref = refs[10:15]
    wk_t, w, pos_vis, pos_own, wq_t, km_t, vm, w_out, w_pix, target, sems = refs[15:]
    loads = start(
        sems,
        0,
        (pos_vis_in, pos_vis),
        (wk_t_in, wk_t),
        (w_in.at[2], w.at[2]),
        (pos_own_in, pos_own),
        (wq_t_in, wq_t),
        (km_t_in, km_t),
        (vm_in, vm),
        (w_out_in, w_out),
        (w_pix_in, w_pix),
        (target_in, target),
        (w_in.at[0], w.at[0]),
        (w_in.at[1], w.at[1]),
    )
    npos_dev, width = pos_own.shape
    nvis = pos_vis.shape[0]
    group = nvis // 2
    member = ids[2]
    groups = width // 128
    per = 128 // DHD
    rows = per * npos_dev
    factor = DHD**-0.5
    emb = jnp.concatenate([emb_own[...], emb_other[...]])
    loads[0].wait()
    vis_hat, vis_inv = row_norm(emb.astype(F32) + pos_vis[...].astype(F32))
    vis_low = vis_hat.astype(BF16)
    finish(loads[1:3])
    kv_hat, kv_inv = head_norm_t(dot_nt(wk_t[...], vis_low))
    kv_t = kv_hat.astype(BF16)
    vv = dot(vis_low, w[2]).astype(BF16)
    position = lax.broadcasted_iota(jnp.int32, (npos_dev, nvis), 0) + member * npos_dev
    hot = jnp.where(position == vis_row[...], 1.0, 0.0)
    seen = jnp.sum(hot, axis=1, keepdims=True)
    hot_low = hot.astype(BF16)
    filled = dot(hot_low, emb) + (1.0 - seen) * mask[...].astype(F32)
    finish(loads[3:5])
    stream = filled + pos_own[...].astype(F32)
    own_hat, own_inv = row_norm(stream)
    q_t, q_inv = head_norm_t(dot_nt(wq_t[...], own_hat.astype(BF16)))
    q_low = q_t.T.astype(BF16)
    head_mask = (
        lax.broadcasted_iota(jnp.int32, (rows, 128), 0) // npos_dev
        == lax.broadcasted_iota(jnp.int32, (rows, 128), 1) // DHD
    )

    def spread(values):
        return jnp.where(head_mask, jnp.concatenate([values] * per, axis=0), jnp.zeros((), values.dtype))

    def gather(values):
        return jnp.sum(jnp.where(head_mask, values, 0.0).reshape(per, npos_dev, 128), axis=0)

    finish(loads[5:7])
    attended, inv_l = [], []
    for at in range(groups):
        cols = slice(at * 128, (at + 1) * 128)
        q_wide = spread(q_low[:, cols])
        em = jnp.exp2(dot(q_wide, km_t[cols, :]) * (factor * LOG2E)) * hidden[...]
        ev = jnp.exp2(dot(q_wide, kv_t[cols, :]) * (factor * LOG2E))
        l_inv = 1.0 / (jnp.sum(em, axis=1, keepdims=True) + jnp.sum(ev, axis=1, keepdims=True))
        em_low, ev_low = em.astype(BF16), ev.astype(BF16)
        em_ref[at] = em_low
        ev_ref[at] = ev_low
        attended.append(gather((dot(em_low, vm[:, cols]) + dot(ev_low, vv[:, cols])) * l_inv))
        inv_l.append(l_inv)
    att = jnp.concatenate(attended, axis=1)
    finish(loads[7:])
    second = stream + dot(att.astype(BF16), w_out[...])
    final_hat, final_inv = row_norm(second)
    full = dot(final_hat.astype(BF16), w_pix[...])
    pred[...] = full.astype(BF16)
    error = jnp.where(seen > 0, 0.0, full - target[...].astype(F32)).astype(BF16)
    g_second = norm_back(final_hat, final_inv, dot_nt(error, w_pix[...]))
    g_att = dot_nt(g_second.astype(BF16), w_out[...]).astype(BF16)
    product = g_att.astype(F32) * att
    gq, gk_t, gv = [], [], []
    for at in range(groups):
        cols = slice(at * 128, (at + 1) * 128)
        q_wide = spread(q_low[:, cols])
        g_wide = spread(g_att[:, cols])
        delta = jnp.sum(spread(product[:, cols]), axis=1, keepdims=True)
        l_inv = inv_l[at]
        pv = ev_ref[at].astype(F32) * l_inv
        gs_v = (pv * (dot_nt(g_wide, vv[:, cols]) - delta)).astype(BF16)
        pm = em_ref[at].astype(F32) * l_inv
        gs_m = (pm * (dot_nt(g_wide, vm[:, cols]) - delta)).astype(BF16)
        gq.append(gather(dot_nt(gs_m, km_t[cols, :]) + dot_nt(gs_v, kv_t[cols, :])) * factor)
        gk_t.append(dot_tn(q_wide, gs_v) * factor)
        gv.append(dot_tn(pv.astype(BF16), g_wide).astype(BF16))
    gq_back = head_back_t(q_t, q_inv, jnp.concatenate(gq, axis=1).T).T.astype(BF16)
    g_stream_own = g_second + norm_back(own_hat, own_inv, dot_nt(gq_back, w[0]))
    gk_back = head_back_t(kv_hat, kv_inv, jnp.concatenate(gk_t, axis=0)).T.astype(BF16)
    from_keys = dot_nt(gk_back, w[1]) + dot_nt(jnp.concatenate(gv, axis=1), w[2])
    part = norm_back(vis_hat, vis_inv, from_keys) + dot_tn(hot_low, g_stream_own.astype(BF16))
    g_own[...] = part[:group]
    g_other[...] = part[group:].astype(BF16)


def shards(
    patches,
    vis_index,
    input_weight,
    output_weight,
    embed_weight,
    mask_token,
    position_table,
    decoder_input,
    decoder_output,
    pixel_weight,
    target,
):
    section = lax.axis_index("section")
    column = lax.axis_index("mp")
    member = lax.axis_index(("section", "mp"))
    copies = lax.axis_size("dp")
    ids = jnp.stack([section, column, member]).astype(jnp.int32)
    x_own = patches[0]
    tok, model = x_own.shape
    half = model // 2
    slab, dec_width = embed_weight.shape
    width = output_weight.shape[0]
    heads = width // HD
    group = 8 * tok
    nvis = 2 * group
    pos_dev = position_table.shape[0]
    npos = 16 * pos_dev

    def swap(value):
        return lax.ppermute(value, "section", [(0, 1), (1, 0)])

    def shift(value, by):
        return lax.ppermute(value, "mp", [(i, (i + by) % 8) for i in range(8)])

    def exchange(value, axis):
        return lax.all_to_all(value, axis, 0, 0, tiled=True)

    mine = lax.dynamic_slice_in_dim(x_own, section * half, half, 1)
    theirs = swap(lax.dynamic_slice_in_dim(x_own, (1 - section) * half, half, 1))
    dec_cols = dec_width // copies
    we_t = lax.dynamic_slice_in_dim(embed_weight, lax.axis_index("dp") * dec_cols, dec_cols, 1).T
    we_t = we_t.reshape(dec_cols // 32, 32, slab).transpose(1, 0, 2).reshape(32, -1)
    we_right, we_left = shift(we_t, 1), shift(we_t, -1)
    chunk = jnp.concatenate([mine, theirs])
    right = jnp.concatenate([chunk, we_right], axis=1)
    left = jnp.concatenate([chunk, we_left], axis=1)
    chunks, columns = {0: right}, {0: we_t, -1: we_right, 1: we_left}
    for step in range(1, 5):
        right = shift(right, 1)
        if step < 4:
            left = shift(left, -1)
            right, left = lax.optimization_barrier((right, left))
            chunks[step] = left
            columns[step + 1] = left
        chunks[-step] = right
        columns[-step - 1] = right

    row = jnp.zeros((nvis,), jnp.int32)
    row = lax.dynamic_update_slice_in_dim(row, vis_index[0], member * tok, 0)
    codes = jnp.pad(jnp.stack([row // 32, row % 32]), ((0, 14), (0, dec_width - nvis)))
    table = jnp.concatenate([position_table, codes.astype(BF16)])
    table, _ = lax.optimization_barrier((table, chunks[-3]))
    table = lax.all_gather(table, ("section", "mp"), axis=0, tiled=False)

    w_in = input_weight.transpose(1, 0, 2)
    held = sds((half, 3 * width), BF16)
    ordered = [chunks[offset] for offset in OFFSETS]
    p_part, xp_part, wp_low = call(
        project_kernel,
        [
            sds((nvis + 16, 3 * width + 128), BF16),
            sds((nvis, dec_width), F32),
            sds((dec_cols, width), BF16),
        ],
        ids,
        embed_weight,
        *ordered[:7],
        *[columns[offset] for offset in OFFSETS],
        output_weight,
        w_in,
        scratch=[
            sds((7, 2 * tok, half), BF16),
            sds((14 * tok + 16, half), BF16),
            held,
            sds((dec_cols, half), BF16),
            sds(output_weight.shape, BF16),
        ],
        far=tuple(range(2, 19)),
        copies=14 + 8 * (dec_cols // 32),
    )
    wp_other = swap(wp_low)
    p_own, xp_own, xp_send = call(
        project_last_kernel,
        [
            sds((nvis + 16, 3 * width + 128), BF16),
            sds((group, dec_width), F32),
            sds((group, dec_width), BF16),
        ],
        ids,
        embed_weight,
        p_part,
        xp_part,
        ordered[7],
        w_in,
        scratch=[sds((2 * tok, half), BF16), held],
        far=(4, 5),
        copies=13,
    )
    p_other = swap(p_own)
    xp_other = swap(xp_send)
    wp_other, _ = lax.optimization_barrier((wp_other, xp_send))
    (wp_parts,) = call(spread_kernel, [sds((copies, dec_cols, width), BF16)], ids, wp_low, wp_other)
    wp_parts, _ = lax.optimization_barrier((wp_parts, xp_other))
    wpt = exchange(wp_parts, "dp").reshape(dec_width, width)
    saved = [
        sds((heads, nvis, nvis), BF16),
        sds((nvis, width), BF16),
        sds((nvis, width), BF16),
        sds((nvis, width), BF16),
        sds((nvis, 128), F32),
    ]
    att, e_enc, q_enc, k_enc, v_enc, aux = call(
        attend_kernel,
        [sds((group, width), BF16)] + saved,
        ids,
        p_own,
        p_other,
        scratch=saved,
        far_out=(1, 2, 3, 4, 5),
        copies=heads + 4,
    )
    (embed_part,) = call(
        embed_kernel, [sds((8, tok, dec_width), BF16)], ids, att, wpt, xp_own, xp_other
    )

    w_dec = decoder_input.transpose(1, 0, 2)
    mask_row = mask_token.reshape(1, dec_width)
    (embed_sum,) = call(sum_kernel, [sds((8, tok, dec_width), BF16)], ids, exchange(embed_part, "mp"), limit=16)
    table, _ = lax.optimization_barrier((table, embed_sum))
    pos_vis, vis_row, hidden, km_t, vm, wq_t, wk_t = call(
        mask_kernel,
        [
            sds((nvis, dec_width), BF16),
            sds((1, nvis), jnp.int32),
            sds((1, npos), F32),
            sds((dec_width, npos), BF16),
            sds((npos, dec_width), BF16),
            sds((dec_width, dec_width), BF16),
            sds((dec_width, dec_width), BF16),
        ],
        ids,
        table,
        mask_row,
        w_dec,
        scratch=[sds(table.shape, BF16), sds(w_dec.shape, BF16)],
        far=(1, 3),
        copies=2,
    )
    emb_own = exchange(embed_sum, "mp").reshape(group, dec_width)
    emb_own, _ = lax.optimization_barrier((emb_own, hidden))
    emb_other = swap(emb_own)

    groups = dec_width // 128
    rows = (128 // DHD) * pos_dev
    prediction, g_own, g_send = call(
        decoder_kernel,
        [
            sds((pos_dev, target.shape[2]), BF16),
            sds((group, dec_width), F32),
            sds((group, dec_width), BF16),
        ],
        ids,
        emb_own,
        emb_other,
        mask_row,
        vis_row,
        hidden,
        wk_t,
        w_dec,
        pos_vis,
        position_table,
        wq_t,
        km_t,
        vm,
        decoder_output,
        pixel_weight,
        target[0],
        scratch=[sds((groups, rows, npos), BF16), sds((groups, rows, nvis), BF16)]
        + [sds(wk_t.shape, BF16), sds(w_dec.shape, BF16), sds(pos_vis.shape, BF16)]
        + [sds(position_table.shape, BF16), sds(wq_t.shape, BF16), sds(km_t.shape, BF16), sds(vm.shape, BF16)]
        + [sds(decoder_output.shape, BF16), sds(pixel_weight.shape, BF16), sds(target.shape[1:], BF16)],
        far=tuple(range(6, 16)),
        copies=12,
    )
    g_part = (g_own + swap(g_send).astype(F32)).astype(BF16).reshape(8, tok, dec_width)
    (g_sum,) = call(sum_kernel, [sds((8, tok, dec_width), BF16)], ids, exchange(g_part, "mp"), limit=16)
    ge_own = exchange(g_sum, "mp").reshape(group, dec_width)
    ge_other = swap(ge_own)

    right, left, parts = call(
        encoder_back_kernel,
        [
            sds((tok, half + 128), BF16),
            sds((tok, half + 128), BF16),
            sds((8, 2 * tok, half + 128), BF16),
        ],
        ids,
        ge_own,
        ge_other,
        embed_weight,
        wpt,
        e_enc,
        q_enc,
        k_enc,
        v_enc,
        aux,
        w_in,
        *ordered,
        scratch=[sds((dec_width, width), BF16)]
        + saved
        + [sds((2, 8, tok, half), BF16), held]
        + [sds((nvis, 3 * width), BF16), sds((8, 2 * tok, half + 128), BF16)],
        far=tuple(range(4, 19)),
        far_out=(2,),
        copies=26,
    )

    def part(offset):
        return lax.dynamic_index_in_dim(parts, (column + offset) % 8, 0, False).astype(F32)

    right, left = lax.optimization_barrier((shift(right, 1), shift(left, -1)))
    ahead, behind = part(3), part(-3)
    right = jnp.concatenate([right.astype(F32) + ahead[:tok], ahead[tok:]]).astype(BF16)
    left = jnp.concatenate([behind[:tok], left.astype(F32) + behind[tok:]]).astype(BF16)
    for offset in (2, 1):
        right, left = lax.optimization_barrier((shift(right, 1), shift(left, -1)))
        right = (right.astype(F32) + part(offset)).astype(BF16)
        left = (left.astype(F32) + part(-offset)).astype(BF16)
    total = shift(right, 1).astype(F32) + shift(left, -1).astype(F32) + part(0)
    (patch_grad,) = call(
        final_kernel,
        [sds((tok, model), BF16)],
        ids,
        x_own,
        total,
        swap(total[tok:].astype(BF16)),
        limit=16,
    )
    return (prediction[None], patch_grad[None])


def solution(mesh):
    group = ("section", "mp")
    in_specs = (
        P("dp", group, None),
        P("dp", group),
        P("section", None, "mp"),
        P("mp", "section"),
        P(group, None),
        P(),
        P(group, None),
        P(),
        P(),
        P(),
        P("dp", group, None),
    )
    out_specs = (P("dp", group, None), P("dp", group, None))
    return jax.shard_map(shards, mesh=mesh, in_specs=in_specs, out_specs=out_specs, check_vma=False)
```

```python
import math

import jax
import jax.numpy as jnp
from jax import lax
from jax.experimental import pallas as pl
from jax.experimental.pallas import tpu as pltpu
from jax.sharding import PartitionSpec as P

HD = 128
DHEADS = 16
DHD = 32
EPSILON = 1e-06
LOG2E = math.log2(math.e)
F32 = jnp.float32
BF16 = jnp.bfloat16
OFFSETS = (0, -1, 1, -2, 2, -3, 3, -4)


def dot(a, b):
    return lax.dot_general(a, b, (((1,), (0,)), ((), ())), preferred_element_type=F32)


def dot_nt(a, b):
    return lax.dot_general(a, b, (((1,), (1,)), ((), ())), preferred_element_type=F32)


def dot_tn(a, b):
    return lax.dot_general(a, b, (((0,), (0,)), ((), ())), preferred_element_type=F32)


def row_norm(values, axis=-1):
    centre = jnp.mean(values, axis=axis, keepdims=True)
    centered = values - centre
    inverse = lax.rsqrt(jnp.mean(centered * centered, axis=axis, keepdims=True) + EPSILON)
    return centered * inverse, inverse


def norm_back(normed, inverse, gradient, axis=-1):
    mean_grad = jnp.mean(gradient, axis=axis, keepdims=True)
    mean_dot = jnp.mean(gradient * normed, axis=axis, keepdims=True)
    return inverse * (gradient - mean_grad - normed * mean_dot)


def lanes(columns, rows):
    lane = lax.broadcasted_iota(jnp.int32, (rows, 128), 1)
    out = jnp.zeros((rows, 128), F32)
    for at, column in enumerate(columns):
        out = jnp.where(lane == at, column, out)
    return out


def call(kernel, outs, *args, scratch=(), far=(), far_out=(), copies=0, limit=58):
    specs = [pl.BlockSpec(memory_space=pltpu.SMEM)]
    for at in range(1, len(args)):
        specs.append(pl.BlockSpec(memory_space=pl.ANY if at in far else pltpu.VMEM))
    out_specs = [
        pl.BlockSpec(memory_space=pl.ANY if at in far_out else pltpu.VMEM) for at in range(len(outs))
    ]
    scratch = [pltpu.VMEM(shape.shape, shape.dtype) for shape in scratch]
    if copies:
        scratch.append(pltpu.SemaphoreType.DMA((copies,)))
    return pl.pallas_call(
        kernel,
        out_shape=tuple(outs),
        in_specs=specs,
        out_specs=tuple(out_specs),
        scratch_shapes=scratch,
        compiler_params=pltpu.CompilerParams(vmem_limit_bytes=limit * 2**20),
    )(*args)


def start(sems, first, *pairs):
    copies = [
        pltpu.make_async_copy(source, target, sems.at[first + at]) for at, (source, target) in enumerate(pairs)
    ]
    for copy in copies:
        copy.start()
    return copies


def finish(copies):
    for copy in copies:
        copy.wait()


def sds(shape, dtype):
    return jax.ShapeDtypeStruct(shape, dtype)


def weight_copies(w, held, pieces):
    _, rows, width = w.shape
    size = rows // pieces
    return [
        (w.at[at, pl.ds(piece * size, size)], held.at[pl.ds(piece * size, size), pl.ds(at * width, width)])
        for piece in range(pieces)
        for at in range(3)
    ]


def split3(values):
    first = values.astype(BF16).astype(F32)
    second = (values - first).astype(BF16).astype(F32)
    return [first, second, values - first - second]


def centre_rows(value):
    wide = value.astype(F32)
    centre = jnp.mean(wide, axis=1, keepdims=True)
    centered = wide - centre
    spread = jnp.sum(centered * centered, axis=1, keepdims=True)
    return centered.astype(BF16), lanes(split3(centre) + split3(spread), value.shape[0]).astype(BF16)


def place_rows(rows, at, target, cols=slice(None)):
    tok = rows.shape[0] // 2
    row = pl.multiple_of(at * tok, tok)
    target[pl.ds(row, tok), cols] = rows[:tok]
    target[pl.ds(row + 8 * tok, tok), cols] = rows[tok:]


def fold_kernel(ids, *refs):
    columns, wo_in, out = refs[:8], refs[8], refs[9]
    wt, wo, sems = refs[10:]
    half = wo.shape[1]
    slab = half // 8
    pieces = wt.shape[0] // 32
    loads = start(sems, 0, (wo_in, wo))
    for index, (source, offset) in enumerate(zip(columns, OFFSETS)):
        column = pl.multiple_of(lax.rem(ids[1] + offset + 8, 8) * slab, 128)
        base = source.shape[1] - pieces * slab
        for piece in range(pieces):
            target = wt.at[pl.ds(piece * 32, 32), pl.ds(column, slab)]
            source_part = source.at[:, pl.ds(base + piece * slab, slab)]
            loads += start(sems, 1 + index * pieces + piece, (source_part, target))
    finish(loads)
    total = dot_nt(wt[...], wo[...]).astype(BF16)
    for at in range(out.shape[0]):
        out[at] = total


def centre_rows(value):
    wide = value.astype(F32)
    centre = jnp.mean(wide, axis=1, keepdims=True)
    centered = wide - centre
    spread = jnp.sum(centered * centered, axis=1, keepdims=True)
    return centered.astype(BF16), lanes(split3(centre) + split3(spread), value.shape[0]).astype(BF16)


def place_rows(rows, at, target, cols=slice(None)):
    tok = rows.shape[0] // 2
    row = pl.multiple_of(at * tok, tok)
    target[pl.ds(row, tok), cols] = rows[:tok]
    target[pl.ds(row + 8 * tok, tok), cols] = rows[tok:]


def project_kernel(ids, we, *refs):
    chunks, w = refs[:8], refs[8]
    p_out, xp_own, xp_send = refs[9:12]
    held_chunks, xc, held, xs, sems = refs[12:]
    half, width3 = held.shape
    slab = half // 8
    rows2 = held_chunks.shape[1]
    rows = 8 * rows2
    m = ids[1]
    arrivals = start(
        sems, 0, *[(chunk.at[:, pl.ds(0, half)], held_chunks.at[at]) for at, chunk in enumerate(chunks)]
    )
    w_loads = start(sems, 8, *weight_copies(w, held, 4))
    own_column = pl.multiple_of(m * slab, 128)
    for index, offset in enumerate(OFFSETS):
        at = lax.rem(m + offset + 8, 8)
        arrivals[index].wait()
        low, moments = centre_rows(held_chunks[index])
        place_rows(low, at, xc)
        place_rows(moments, at, p_out, slice(width3, width3 + 128))
        place_rows(held_chunks[index, :, pl.ds(own_column, slab)], at, xs)
    xc[rows:, :] = jnp.ones((16, half), BF16)
    p_out[rows:, width3:] = jnp.zeros((16, 128), BF16)
    xp = dot(xs[...], we[...])
    xp_own[...] = xp[: rows // 2]
    xp_send[...] = xp[rows // 2 :].astype(BF16)
    quarter = half // 4
    product = jnp.zeros((rows + 16, width3), F32)
    for piece in range(4):
        finish(w_loads[piece * 3 : piece * 3 + 3])
        part = slice(piece * quarter, (piece + 1) * quarter)
        product = product + dot(xc[:, part], held[part, :])
    p_out[:, :width3] = product.astype(BF16)


def attend_kernel(ids, p_own, p_other, att, *refs):
    saved = refs[:5]
    e_out, q_out, k_out, v_out, aux = refs[5:10]
    sems = refs[10]
    rows = p_own.shape[0] - 16
    group = rows // 2
    width = (p_own.shape[1] - 128) // 3
    heads = width // HD
    model = 2 * 8 * width

    def moments(p):
        stats = p[:rows, 3 * width :].astype(F32)
        parts = [stats[:, at : at + 1] for at in range(6)]
        return parts[0] + parts[1] + parts[2], parts[3] + parts[4] + parts[5]

    def exchanged(values):
        return jnp.concatenate([values[group:], values[:group]])

    m_own, s_own = moments(p_own)
    m_other, s_other = [exchanged(value) for value in moments(p_other)]
    gap = (m_own - m_other) * 0.5
    centre = (m_own + m_other) * 0.5
    inverse = lax.rsqrt((s_own + s_other) / model + gap * gap + EPSILON)
    slope = p_own[rows : rows + 1, : 3 * width].astype(F32) - p_other[rows : rows + 1, : 3 * width].astype(F32)
    inv_q, inv_k, inv_l = [], [], []
    factor = LOG2E * HD**-0.5
    stores = []

    def mixture(at):
        cols = slice(at * HD, (at + 1) * HD)
        other = exchanged(p_other[:rows, cols]).astype(F32)
        return inverse * (p_own[:rows, cols].astype(F32) + other + gap * slope[:, cols])

    for head in range(heads):
        cols = slice(head * HD, (head + 1) * HD)
        q_hat, q_inv = row_norm(mixture(head))
        k_hat, k_inv = row_norm(mixture(heads + head))
        v_low = mixture(2 * heads + head).astype(BF16)
        q_low, k_low = q_hat.astype(BF16), k_hat.astype(BF16)
        e = jnp.exp2(dot_nt(q_low, k_low) * factor)
        l_inv = 1.0 / jnp.sum(e, axis=1, keepdims=True)
        e_low = e.astype(BF16)
        e_out[head] = e_low
        stores += start(sems, head, (e_out.at[head], saved[0].at[head]))
        att[:, cols] = (dot(e_low[:group], v_low) * l_inv[:group]).astype(BF16)
        q_out[:, cols] = q_low
        k_out[:, cols] = k_low
        v_out[:, cols] = v_low
        inv_q.append(q_inv)
        inv_k.append(k_inv)
        inv_l.append(l_inv)
    aux[...] = lanes([centre, inverse] + inv_l + inv_q + inv_k, rows)
    stores += start(sems, heads, (q_out, saved[1]), (k_out, saved[2]), (v_out, saved[3]), (aux, saved[4]))
    finish(stores)


def embed_kernel(ids, att, wpt_own, wpt_other, xp_own, xp_other, out, wpt):
    total = (wpt_own[...].astype(F32) + wpt_other[...].astype(F32)).astype(BF16)
    wpt[...] = total
    part = dot_nt(att[...], total) + xp_own[...] + xp_other[...].astype(F32)
    out[...] = part.astype(BF16).reshape(out.shape)


def sum_kernel(ids, parts, out):
    total = jnp.sum(parts[...].astype(F32), axis=0).astype(BF16)
    for at in range(out.shape[0]):
        out[at] = total


def encoder_back_kernel(ids, g_own, g_other, we, *refs):
    sources, w, chunks = refs[:6], refs[6], refs[7:15]
    right, left, parts_out = refs[15:18]
    wpt, e_in, q_in, k_in, v_in, aux, x_in, held, gmix, out, sems = refs[18:]
    rows, width = q_in.shape
    heads = width // HD
    half = held.shape[0]
    slab = half // 8
    tok = x_in.shape[2]
    m = ids[1]
    loads = start(sems, 0, *zip(sources, (wpt, e_in, q_in, k_in, v_in, aux)))
    w_loads = start(sems, 6, *weight_copies(w, held, 1))
    for index, offset in enumerate(OFFSETS):
        at = lax.rem(m + offset + 8, 8)
        for rel in range(2):
            rows_of = chunks[index].at[pl.ds(rel * tok, tok), pl.ds(0, half)]
            w_loads += start(sems, 10 + 2 * index + rel, (rows_of, x_in.at[rel, at]))
    factor = HD**-0.5
    gemb = jnp.concatenate([g_own[...], g_other[...]])
    glayer = dot_nt(gemb, we[...])
    loads[0].wait()
    gatt = dot(gemb, wpt[...]).astype(BF16)
    finish(loads[1:])
    for head in range(heads):
        cols = slice(head * HD, (head + 1) * HD)
        g_head = gatt[:, cols]
        q_low, k_low, v_low = q_in[:, cols], k_in[:, cols], v_in[:, cols]
        l_inv = aux[:, 2 + head : 3 + head]
        q_inv = aux[:, 2 + heads + head : 3 + heads + head]
        k_inv = aux[:, 2 + 2 * heads + head : 3 + 2 * heads + head]
        p = e_in[head].astype(F32) * l_inv
        gp = dot_nt(g_head, v_low)
        delta = jnp.sum(p * gp, axis=1, keepdims=True)
        gs = (p * (gp - delta)).astype(BF16)
        gq = dot(gs, k_low) * factor
        gk = dot_tn(gs, q_low) * factor
        gv = dot_tn(p.astype(BF16), g_head)
        gmix[:, cols] = norm_back(q_low.astype(F32), q_inv, gq).astype(BF16)
        gmix[:, width + head * HD : width + (head + 1) * HD] = norm_back(k_low.astype(F32), k_inv, gk).astype(BF16)
        gmix[:, 2 * width + head * HD : 2 * width + (head + 1) * HD] = gv.astype(BF16)
    finish(w_loads)
    centre, inverse = aux[:, 0:1], aux[:, 1:2]
    total = jnp.zeros((rows, 1), F32)
    total_dot = jnp.zeros((rows, 1), F32)
    for block in range(4):
        cols = slice(2 * block * slab, 2 * (block + 1) * slab)
        g = dot_nt(gmix[...], held[cols, :])
        normed = (x_in[:, :, :, cols].reshape(rows, 2 * slab).astype(F32) - centre) * inverse
        total = total + jnp.sum(g, axis=1, keepdims=True)
        total_dot = total_dot + jnp.sum(g * normed, axis=1, keepdims=True)
        mine = [glayer * jnp.where(2 * block + at == m, 1.0, 0.0) for at in range(2)]
        value = (g * inverse + jnp.concatenate(mine, axis=1)).astype(BF16).reshape(2, 8, tok, 2 * slab)
        out[:, :tok, cols] = value[0]
        out[:, tok:, cols] = value[1]
    sums = lanes((total, total_dot), rows).astype(BF16).reshape(2, 8, tok, 128)
    out[:, :tok, half:] = sums[0]
    out[:, tok:, half:] = sums[1]
    store = start(sems, 9, (out, parts_out))
    right[...] = out[lax.rem(m + 4, 8), :tok]
    left[...] = out[lax.rem(m + 4, 8), tok:]
    finish(store)


def final_kernel(ids, x_own, both, other, out):
    s = ids[0]
    tok, model = x_own.shape
    half = model // 2
    normed, inverse = row_norm(x_own[...].astype(F32))
    mine, theirs = both[:tok, :], other[...].astype(F32)
    total = (mine[:, half : half + 1] + theirs[:, half : half + 1]) / model
    total_dot = (mine[:, half + 1 : half + 2] + theirs[:, half + 1 : half + 2]) / model
    first = jnp.where(s == 0, mine[:, :half], theirs[:, :half])
    second = jnp.where(s == 0, theirs[:, :half], mine[:, :half])
    out[:, :half] = (first - inverse * (total + normed[:, :half] * total_dot)).astype(BF16)
    out[:, half:] = (second - inverse * (total + normed[:, half:] * total_dot)).astype(BF16)


def head_norm_t(values):
    width, n = values.shape
    hat, inverse = row_norm(values.reshape(DHEADS, DHD, n), axis=1)
    return hat.reshape(width, n), inverse


def head_back_t(hat, inverse, gradient):
    width, n = hat.shape
    back = norm_back(
        hat.reshape(DHEADS, DHD, n), inverse, gradient.reshape(DHEADS, DHD, n), axis=1
    )
    return back.reshape(width, n)


def mask_kernel(ids, table_in, mask, w_in, pos_vis, vis_row, hidden, k_t, v, wq_t, wk_t, table, w, sems):
    loads = start(sems, 0, (w_in, w), (table_in, table))
    loads[0].wait()
    wq_t[...] = w[0].T
    wk_t[...] = w[1].T
    loads[1].wait()
    members, pos_dev = table.shape[0], table.shape[1] - 16
    npos, width = members * pos_dev, table.shape[2]
    nvis = vis_row.shape[1]
    pos_all = table[:, :pos_dev, :].reshape(npos, width)
    codes = jnp.sum(table[:, pos_dev:, :].astype(F32), axis=0)
    row = codes[0:1, :nvis] * 32.0 + codes[1:2, :nvis]
    other = jnp.concatenate([row[:, nvis // 2 :], row[:, : nvis // 2]], axis=1)
    vis = jnp.where(ids[0] == 0, row, other).astype(jnp.int32)
    vis_row[...] = vis
    hot = jnp.where(lax.broadcasted_iota(jnp.int32, (npos, nvis), 0) == vis, 1.0, 0.0).astype(BF16)
    pos_vis[...] = dot_tn(hot, pos_all).astype(BF16)
    hidden[...] = 1.0 - dot_nt(jnp.ones((16, nvis), BF16), hot)[0:1, :]
    hat, _ = row_norm(pos_all.astype(F32) + mask[...].astype(F32))
    low = hat.astype(BF16)
    key_hat, _ = head_norm_t(dot_nt(wk_t[...], low))
    k_t[...] = key_hat.astype(BF16)
    v[...] = dot(low, w[2]).astype(BF16)


def decoder_kernel(ids, emb_own, emb_other, mask, vis_row, hidden, *refs):
    wk_t_in, w_in, pos_vis_in, pos_own_in, wq_t_in, km_t_in, vm_in, w_out_in, w_pix_in, target_in = refs[:10]
    pred, g_own, g_other, em_ref, ev_ref = refs[10:15]
    wk_t, w, pos_vis, pos_own, wq_t, km_t, vm, w_out, w_pix, target, sems = refs[15:]
    loads = start(
        sems,
        0,
        (pos_vis_in, pos_vis),
        (wk_t_in, wk_t),
        (w_in.at[2], w.at[2]),
        (pos_own_in, pos_own),
        (wq_t_in, wq_t),
        (km_t_in, km_t),
        (vm_in, vm),
        (w_out_in, w_out),
        (w_pix_in, w_pix),
        (target_in, target),
        (w_in.at[0], w.at[0]),
        (w_in.at[1], w.at[1]),
    )
    npos_dev, width = pos_own.shape
    nvis = pos_vis.shape[0]
    group = nvis // 2
    member = ids[2]
    groups = width // 128
    per = 128 // DHD
    rows = per * npos_dev
    factor = DHD**-0.5
    emb = jnp.concatenate([emb_own[...], emb_other[...]])
    loads[0].wait()
    vis_hat, vis_inv = row_norm(emb.astype(F32) + pos_vis[...].astype(F32))
    vis_low = vis_hat.astype(BF16)
    finish(loads[1:3])
    kv_hat, kv_inv = head_norm_t(dot_nt(wk_t[...], vis_low))
    kv_t = kv_hat.astype(BF16)
    vv = dot(vis_low, w[2]).astype(BF16)
    position = lax.broadcasted_iota(jnp.int32, (npos_dev, nvis), 0) + member * npos_dev
    hot = jnp.where(position == vis_row[...], 1.0, 0.0)
    seen = jnp.sum(hot, axis=1, keepdims=True)
    hot_low = hot.astype(BF16)
    filled = dot(hot_low, emb) + (1.0 - seen) * mask[...].astype(F32)
    finish(loads[3:5])
    stream = filled + pos_own[...].astype(F32)
    own_hat, own_inv = row_norm(stream)
    q_t, q_inv = head_norm_t(dot_nt(wq_t[...], own_hat.astype(BF16)))
    q_low = q_t.T.astype(BF16)
    head_mask = (
        lax.broadcasted_iota(jnp.int32, (rows, 128), 0) // npos_dev
        == lax.broadcasted_iota(jnp.int32, (rows, 128), 1) // DHD
    )

    def spread(values):
        return jnp.where(head_mask, jnp.concatenate([values] * per, axis=0), jnp.zeros((), values.dtype))

    def gather(values):
        return jnp.sum(jnp.where(head_mask, values, 0.0).reshape(per, npos_dev, 128), axis=0)

    finish(loads[5:7])
    attended, inv_l = [], []
    for at in range(groups):
        cols = slice(at * 128, (at + 1) * 128)
        q_wide = spread(q_low[:, cols])
        em = jnp.exp2(dot(q_wide, km_t[cols, :]) * (factor * LOG2E)) * hidden[...]
        ev = jnp.exp2(dot(q_wide, kv_t[cols, :]) * (factor * LOG2E))
        l_inv = 1.0 / (jnp.sum(em, axis=1, keepdims=True) + jnp.sum(ev, axis=1, keepdims=True))
        em_low, ev_low = em.astype(BF16), ev.astype(BF16)
        em_ref[at] = em_low
        ev_ref[at] = ev_low
        attended.append(gather((dot(em_low, vm[:, cols]) + dot(ev_low, vv[:, cols])) * l_inv))
        inv_l.append(l_inv)
    att = jnp.concatenate(attended, axis=1)
    finish(loads[7:])
    second = stream + dot(att.astype(BF16), w_out[...])
    final_hat, final_inv = row_norm(second)
    full = dot(final_hat.astype(BF16), w_pix[...])
    pred[...] = full.astype(BF16)
    error = jnp.where(seen > 0, 0.0, full - target[...].astype(F32)).astype(BF16)
    g_second = norm_back(final_hat, final_inv, dot_nt(error, w_pix[...]))
    g_att = dot_nt(g_second.astype(BF16), w_out[...]).astype(BF16)
    product = g_att.astype(F32) * att
    gq, gk_t, gv = [], [], []
    for at in range(groups):
        cols = slice(at * 128, (at + 1) * 128)
        q_wide = spread(q_low[:, cols])
        g_wide = spread(g_att[:, cols])
        delta = jnp.sum(spread(product[:, cols]), axis=1, keepdims=True)
        l_inv = inv_l[at]
        pv = ev_ref[at].astype(F32) * l_inv
        gs_v = (pv * (dot_nt(g_wide, vv[:, cols]) - delta)).astype(BF16)
        pm = em_ref[at].astype(F32) * l_inv
        gs_m = (pm * (dot_nt(g_wide, vm[:, cols]) - delta)).astype(BF16)
        gq.append(gather(dot_nt(gs_m, km_t[cols, :]) + dot_nt(gs_v, kv_t[cols, :])) * factor)
        gk_t.append(dot_tn(q_wide, gs_v) * factor)
        gv.append(dot_tn(pv.astype(BF16), g_wide).astype(BF16))
    gq_back = head_back_t(q_t, q_inv, jnp.concatenate(gq, axis=1).T).T.astype(BF16)
    g_stream_own = g_second + norm_back(own_hat, own_inv, dot_nt(gq_back, w[0]))
    gk_back = head_back_t(kv_hat, kv_inv, jnp.concatenate(gk_t, axis=0)).T.astype(BF16)
    from_keys = dot_nt(gk_back, w[1]) + dot_nt(jnp.concatenate(gv, axis=1), w[2])
    part = norm_back(vis_hat, vis_inv, from_keys) + dot_tn(hot_low, g_stream_own.astype(BF16))
    g_own[...] = part[:group]
    g_other[...] = part[group:].astype(BF16)


def shards(
    patches,
    vis_index,
    input_weight,
    output_weight,
    embed_weight,
    mask_token,
    position_table,
    decoder_input,
    decoder_output,
    pixel_weight,
    target,
):
    section = lax.axis_index("section")
    column = lax.axis_index("mp")
    member = lax.axis_index(("section", "mp"))
    copies = lax.axis_size("dp")
    ids = jnp.stack([section, column, member]).astype(jnp.int32)
    x_own = patches[0]
    tok, model = x_own.shape
    half = model // 2
    slab, dec_width = embed_weight.shape
    width = output_weight.shape[0]
    heads = width // HD
    group = 8 * tok
    nvis = 2 * group
    pos_dev = position_table.shape[0]
    npos = 16 * pos_dev

    def swap(value):
        return lax.ppermute(value, "section", [(0, 1), (1, 0)])

    def shift(value, by):
        return lax.ppermute(value, "mp", [(i, (i + by) % 8) for i in range(8)])

    def exchange(value, axis):
        return lax.all_to_all(value, axis, 0, 0, tiled=True)

    mine = lax.dynamic_slice_in_dim(x_own, section * half, half, 1)
    theirs = swap(lax.dynamic_slice_in_dim(x_own, (1 - section) * half, half, 1))
    dec_cols = dec_width // copies
    we_t = lax.dynamic_slice_in_dim(embed_weight, lax.axis_index("dp") * dec_cols, dec_cols, 1).T
    we_t = we_t.reshape(dec_cols // 32, 32, slab).transpose(1, 0, 2).reshape(32, -1)
    we_right, we_left = shift(we_t, 1), shift(we_t, -1)
    chunk = jnp.concatenate([mine, theirs])
    right = jnp.concatenate([chunk, we_right], axis=1)
    left = jnp.concatenate([chunk, we_left], axis=1)
    chunks, columns = {0: right}, {0: we_t, -1: we_right, 1: we_left}
    for step in range(1, 5):
        right = shift(right, 1)
        if step < 4:
            left = shift(left, -1)
            right, left = lax.optimization_barrier((right, left))
            chunks[step] = left
            columns[step + 1] = left
        chunks[-step] = right
        columns[-step - 1] = right

    row = jnp.zeros((nvis,), jnp.int32)
    row = lax.dynamic_update_slice_in_dim(row, vis_index[0], member * tok, 0)
    codes = jnp.pad(jnp.stack([row // 32, row % 32]), ((0, 14), (0, dec_width - nvis)))
    table = jnp.concatenate([position_table, codes.astype(BF16)])
    table, _ = lax.optimization_barrier((table, chunks[-3]))
    table = lax.all_gather(table, ("section", "mp"), axis=0, tiled=False)

    w_in = input_weight.transpose(1, 0, 2)
    held = sds((half, 3 * width), BF16)
    ordered = [chunks[offset] for offset in OFFSETS]
    (wp_parts,) = call(
        fold_kernel,
        [sds((copies, dec_cols, width), BF16)],
        ids,
        *[columns[offset] for offset in OFFSETS],
        output_weight,
        scratch=[sds((dec_cols, half), BF16), sds(output_weight.shape, BF16)],
        far=tuple(range(1, 10)),
        copies=1 + 8 * (dec_cols // 32),
    )
    wpt_own = exchange(wp_parts, "dp").reshape(dec_width, width)
    ids_late, _ = lax.optimization_barrier((ids, wp_parts))
    p_own, xp_own, xp_send = call(
        project_kernel,
        [
            sds((nvis + 16, 3 * width + 128), BF16),
            sds((group, dec_width), F32),
            sds((group, dec_width), BF16),
        ],
        ids_late,
        embed_weight,
        *ordered,
        w_in,
        scratch=[
            sds((8, 2 * tok, half), BF16),
            sds((nvis + 16, half), BF16),
            held,
            sds((nvis, slab), BF16),
        ],
        far=tuple(range(2, 11)),
        copies=20,
    )
    p_other = swap(p_own)
    xp_other = swap(xp_send)
    wpt_other = swap(wpt_own)
    saved = [
        sds((heads, nvis, nvis), BF16),
        sds((nvis, width), BF16),
        sds((nvis, width), BF16),
        sds((nvis, width), BF16),
        sds((nvis, 128), F32),
    ]
    att, e_enc, q_enc, k_enc, v_enc, aux = call(
        attend_kernel,
        [sds((group, width), BF16)] + saved,
        ids,
        p_own,
        p_other,
        scratch=saved,
        far_out=(1, 2, 3, 4, 5),
        copies=heads + 4,
    )
    embed_part, wpt = call(
        embed_kernel,
        [sds((8, tok, dec_width), BF16), sds((dec_width, width), BF16)],
        ids,
        att,
        wpt_own,
        wpt_other,
        xp_own,
        xp_other,
    )

    w_dec = decoder_input.transpose(1, 0, 2)
    mask_row = mask_token.reshape(1, dec_width)
    (embed_sum,) = call(sum_kernel, [sds((8, tok, dec_width), BF16)], ids, exchange(embed_part, "mp"), limit=16)
    table, _ = lax.optimization_barrier((table, embed_sum))
    pos_vis, vis_row, hidden, km_t, vm, wq_t, wk_t = call(
        mask_kernel,
        [
            sds((nvis, dec_width), BF16),
            sds((1, nvis), jnp.int32),
            sds((1, npos), F32),
            sds((dec_width, npos), BF16),
            sds((npos, dec_width), BF16),
            sds((dec_width, dec_width), BF16),
            sds((dec_width, dec_width), BF16),
        ],
        ids,
        table,
        mask_row,
        w_dec,
        scratch=[sds(table.shape, BF16), sds(w_dec.shape, BF16)],
        far=(1, 3),
        copies=2,
    )
    emb_own = exchange(embed_sum, "mp").reshape(group, dec_width)
    emb_own, _ = lax.optimization_barrier((emb_own, hidden))
    emb_other = swap(emb_own)

    groups = dec_width // 128
    rows = (128 // DHD) * pos_dev
    prediction, g_own, g_send = call(
        decoder_kernel,
        [
            sds((pos_dev, target.shape[2]), BF16),
            sds((group, dec_width), F32),
            sds((group, dec_width), BF16),
        ],
        ids,
        emb_own,
        emb_other,
        mask_row,
        vis_row,
        hidden,
        wk_t,
        w_dec,
        pos_vis,
        position_table,
        wq_t,
        km_t,
        vm,
        decoder_output,
        pixel_weight,
        target[0],
        scratch=[sds((groups, rows, npos), BF16), sds((groups, rows, nvis), BF16)]
        + [sds(wk_t.shape, BF16), sds(w_dec.shape, BF16), sds(pos_vis.shape, BF16)]
        + [sds(position_table.shape, BF16), sds(wq_t.shape, BF16), sds(km_t.shape, BF16), sds(vm.shape, BF16)]
        + [sds(decoder_output.shape, BF16), sds(pixel_weight.shape, BF16), sds(target.shape[1:], BF16)],
        far=tuple(range(6, 16)),
        copies=12,
    )
    g_part = (g_own + swap(g_send).astype(F32)).astype(BF16).reshape(8, tok, dec_width)
    (g_sum,) = call(sum_kernel, [sds((8, tok, dec_width), BF16)], ids, exchange(g_part, "mp"), limit=16)
    ge_own = exchange(g_sum, "mp").reshape(group, dec_width)
    ge_other = swap(ge_own)

    right, left, parts = call(
        encoder_back_kernel,
        [
            sds((tok, half + 128), BF16),
            sds((tok, half + 128), BF16),
            sds((8, 2 * tok, half + 128), BF16),
        ],
        ids,
        ge_own,
        ge_other,
        embed_weight,
        wpt,
        e_enc,
        q_enc,
        k_enc,
        v_enc,
        aux,
        w_in,
        *ordered,
        scratch=[sds((dec_width, width), BF16)]
        + saved
        + [sds((2, 8, tok, half), BF16), held]
        + [sds((nvis, 3 * width), BF16), sds((8, 2 * tok, half + 128), BF16)],
        far=tuple(range(4, 19)),
        far_out=(2,),
        copies=26,
    )

    def part(offset):
        return lax.dynamic_index_in_dim(parts, (column + offset) % 8, 0, False).astype(F32)

    right, left = lax.optimization_barrier((shift(right, 1), shift(left, -1)))
    ahead, behind = part(3), part(-3)
    right = jnp.concatenate([right.astype(F32) + ahead[:tok], ahead[tok:]]).astype(BF16)
    left = jnp.concatenate([behind[:tok], left.astype(F32) + behind[tok:]]).astype(BF16)
    for offset in (2, 1):
        right, left = lax.optimization_barrier((shift(right, 1), shift(left, -1)))
        right = (right.astype(F32) + part(offset)).astype(BF16)
        left = (left.astype(F32) + part(-offset)).astype(BF16)
    total = shift(right, 1).astype(F32) + shift(left, -1).astype(F32) + part(0)
    (patch_grad,) = call(
        final_kernel,
        [sds((tok, model), BF16)],
        ids,
        x_own,
        total,
        swap(total[tok:].astype(BF16)),
        limit=16,
    )
    return (prediction[None], patch_grad[None])


def solution(mesh):
    group = ("section", "mp")
    in_specs = (
        P("dp", group, None),
        P("dp", group),
        P("section", None, "mp"),
        P("mp", "section"),
        P(group, None),
        P(),
        P(group, None),
        P(),
        P(),
        P(),
        P("dp", group, None),
    )
    out_specs = (P("dp", group, None), P("dp", group, None))
    return jax.shard_map(shards, mesh=mesh, in_specs=in_specs, out_specs=out_specs, check_vma=False)
```

```python
import math

import jax
import jax.numpy as jnp
from jax import lax
from jax.experimental import pallas as pl
from jax.experimental.pallas import tpu as pltpu
from jax.sharding import PartitionSpec as P

HD = 128
DHEADS = 16
DHD = 32
EPSILON = 1e-06
LOG2E = math.log2(math.e)
F32 = jnp.float32
BF16 = jnp.bfloat16
OFFSETS = (0, -1, 1, -2, 2, -3, 3, -4)


def dot(a, b):
    return lax.dot_general(a, b, (((1,), (0,)), ((), ())), preferred_element_type=F32)


def dot_nt(a, b):
    return lax.dot_general(a, b, (((1,), (1,)), ((), ())), preferred_element_type=F32)


def dot_tn(a, b):
    return lax.dot_general(a, b, (((0,), (0,)), ((), ())), preferred_element_type=F32)


def row_norm(values, axis=-1):
    centre = jnp.mean(values, axis=axis, keepdims=True)
    centered = values - centre
    inverse = lax.rsqrt(jnp.mean(centered * centered, axis=axis, keepdims=True) + EPSILON)
    return centered * inverse, inverse


def norm_back(normed, inverse, gradient, axis=-1):
    mean_grad = jnp.mean(gradient, axis=axis, keepdims=True)
    mean_dot = jnp.mean(gradient * normed, axis=axis, keepdims=True)
    return inverse * (gradient - mean_grad - normed * mean_dot)


def lanes(columns, rows):
    lane = lax.broadcasted_iota(jnp.int32, (rows, 128), 1)
    out = jnp.zeros((rows, 128), F32)
    for at, column in enumerate(columns):
        out = jnp.where(lane == at, column, out)
    return out


def call(kernel, outs, *args, scratch=(), far=(), far_out=(), copies=0, limit=58):
    specs = [pl.BlockSpec(memory_space=pltpu.SMEM)]
    for at in range(1, len(args)):
        specs.append(pl.BlockSpec(memory_space=pl.ANY if at in far else pltpu.VMEM))
    out_specs = [
        pl.BlockSpec(memory_space=pl.ANY if at in far_out else pltpu.VMEM) for at in range(len(outs))
    ]
    scratch = [pltpu.VMEM(shape.shape, shape.dtype) for shape in scratch]
    if copies:
        scratch.append(pltpu.SemaphoreType.DMA((copies,)))
    return pl.pallas_call(
        kernel,
        out_shape=tuple(outs),
        in_specs=specs,
        out_specs=tuple(out_specs),
        scratch_shapes=scratch,
        compiler_params=pltpu.CompilerParams(vmem_limit_bytes=limit * 2**20),
    )(*args)


def start(sems, first, *pairs):
    copies = [
        pltpu.make_async_copy(source, target, sems.at[first + at]) for at, (source, target) in enumerate(pairs)
    ]
    for copy in copies:
        copy.start()
    return copies


def finish(copies):
    for copy in copies:
        copy.wait()


def sds(shape, dtype):
    return jax.ShapeDtypeStruct(shape, dtype)


def weight_copies(w, held, pieces):
    _, rows, width = w.shape
    size = rows // pieces
    return [
        (w.at[at, pl.ds(piece * size, size)], held.at[pl.ds(piece * size, size), pl.ds(at * width, width)])
        for piece in range(pieces)
        for at in range(3)
    ]


def split3(values):
    first = values.astype(BF16).astype(F32)
    second = (values - first).astype(BF16).astype(F32)
    return [first, second, values - first - second]


def centre_rows(value):
    wide = value.astype(F32)
    centre = jnp.mean(wide, axis=1, keepdims=True)
    centered = wide - centre
    spread = jnp.sum(centered * centered, axis=1, keepdims=True)
    return centered.astype(BF16), lanes(split3(centre) + split3(spread), value.shape[0]).astype(BF16)


def place_rows(rows, at, target, cols=slice(None)):
    tok = rows.shape[0] // 2
    row = pl.multiple_of(at * tok, tok)
    target[pl.ds(row, tok), cols] = rows[:tok]
    target[pl.ds(row + 8 * tok, tok), cols] = rows[tok:]


def fold_kernel(ids, *refs):
    columns, wo_in, out = refs[:8], refs[8], refs[9]
    wt, wo, sems = refs[10:]
    half = wo.shape[1]
    slab = half // 8
    pieces = wt.shape[0] // 32
    loads = start(sems, 0, (wo_in, wo))
    for index, (source, offset) in enumerate(zip(columns, OFFSETS)):
        column = pl.multiple_of(lax.rem(ids[1] + offset + 8, 8) * slab, 128)
        base = source.shape[1] - pieces * slab
        for piece in range(pieces):
            target = wt.at[pl.ds(piece * 32, 32), pl.ds(column, slab)]
            source_part = source.at[:, pl.ds(base + piece * slab, slab)]
            loads += start(sems, 1 + index * pieces + piece, (source_part, target))
    finish(loads)
    total = dot_nt(wt[...], wo[...]).astype(BF16)
    for at in range(out.shape[0]):
        out[at] = total


def centre_rows(value):
    wide = value.astype(F32)
    centre = jnp.mean(wide, axis=1, keepdims=True)
    centered = wide - centre
    spread = jnp.sum(centered * centered, axis=1, keepdims=True)
    return centered.astype(BF16), lanes(split3(centre) + split3(spread), value.shape[0]).astype(BF16)


def place_rows(rows, at, target, cols=slice(None)):
    tok = rows.shape[0] // 2
    row = pl.multiple_of(at * tok, tok)
    target[pl.ds(row, tok), cols] = rows[:tok]
    target[pl.ds(row + 8 * tok, tok), cols] = rows[tok:]


def project_kernel(ids, we, *refs):
    chunks, w = refs[:8], refs[8]
    p_out, xp_own, xp_send = refs[9:12]
    held_chunks, xc, held, xs, sems = refs[12:]
    half, width3 = held.shape
    slab = half // 8
    rows2 = held_chunks.shape[1]
    rows = 8 * rows2
    m = ids[1]
    arrivals = start(
        sems, 0, *[(chunk.at[:, pl.ds(0, half)], held_chunks.at[at]) for at, chunk in enumerate(chunks)]
    )
    w_loads = start(sems, 8, *weight_copies(w, held, 4))
    own_column = pl.multiple_of(m * slab, 128)
    for index, offset in enumerate(OFFSETS):
        at = lax.rem(m + offset + 8, 8)
        arrivals[index].wait()
        low, moments = centre_rows(held_chunks[index])
        place_rows(low, at, xc)
        place_rows(moments, at, p_out, slice(width3, width3 + 128))
        place_rows(held_chunks[index, :, pl.ds(own_column, slab)], at, xs)
    xc[rows:, :] = jnp.ones((16, half), BF16)
    p_out[rows:, width3:] = jnp.zeros((16, 128), BF16)
    xp = dot(xs[...], we[...])
    xp_own[...] = xp[: rows // 2]
    xp_send[...] = xp[rows // 2 :].astype(BF16)
    quarter = half // 4
    product = jnp.zeros((rows + 16, width3), F32)
    for piece in range(4):
        finish(w_loads[piece * 3 : piece * 3 + 3])
        part = slice(piece * quarter, (piece + 1) * quarter)
        product = product + dot(xc[:, part], held[part, :])
    p_out[:, :width3] = product.astype(BF16)


def scene_mixture(p_own, p_other):
    rows = p_own.shape[0] - 16
    group = rows // 2
    width3 = p_own.shape[1] - 128
    model = 16 * (width3 // 3)

    def moments(p):
        stats = p[:rows, width3:].astype(F32)
        parts = [stats[:, at : at + 1] for at in range(6)]
        return parts[0] + parts[1] + parts[2], parts[3] + parts[4] + parts[5]

    def exchanged(values):
        return jnp.concatenate([values[group:], values[:group]])

    m_own, s_own = moments(p_own)
    m_other, s_other = [exchanged(value) for value in moments(p_other)]
    gap = (m_own - m_other) * 0.5
    centre = (m_own + m_other) * 0.5
    inverse = lax.rsqrt((s_own + s_other) / model + gap * gap + EPSILON)
    slope = p_own[rows : rows + 1, :width3].astype(F32) - p_other[rows : rows + 1, :width3].astype(F32)

    def mixture(at, count):
        cols = slice(at * HD, (at + 1) * HD)
        other = p_other[group : group + min(count, group), cols]
        if count > group:
            other = jnp.concatenate([other, p_other[: count - group, cols]])
        total = p_own[:count, cols].astype(F32) + other.astype(F32) + gap[:count] * slope[:, cols]
        return inverse[:count] * total

    return centre, inverse, mixture


def attend_kernel(ids, p_own, p_other, att):
    rows = p_own.shape[0] - 16
    heads = att.shape[1] // HD
    _, _, mixture = scene_mixture(p_own, p_other)
    factor = LOG2E * HD**-0.5
    for head in range(heads):
        q_low = row_norm(mixture(head, rows // 2))[0].astype(BF16)
        k_low = row_norm(mixture(heads + head, rows))[0].astype(BF16)
        v_low = mixture(2 * heads + head, rows).astype(BF16)
        e = jnp.exp2(dot_nt(q_low, k_low) * factor)
        l_inv = 1.0 / jnp.sum(e, axis=1, keepdims=True)
        att[:, head * HD : (head + 1) * HD] = (dot(e.astype(BF16), v_low) * l_inv).astype(BF16)


def save_kernel(ids, p_own, p_other, *refs):
    saved = refs[:5]
    e_out, q_out, k_out, v_out, aux, sems = refs[5:]
    rows, width = q_out.shape
    heads = width // HD
    centre, inverse, mixture = scene_mixture(p_own, p_other)
    inv_q, inv_k, inv_l = [], [], []
    factor = LOG2E * HD**-0.5
    stores = []
    for head in range(heads):
        cols = slice(head * HD, (head + 1) * HD)
        q_hat, q_inv = row_norm(mixture(head, rows))
        k_hat, k_inv = row_norm(mixture(heads + head, rows))
        q_low, k_low = q_hat.astype(BF16), k_hat.astype(BF16)
        e = jnp.exp2(dot_nt(q_low, k_low) * factor)
        e_out[head] = e.astype(BF16)
        stores += start(sems, head, (e_out.at[head], saved[0].at[head]))
        q_out[:, cols] = q_low
        k_out[:, cols] = k_low
        v_out[:, cols] = mixture(2 * heads + head, rows).astype(BF16)
        inv_q.append(q_inv)
        inv_k.append(k_inv)
        inv_l.append(1.0 / jnp.sum(e, axis=1, keepdims=True))
    aux[...] = lanes([centre, inverse] + inv_l + inv_q + inv_k, rows)
    stores += start(sems, heads, (q_out, saved[1]), (k_out, saved[2]), (v_out, saved[3]), (aux, saved[4]))
    finish(stores)


def embed_kernel(ids, att, wpt_own, wpt_other, xp_own, xp_other, out, wpt):
    total = (wpt_own[...].astype(F32) + wpt_other[...].astype(F32)).astype(BF16)
    wpt[...] = total
    part = dot_nt(att[...], total) + xp_own[...] + xp_other[...].astype(F32)
    out[...] = part.astype(BF16).reshape(out.shape)


def sum_kernel(ids, parts, out):
    total = jnp.sum(parts[...].astype(F32), axis=0).astype(BF16)
    for at in range(out.shape[0]):
        out[at] = total


def encoder_back_kernel(ids, g_own, g_other, we, *refs):
    sources, w, chunks = refs[:6], refs[6], refs[7:15]
    right, left, parts_out = refs[15:18]
    wpt, e_in, q_in, k_in, v_in, aux, x_in, held, gmix, out, sems = refs[18:]
    rows, width = q_in.shape
    heads = width // HD
    half = held.shape[0]
    slab = half // 8
    tok = x_in.shape[2]
    m = ids[1]
    loads = start(sems, 0, *zip(sources, (wpt, e_in, q_in, k_in, v_in, aux)))
    w_loads = start(sems, 6, *weight_copies(w, held, 1))
    for index, offset in enumerate(OFFSETS):
        at = lax.rem(m + offset + 8, 8)
        for rel in range(2):
            rows_of = chunks[index].at[pl.ds(rel * tok, tok), pl.ds(0, half)]
            w_loads += start(sems, 10 + 2 * index + rel, (rows_of, x_in.at[rel, at]))
    factor = HD**-0.5
    gemb = jnp.concatenate([g_own[...], g_other[...]])
    glayer = dot_nt(gemb, we[...])
    loads[0].wait()
    gatt = dot(gemb, wpt[...]).astype(BF16)
    finish(loads[1:])
    for head in range(heads):
        cols = slice(head * HD, (head + 1) * HD)
        g_head = gatt[:, cols]
        q_low, k_low, v_low = q_in[:, cols], k_in[:, cols], v_in[:, cols]
        l_inv = aux[:, 2 + head : 3 + head]
        q_inv = aux[:, 2 + heads + head : 3 + heads + head]
        k_inv = aux[:, 2 + 2 * heads + head : 3 + 2 * heads + head]
        p = e_in[head].astype(F32) * l_inv
        gp = dot_nt(g_head, v_low)
        delta = jnp.sum(p * gp, axis=1, keepdims=True)
        gs = (p * (gp - delta)).astype(BF16)
        gq = dot(gs, k_low) * factor
        gk = dot_tn(gs, q_low) * factor
        gv = dot_tn(p.astype(BF16), g_head)
        gmix[:, cols] = norm_back(q_low.astype(F32), q_inv, gq).astype(BF16)
        gmix[:, width + head * HD : width + (head + 1) * HD] = norm_back(k_low.astype(F32), k_inv, gk).astype(BF16)
        gmix[:, 2 * width + head * HD : 2 * width + (head + 1) * HD] = gv.astype(BF16)
    finish(w_loads)
    centre, inverse = aux[:, 0:1], aux[:, 1:2]
    total = jnp.zeros((rows, 1), F32)
    total_dot = jnp.zeros((rows, 1), F32)
    stores = []
    for block in range(4):
        cols = slice(2 * block * slab, 2 * (block + 1) * slab)
        g = dot_nt(gmix[...], held[cols, :])
        normed = (x_in[:, :, :, cols].reshape(rows, 2 * slab).astype(F32) - centre) * inverse
        total = total + jnp.sum(g, axis=1, keepdims=True)
        total_dot = total_dot + jnp.sum(g * normed, axis=1, keepdims=True)
        mine = [glayer * jnp.where(2 * block + at == m, 1.0, 0.0) for at in range(2)]
        value = (g * inverse + jnp.concatenate(mine, axis=1)).astype(BF16).reshape(2, 8, tok, 2 * slab)
        out[:, :tok, cols] = value[0]
        out[:, tok:, cols] = value[1]
        span = pl.ds(cols.start, 2 * slab)
        stores += start(sems, 26 + block, (out.at[:, :, span], parts_out.at[:, :, span]))
    sums = lanes((total, total_dot), rows).astype(BF16).reshape(2, 8, tok, 128)
    out[:, :tok, half:] = sums[0]
    out[:, tok:, half:] = sums[1]
    span = pl.ds(half, 128)
    stores += start(sems, 9, (out.at[:, :, span], parts_out.at[:, :, span]))
    right[...] = out[lax.rem(m + 4, 8), :tok]
    left[...] = out[lax.rem(m + 4, 8), tok:]
    finish(stores)


def final_kernel(ids, x_own, both, other, out):
    s = ids[0]
    tok, model = x_own.shape
    half = model // 2
    normed, inverse = row_norm(x_own[...].astype(F32))
    mine, theirs = both[:tok, :], other[...].astype(F32)
    total = (mine[:, half : half + 1] + theirs[:, half : half + 1]) / model
    total_dot = (mine[:, half + 1 : half + 2] + theirs[:, half + 1 : half + 2]) / model
    first = jnp.where(s == 0, mine[:, :half], theirs[:, :half])
    second = jnp.where(s == 0, theirs[:, :half], mine[:, :half])
    out[:, :half] = (first - inverse * (total + normed[:, :half] * total_dot)).astype(BF16)
    out[:, half:] = (second - inverse * (total + normed[:, half:] * total_dot)).astype(BF16)


def head_norm_t(values):
    width, n = values.shape
    hat, inverse = row_norm(values.reshape(DHEADS, DHD, n), axis=1)
    return hat.reshape(width, n), inverse


def head_back_t(hat, inverse, gradient):
    width, n = hat.shape
    back = norm_back(
        hat.reshape(DHEADS, DHD, n), inverse, gradient.reshape(DHEADS, DHD, n), axis=1
    )
    return back.reshape(width, n)


def mask_kernel(ids, table_in, mask, w_in, *refs):
    vis_row, hidden, pos_vis_out, k_t_out, v_out, wq_t_out, wk_t_out = refs[:7]
    pos_vis, k_t, v, wq_t, wk_t, table, w, sems = refs[7:]
    loads = start(sems, 0, (w_in, w), (table_in, table))
    loads[0].wait()
    wq_t[...] = w[0].T
    wk_t[...] = w[1].T
    stores = start(sems, 2, (wq_t, wq_t_out), (wk_t, wk_t_out))
    loads[1].wait()
    members, pos_dev = table.shape[0], table.shape[1] - 16
    npos, width = members * pos_dev, table.shape[2]
    nvis = vis_row.shape[1]
    pos_all = table[:, :pos_dev, :].reshape(npos, width)
    codes = jnp.sum(table[:, pos_dev:, :].astype(F32), axis=0)
    row = codes[0:1, :nvis] * 32.0 + codes[1:2, :nvis]
    other = jnp.concatenate([row[:, nvis // 2 :], row[:, : nvis // 2]], axis=1)
    vis = jnp.where(ids[0] == 0, row, other).astype(jnp.int32)
    vis_row[...] = vis
    hot = jnp.where(lax.broadcasted_iota(jnp.int32, (npos, nvis), 0) == vis, 1.0, 0.0).astype(BF16)
    hat, _ = row_norm(pos_all.astype(F32) + mask[...].astype(F32))
    low = hat.astype(BF16)
    v[...] = dot(low, w[2]).astype(BF16)
    stores += start(sems, 4, (v, v_out))
    key_hat, _ = head_norm_t(dot_nt(wk_t[...], low))
    k_t[...] = key_hat.astype(BF16)
    stores += start(sems, 5, (k_t, k_t_out))
    pos_vis[...] = dot_tn(hot, pos_all).astype(BF16)
    stores += start(sems, 6, (pos_vis, pos_vis_out))
    hidden[...] = 1.0 - dot_nt(jnp.ones((16, nvis), BF16), hot)[0:1, :]
    finish(stores)


def decoder_kernel(ids, emb_own, emb_other, mask, vis_row, hidden, *refs):
    wk_t_in, w_in, pos_vis_in, pos_own_in, wq_t_in, km_t_in, vm_in, w_out_in, w_pix_in, target_in = refs[:10]
    pred, g_own, g_other, em_ref, ev_ref = refs[10:15]
    wk_t, w, pos_vis, pos_own, wq_t, km_t, vm, w_out, w_pix, target, sems = refs[15:]
    loads = start(
        sems,
        0,
        (pos_vis_in, pos_vis),
        (wk_t_in, wk_t),
        (w_in.at[2], w.at[2]),
        (pos_own_in, pos_own),
        (wq_t_in, wq_t),
        (km_t_in, km_t),
        (vm_in, vm),
        (w_out_in, w_out),
        (w_pix_in, w_pix),
        (target_in, target),
        (w_in.at[0], w.at[0]),
        (w_in.at[1], w.at[1]),
    )
    npos_dev, width = pos_own.shape
    nvis = pos_vis.shape[0]
    group = nvis // 2
    member = ids[2]
    groups = width // 128
    per = 128 // DHD
    rows = per * npos_dev
    factor = DHD**-0.5
    emb = jnp.concatenate([emb_own[...], emb_other[...]])
    loads[0].wait()
    vis_hat, vis_inv = row_norm(emb.astype(F32) + pos_vis[...].astype(F32))
    vis_low = vis_hat.astype(BF16)
    finish(loads[1:3])
    kv_hat, kv_inv = head_norm_t(dot_nt(wk_t[...], vis_low))
    kv_t = kv_hat.astype(BF16)
    vv = dot(vis_low, w[2]).astype(BF16)
    position = lax.broadcasted_iota(jnp.int32, (npos_dev, nvis), 0) + member * npos_dev
    hot = jnp.where(position == vis_row[...], 1.0, 0.0)
    seen = jnp.sum(hot, axis=1, keepdims=True)
    hot_low = hot.astype(BF16)
    filled = dot(hot_low, emb) + (1.0 - seen) * mask[...].astype(F32)
    finish(loads[3:5])
    stream = filled + pos_own[...].astype(F32)
    own_hat, own_inv = row_norm(stream)
    q_t, q_inv = head_norm_t(dot_nt(wq_t[...], own_hat.astype(BF16)))
    q_low = q_t.T.astype(BF16)
    head_mask = (
        lax.broadcasted_iota(jnp.int32, (rows, 128), 0) // npos_dev
        == lax.broadcasted_iota(jnp.int32, (rows, 128), 1) // DHD
    )

    def spread(values):
        return jnp.where(head_mask, jnp.concatenate([values] * per, axis=0), jnp.zeros((), values.dtype))

    def gather(values):
        return jnp.sum(jnp.where(head_mask, values, 0.0).reshape(per, npos_dev, 128), axis=0)

    finish(loads[5:7])
    attended, inv_l = [], []
    for at in range(groups):
        cols = slice(at * 128, (at + 1) * 128)
        q_wide = spread(q_low[:, cols])
        em = jnp.exp2(dot(q_wide, km_t[cols, :]) * (factor * LOG2E)) * hidden[...]
        ev = jnp.exp2(dot(q_wide, kv_t[cols, :]) * (factor * LOG2E))
        l_inv = 1.0 / (jnp.sum(em, axis=1, keepdims=True) + jnp.sum(ev, axis=1, keepdims=True))
        em_low, ev_low = em.astype(BF16), ev.astype(BF16)
        em_ref[at] = em_low
        ev_ref[at] = ev_low
        attended.append(gather((dot(em_low, vm[:, cols]) + dot(ev_low, vv[:, cols])) * l_inv))
        inv_l.append(l_inv)
    att = jnp.concatenate(attended, axis=1)
    finish(loads[7:])
    second = stream + dot(att.astype(BF16), w_out[...])
    final_hat, final_inv = row_norm(second)
    full = dot(final_hat.astype(BF16), w_pix[...])
    pred[...] = full.astype(BF16)
    error = jnp.where(seen > 0, 0.0, full - target[...].astype(F32)).astype(BF16)
    g_second = norm_back(final_hat, final_inv, dot_nt(error, w_pix[...]))
    g_att = dot_nt(g_second.astype(BF16), w_out[...]).astype(BF16)
    product = g_att.astype(F32) * att
    gq, gk_t, gv = [], [], []
    for at in range(groups):
        cols = slice(at * 128, (at + 1) * 128)
        q_wide = spread(q_low[:, cols])
        g_wide = spread(g_att[:, cols])
        delta = jnp.sum(spread(product[:, cols]), axis=1, keepdims=True)
        l_inv = inv_l[at]
        pv = ev_ref[at].astype(F32) * l_inv
        gs_v = (pv * (dot_nt(g_wide, vv[:, cols]) - delta)).astype(BF16)
        pm = em_ref[at].astype(F32) * l_inv
        gs_m = (pm * (dot_nt(g_wide, vm[:, cols]) - delta)).astype(BF16)
        gq.append(gather(dot_nt(gs_m, km_t[cols, :]) + dot_nt(gs_v, kv_t[cols, :])) * factor)
        gk_t.append(dot_tn(q_wide, gs_v) * factor)
        gv.append(dot_tn(pv.astype(BF16), g_wide).astype(BF16))
    gq_back = head_back_t(q_t, q_inv, jnp.concatenate(gq, axis=1).T).T.astype(BF16)
    g_stream_own = g_second + norm_back(own_hat, own_inv, dot_nt(gq_back, w[0]))
    gk_back = head_back_t(kv_hat, kv_inv, jnp.concatenate(gk_t, axis=0)).T.astype(BF16)
    from_keys = dot_nt(gk_back, w[1]) + dot_nt(jnp.concatenate(gv, axis=1), w[2])
    part = norm_back(vis_hat, vis_inv, from_keys) + dot_tn(hot_low, g_stream_own.astype(BF16))
    g_own[...] = part[:group]
    g_other[...] = part[group:].astype(BF16)


def shards(
    patches,
    vis_index,
    input_weight,
    output_weight,
    embed_weight,
    mask_token,
    position_table,
    decoder_input,
    decoder_output,
    pixel_weight,
    target,
):
    section = lax.axis_index("section")
    column = lax.axis_index("mp")
    member = lax.axis_index(("section", "mp"))
    copies = lax.axis_size("dp")
    ids = jnp.stack([section, column, member]).astype(jnp.int32)
    x_own = patches[0]
    tok, model = x_own.shape
    half = model // 2
    slab, dec_width = embed_weight.shape
    width = output_weight.shape[0]
    heads = width // HD
    group = 8 * tok
    nvis = 2 * group
    pos_dev = position_table.shape[0]
    npos = 16 * pos_dev

    def swap(value):
        return lax.ppermute(value, "section", [(0, 1), (1, 0)])

    def shift(value, by):
        return lax.ppermute(value, "mp", [(i, (i + by) % 8) for i in range(8)])

    def exchange(value, axis):
        return lax.all_to_all(value, axis, 0, 0, tiled=True)

    mine = lax.dynamic_slice_in_dim(x_own, section * half, half, 1)
    theirs = lax.dynamic_slice_in_dim(swap(x_own), section * half, half, 1)
    dec_cols = dec_width // copies
    we_t = lax.dynamic_slice_in_dim(embed_weight, lax.axis_index("dp") * dec_cols, dec_cols, 1).T
    we_t = we_t.reshape(dec_cols // 32, 32, slab).transpose(1, 0, 2).reshape(32, -1)
    we_right, we_left = shift(we_t, 1), shift(we_t, -1)
    chunk = jnp.concatenate([mine, theirs])
    right = jnp.concatenate([chunk, we_right], axis=1)
    left = jnp.concatenate([chunk, we_left], axis=1)
    chunks, columns = {0: right}, {0: we_t, -1: we_right, 1: we_left}
    for step in range(1, 5):
        right = shift(right, 1)
        if step < 4:
            left = shift(left, -1)
            right, left = lax.optimization_barrier((right, left))
            chunks[step] = left
            columns[step + 1] = left
        chunks[-step] = right
        columns[-step - 1] = right

    row = jnp.zeros((nvis,), jnp.int32)
    row = lax.dynamic_update_slice_in_dim(row, vis_index[0], member * tok, 0)
    codes = jnp.pad(jnp.stack([row // 32, row % 32]), ((0, 14), (0, dec_width - nvis)))
    table = jnp.concatenate([position_table, codes.astype(BF16)])
    table, _ = lax.optimization_barrier((table, chunks[-3]))
    table = lax.all_gather(table, ("section", "mp"), axis=0, tiled=False)

    w_in = input_weight.transpose(1, 0, 2)
    held = sds((half, 3 * width), BF16)
    ordered = [chunks[offset] for offset in OFFSETS]
    (wp_parts,) = call(
        fold_kernel,
        [sds((copies, dec_cols, width), BF16)],
        ids,
        *[columns[offset] for offset in OFFSETS],
        output_weight,
        scratch=[sds((dec_cols, half), BF16), sds(output_weight.shape, BF16)],
        far=tuple(range(1, 10)),
        copies=1 + 8 * (dec_cols // 32),
    )
    wpt_own = exchange(wp_parts, "dp").reshape(dec_width, width)
    ids_late, _ = lax.optimization_barrier((ids, wp_parts))
    p_own, xp_own, xp_send = call(
        project_kernel,
        [
            sds((nvis + 16, 3 * width + 128), BF16),
            sds((group, dec_width), F32),
            sds((group, dec_width), BF16),
        ],
        ids_late,
        embed_weight,
        *ordered,
        w_in,
        scratch=[
            sds((8, 2 * tok, half), BF16),
            sds((nvis + 16, half), BF16),
            held,
            sds((nvis, slab), BF16),
        ],
        far=tuple(range(2, 11)),
        copies=20,
    )
    p_other = swap(p_own)
    xp_other = swap(xp_send)
    wpt_other = swap(wpt_own)
    saved = [
        sds((heads, nvis, nvis), BF16),
        sds((nvis, width), BF16),
        sds((nvis, width), BF16),
        sds((nvis, width), BF16),
        sds((nvis, 128), F32),
    ]
    (att,) = call(attend_kernel, [sds((group, width), BF16)], ids, p_own, p_other, limit=32)
    embed_part, wpt = call(
        embed_kernel,
        [sds((8, tok, dec_width), BF16), sds((dec_width, width), BF16)],
        ids,
        att,
        wpt_own,
        wpt_other,
        xp_own,
        xp_other,
    )

    w_dec = decoder_input.transpose(1, 0, 2)
    mask_row = mask_token.reshape(1, dec_width)
    ids_saved, _ = lax.optimization_barrier((ids, embed_part))
    e_enc, q_enc, k_enc, v_enc, aux = call(
        save_kernel,
        saved,
        ids_saved,
        p_own,
        p_other,
        scratch=saved,
        far_out=(0, 1, 2, 3, 4),
        copies=heads + 4,
    )
    embed_parts, _ = lax.optimization_barrier((exchange(embed_part, "mp"), aux))
    (embed_sum,) = call(sum_kernel, [sds((8, tok, dec_width), BF16)], ids, embed_parts, limit=16)
    table, _ = lax.optimization_barrier((table, embed_sum))
    prepared = [
        sds((nvis, dec_width), BF16),
        sds((dec_width, npos), BF16),
        sds((npos, dec_width), BF16),
        sds((dec_width, dec_width), BF16),
        sds((dec_width, dec_width), BF16),
    ]
    vis_row, hidden, pos_vis, km_t, vm, wq_t, wk_t = call(
        mask_kernel,
        [sds((1, nvis), jnp.int32), sds((1, npos), F32)] + prepared,
        ids,
        table,
        mask_row,
        w_dec,
        scratch=prepared + [sds(table.shape, BF16), sds(w_dec.shape, BF16)],
        far=(1, 3),
        far_out=(2, 3, 4, 5, 6),
        copies=7,
    )
    emb_own = exchange(embed_sum, "mp").reshape(group, dec_width)
    emb_own, _ = lax.optimization_barrier((emb_own, hidden))
    emb_other = swap(emb_own)

    groups = dec_width // 128
    rows = (128 // DHD) * pos_dev
    prediction, g_own, g_send = call(
        decoder_kernel,
        [
            sds((pos_dev, target.shape[2]), BF16),
            sds((group, dec_width), F32),
            sds((group, dec_width), BF16),
        ],
        ids,
        emb_own,
        emb_other,
        mask_row,
        vis_row,
        hidden,
        wk_t,
        w_dec,
        pos_vis,
        position_table,
        wq_t,
        km_t,
        vm,
        decoder_output,
        pixel_weight,
        target[0],
        scratch=[sds((groups, rows, npos), BF16), sds((groups, rows, nvis), BF16)]
        + [sds(wk_t.shape, BF16), sds(w_dec.shape, BF16), sds(pos_vis.shape, BF16)]
        + [sds(position_table.shape, BF16), sds(wq_t.shape, BF16), sds(km_t.shape, BF16), sds(vm.shape, BF16)]
        + [sds(decoder_output.shape, BF16), sds(pixel_weight.shape, BF16), sds(target.shape[1:], BF16)],
        far=tuple(range(6, 16)),
        copies=12,
    )
    g_part = (g_own + swap(g_send).astype(F32)).astype(BF16).reshape(8, tok, dec_width)
    (g_sum,) = call(sum_kernel, [sds((8, tok, dec_width), BF16)], ids, exchange(g_part, "mp"), limit=16)
    ge_own = exchange(g_sum, "mp").reshape(group, dec_width)
    ge_other = swap(ge_own)

    right, left, parts = call(
        encoder_back_kernel,
        [
            sds((tok, half + 128), BF16),
            sds((tok, half + 128), BF16),
            sds((8, 2 * tok, half + 128), BF16),
        ],
        ids,
        ge_own,
        ge_other,
        embed_weight,
        wpt,
        e_enc,
        q_enc,
        k_enc,
        v_enc,
        aux,
        w_in,
        *ordered,
        scratch=[sds((dec_width, width), BF16)]
        + saved
        + [sds((2, 8, tok, half), BF16), held]
        + [sds((nvis, 3 * width), BF16), sds((8, 2 * tok, half + 128), BF16)],
        far=tuple(range(4, 19)),
        far_out=(2,),
        copies=30,
    )

    def part(offset):
        return lax.dynamic_index_in_dim(parts, (column + offset) % 8, 0, False).astype(F32)

    right, left = lax.optimization_barrier((shift(right, 1), shift(left, -1)))
    ahead, behind = part(3), part(-3)
    right = jnp.concatenate([right.astype(F32) + ahead[:tok], ahead[tok:]]).astype(BF16)
    left = jnp.concatenate([behind[:tok], left.astype(F32) + behind[tok:]]).astype(BF16)
    for offset in (2, 1):
        right, left = lax.optimization_barrier((shift(right, 1), shift(left, -1)))
        right = (right.astype(F32) + part(offset)).astype(BF16)
        left = (left.astype(F32) + part(-offset)).astype(BF16)
    total = shift(right, 1).astype(F32) + shift(left, -1).astype(F32) + part(0)
    (patch_grad,) = call(
        final_kernel,
        [sds((tok, model), BF16)],
        ids,
        x_own,
        total,
        swap(total[tok:].astype(BF16)),
        limit=16,
    )
    return (prediction[None], patch_grad[None])


def solution(mesh):
    group = ("section", "mp")
    in_specs = (
        P("dp", group, None),
        P("dp", group),
        P("section", None, "mp"),
        P("mp", "section"),
        P(group, None),
        P(),
        P(group, None),
        P(),
        P(),
        P(),
        P("dp", group, None),
    )
    out_specs = (P("dp", group, None), P("dp", group, None))
    return jax.shard_map(shards, mesh=mesh, in_specs=in_specs, out_specs=out_specs, check_vma=False)
```

```python
import math

import jax
import jax.numpy as jnp
from jax import lax
from jax.experimental import pallas as pl
from jax.experimental.pallas import tpu as pltpu
from jax.sharding import PartitionSpec as P

HD = 128
DHEADS = 16
DHD = 32
EPSILON = 1e-06
LOG2E = math.log2(math.e)
F32 = jnp.float32
BF16 = jnp.bfloat16
OFFSETS = (0, -1, 1, -2, 2, -3, 3, -4)


def dot(a, b):
    return lax.dot_general(a, b, (((1,), (0,)), ((), ())), preferred_element_type=F32)


def dot_nt(a, b):
    return lax.dot_general(a, b, (((1,), (1,)), ((), ())), preferred_element_type=F32)


def dot_tn(a, b):
    return lax.dot_general(a, b, (((0,), (0,)), ((), ())), preferred_element_type=F32)


def row_norm(values, axis=-1):
    centre = jnp.mean(values, axis=axis, keepdims=True)
    centered = values - centre
    inverse = lax.rsqrt(jnp.mean(centered * centered, axis=axis, keepdims=True) + EPSILON)
    return centered * inverse, inverse


def norm_back(normed, inverse, gradient, axis=-1):
    mean_grad = jnp.mean(gradient, axis=axis, keepdims=True)
    mean_dot = jnp.mean(gradient * normed, axis=axis, keepdims=True)
    return inverse * (gradient - mean_grad - normed * mean_dot)


def lanes(columns, rows):
    lane = lax.broadcasted_iota(jnp.int32, (rows, 128), 1)
    out = jnp.zeros((rows, 128), F32)
    for at, column in enumerate(columns):
        out = jnp.where(lane == at, column, out)
    return out


def call(kernel, outs, *args, scratch=(), far=(), far_out=(), copies=0, limit=58):
    specs = [pl.BlockSpec(memory_space=pltpu.SMEM)]
    for at in range(1, len(args)):
        specs.append(pl.BlockSpec(memory_space=pl.ANY if at in far else pltpu.VMEM))
    out_specs = [
        pl.BlockSpec(memory_space=pl.ANY if at in far_out else pltpu.VMEM) for at in range(len(outs))
    ]
    scratch = [pltpu.VMEM(shape.shape, shape.dtype) for shape in scratch]
    if copies:
        scratch.append(pltpu.SemaphoreType.DMA((copies,)))
    return pl.pallas_call(
        kernel,
        out_shape=tuple(outs),
        in_specs=specs,
        out_specs=tuple(out_specs),
        scratch_shapes=scratch,
        compiler_params=pltpu.CompilerParams(vmem_limit_bytes=limit * 2**20),
    )(*args)


def start(sems, first, *pairs):
    copies = [
        pltpu.make_async_copy(source, target, sems.at[first + at]) for at, (source, target) in enumerate(pairs)
    ]
    for copy in copies:
        copy.start()
    return copies


def finish(copies):
    for copy in copies:
        copy.wait()


def sds(shape, dtype):
    return jax.ShapeDtypeStruct(shape, dtype)


def weight_copies(w, held, pieces):
    _, rows, width = w.shape
    size = rows // pieces
    return [
        (w.at[at, pl.ds(piece * size, size)], held.at[pl.ds(piece * size, size), pl.ds(at * width, width)])
        for piece in range(pieces)
        for at in range(3)
    ]


def split3(values):
    first = values.astype(BF16).astype(F32)
    second = (values - first).astype(BF16).astype(F32)
    return [first, second, values - first - second]


def centre_rows(value):
    wide = value.astype(F32)
    centre = jnp.mean(wide, axis=1, keepdims=True)
    centered = wide - centre
    spread = jnp.sum(centered * centered, axis=1, keepdims=True)
    return centered.astype(BF16), lanes(split3(centre) + split3(spread), value.shape[0]).astype(BF16)


def place_rows(rows, at, target, cols=slice(None)):
    tok = rows.shape[0] // 2
    row = pl.multiple_of(at * tok, tok)
    target[pl.ds(row, tok), cols] = rows[:tok]
    target[pl.ds(row + 8 * tok, tok), cols] = rows[tok:]


def fold_kernel(ids, *refs):
    columns, wo_in, out = refs[:8], refs[8], refs[9]
    wt, wo, sems = refs[10:]
    half = wo.shape[1]
    slab = half // 8
    pieces = wt.shape[0] // 32
    loads = start(sems, 0, (wo_in, wo))
    for index, (source, offset) in enumerate(zip(columns, OFFSETS)):
        column = pl.multiple_of(lax.rem(ids[1] + offset + 8, 8) * slab, 128)
        base = source.shape[1] - pieces * slab
        for piece in range(pieces):
            target = wt.at[pl.ds(piece * 32, 32), pl.ds(column, slab)]
            source_part = source.at[:, pl.ds(base + piece * slab, slab)]
            loads += start(sems, 1 + index * pieces + piece, (source_part, target))
    finish(loads)
    total = dot_nt(wt[...], wo[...]).astype(BF16)
    for at in range(out.shape[0]):
        out[at] = total


def centre_rows(value):
    wide = value.astype(F32)
    centre = jnp.mean(wide, axis=1, keepdims=True)
    centered = wide - centre
    spread = jnp.sum(centered * centered, axis=1, keepdims=True)
    return centered.astype(BF16), lanes(split3(centre) + split3(spread), value.shape[0]).astype(BF16)


def place_rows(rows, at, target, cols=slice(None)):
    tok = rows.shape[0] // 2
    row = pl.multiple_of(at * tok, tok)
    target[pl.ds(row, tok), cols] = rows[:tok]
    target[pl.ds(row + 8 * tok, tok), cols] = rows[tok:]


def project_kernel(ids, we, *refs):
    chunks, w = refs[:8], refs[8]
    p_out, xp_own, xp_send = refs[9:12]
    held_chunks, xc, held, xs, sems = refs[12:]
    half, width3 = held.shape
    slab = half // 8
    rows2 = held_chunks.shape[1]
    rows = 8 * rows2
    m = ids[1]
    arrivals = start(
        sems, 0, *[(chunk.at[:, pl.ds(0, half)], held_chunks.at[at]) for at, chunk in enumerate(chunks)]
    )
    w_loads = start(sems, 8, *weight_copies(w, held, 4))
    own_column = pl.multiple_of(m * slab, 128)
    for index, offset in enumerate(OFFSETS):
        at = lax.rem(m + offset + 8, 8)
        arrivals[index].wait()
        low, moments = centre_rows(held_chunks[index])
        place_rows(low, at, xc)
        place_rows(moments, at, p_out, slice(width3, width3 + 128))
        place_rows(held_chunks[index, :, pl.ds(own_column, slab)], at, xs)
    xc[rows:, :] = jnp.ones((16, half), BF16)
    p_out[rows:, width3:] = jnp.zeros((16, 128), BF16)
    xp = dot(xs[...], we[...])
    xp_own[...] = xp[: rows // 2]
    xp_send[...] = xp[rows // 2 :].astype(BF16)
    quarter = half // 4
    product = jnp.zeros((rows + 16, width3), F32)
    for piece in range(4):
        finish(w_loads[piece * 3 : piece * 3 + 3])
        part = slice(piece * quarter, (piece + 1) * quarter)
        product = product + dot(xc[:, part], held[part, :])
    p_out[:, :width3] = product.astype(BF16)


def scene_mixture(p_own, p_other):
    rows = p_own.shape[0] - 16
    group = rows // 2
    width3 = p_own.shape[1] - 128
    model = 16 * (width3 // 3)

    def moments(p):
        stats = p[:rows, width3:].astype(F32)
        parts = [stats[:, at : at + 1] for at in range(6)]
        return parts[0] + parts[1] + parts[2], parts[3] + parts[4] + parts[5]

    def exchanged(values):
        return jnp.concatenate([values[group:], values[:group]])

    m_own, s_own = moments(p_own)
    m_other, s_other = [exchanged(value) for value in moments(p_other)]
    gap = (m_own - m_other) * 0.5
    centre = (m_own + m_other) * 0.5
    inverse = lax.rsqrt((s_own + s_other) / model + gap * gap + EPSILON)
    slope = p_own[rows : rows + 1, :width3].astype(F32) - p_other[rows : rows + 1, :width3].astype(F32)

    def mixture(at, count):
        cols = slice(at * HD, (at + 1) * HD)
        other = p_other[group : group + min(count, group), cols]
        if count > group:
            other = jnp.concatenate([other, p_other[: count - group, cols]])
        total = p_own[:count, cols].astype(F32) + other.astype(F32) + gap[:count] * slope[:, cols]
        return inverse[:count] * total

    return centre, inverse, mixture


def attend_kernel(ids, p_own, p_other, att):
    rows = p_own.shape[0] - 16
    heads = att.shape[1] // HD
    _, _, mixture = scene_mixture(p_own, p_other)
    factor = LOG2E * HD**-0.5
    for head in range(heads):
        q_low = row_norm(mixture(head, rows // 2))[0].astype(BF16)
        k_low = row_norm(mixture(heads + head, rows))[0].astype(BF16)
        v_low = mixture(2 * heads + head, rows).astype(BF16)
        e = jnp.exp2(dot_nt(q_low, k_low) * factor)
        l_inv = 1.0 / jnp.sum(e, axis=1, keepdims=True)
        att[:, head * HD : (head + 1) * HD] = (dot(e.astype(BF16), v_low) * l_inv).astype(BF16)


def save_kernel(ids, p_own, p_other, w_in, *refs):
    saved, turned = refs[:5], refs[5:7]
    e_out, q_out, k_out, v_out, aux, w, w_t, sems = refs[7:]
    loads = start(sems, 8, (w_in.at[0], w.at[0]), (w_in.at[1], w.at[1]))
    rows, width = q_out.shape
    heads = width // HD
    centre, inverse, mixture = scene_mixture(p_own, p_other)
    inv_q, inv_k, inv_l = [], [], []
    factor = LOG2E * HD**-0.5
    stores = []
    for head in range(heads):
        cols = slice(head * HD, (head + 1) * HD)
        q_hat, q_inv = row_norm(mixture(head, rows))
        k_hat, k_inv = row_norm(mixture(heads + head, rows))
        q_low, k_low = q_hat.astype(BF16), k_hat.astype(BF16)
        e = jnp.exp2(dot_nt(q_low, k_low) * factor)
        e_out[head] = e.astype(BF16)
        stores += start(sems, head, (e_out.at[head], saved[0].at[head]))
        q_out[:, cols] = q_low
        k_out[:, cols] = k_low
        v_out[:, cols] = mixture(2 * heads + head, rows).astype(BF16)
        inv_q.append(q_inv)
        inv_k.append(k_inv)
        inv_l.append(1.0 / jnp.sum(e, axis=1, keepdims=True))
    aux[...] = lanes([centre, inverse] + inv_l + inv_q + inv_k, rows)
    stores += start(sems, heads, (q_out, saved[1]), (k_out, saved[2]), (v_out, saved[3]), (aux, saved[4]))
    finish(loads)
    for at in range(2):
        w_t[at] = w[at].T
    stores += start(sems, 10, (w_t.at[0], turned[0]), (w_t.at[1], turned[1]))
    finish(stores)


def embed_kernel(ids, att, wpt_own, wpt_other, xp_own, xp_other, out, wpt):
    total = (wpt_own[...].astype(F32) + wpt_other[...].astype(F32)).astype(BF16)
    wpt[...] = total
    part = dot_nt(att[...], total) + xp_own[...] + xp_other[...].astype(F32)
    out[...] = part.astype(BF16).reshape(out.shape)


def sum_kernel(ids, parts, out):
    total = jnp.sum(parts[...].astype(F32), axis=0).astype(BF16)
    for at in range(out.shape[0]):
        out[at] = total


def encoder_back_kernel(ids, g_own, g_other, we, *refs):
    sources, w, chunks = refs[:6], refs[6], refs[7:15]
    right, left, parts_out = refs[15:18]
    wpt, e_in, q_in, k_in, v_in, aux, x_in, held, gmix, out, sems = refs[18:]
    rows, width = q_in.shape
    heads = width // HD
    half = held.shape[0]
    slab = half // 8
    tok = x_in.shape[2]
    m = ids[1]
    loads = start(sems, 0, *zip(sources, (wpt, e_in, q_in, k_in, v_in, aux)))
    w_loads = start(sems, 6, *weight_copies(w, held, 1))
    for index, offset in enumerate(OFFSETS):
        at = lax.rem(m + offset + 8, 8)
        for rel in range(2):
            rows_of = chunks[index].at[pl.ds(rel * tok, tok), pl.ds(0, half)]
            w_loads += start(sems, 10 + 2 * index + rel, (rows_of, x_in.at[rel, at]))
    factor = HD**-0.5
    gemb = jnp.concatenate([g_own[...], g_other[...]])
    glayer = dot_nt(gemb, we[...])
    loads[0].wait()
    gatt = dot(gemb, wpt[...]).astype(BF16)
    finish(loads[1:])
    for head in range(heads):
        cols = slice(head * HD, (head + 1) * HD)
        g_head = gatt[:, cols]
        q_low, k_low, v_low = q_in[:, cols], k_in[:, cols], v_in[:, cols]
        l_inv = aux[:, 2 + head : 3 + head]
        q_inv = aux[:, 2 + heads + head : 3 + heads + head]
        k_inv = aux[:, 2 + 2 * heads + head : 3 + 2 * heads + head]
        p = e_in[head].astype(F32) * l_inv
        gp = dot_nt(g_head, v_low)
        delta = jnp.sum(p * gp, axis=1, keepdims=True)
        gs = (p * (gp - delta)).astype(BF16)
        gq = dot(gs, k_low) * factor
        gk = dot_tn(gs, q_low) * factor
        gv = dot_tn(p.astype(BF16), g_head)
        gmix[:, cols] = norm_back(q_low.astype(F32), q_inv, gq).astype(BF16)
        gmix[:, width + head * HD : width + (head + 1) * HD] = norm_back(k_low.astype(F32), k_inv, gk).astype(BF16)
        gmix[:, 2 * width + head * HD : 2 * width + (head + 1) * HD] = gv.astype(BF16)
    finish(w_loads)
    centre, inverse = aux[:, 0:1], aux[:, 1:2]
    total = jnp.zeros((rows, 1), F32)
    total_dot = jnp.zeros((rows, 1), F32)
    stores = []
    for block in range(4):
        cols = slice(2 * block * slab, 2 * (block + 1) * slab)
        g = dot_nt(gmix[...], held[cols, :])
        normed = (x_in[:, :, :, cols].reshape(rows, 2 * slab).astype(F32) - centre) * inverse
        total = total + jnp.sum(g, axis=1, keepdims=True)
        total_dot = total_dot + jnp.sum(g * normed, axis=1, keepdims=True)
        mine = [glayer * jnp.where(2 * block + at == m, 1.0, 0.0) for at in range(2)]
        value = (g * inverse + jnp.concatenate(mine, axis=1)).astype(BF16).reshape(2, 8, tok, 2 * slab)
        out[:, :tok, cols] = value[0]
        out[:, tok:, cols] = value[1]
        span = pl.ds(cols.start, 2 * slab)
        stores += start(sems, 26 + block, (out.at[:, :, span], parts_out.at[:, :, span]))
    sums = lanes((total, total_dot), rows).astype(BF16).reshape(2, 8, tok, 128)
    out[:, :tok, half:] = sums[0]
    out[:, tok:, half:] = sums[1]
    span = pl.ds(half, 128)
    stores += start(sems, 9, (out.at[:, :, span], parts_out.at[:, :, span]))
    right[...] = out[lax.rem(m + 4, 8), :tok]
    left[...] = out[lax.rem(m + 4, 8), tok:]
    finish(stores)


def final_kernel(ids, x_own, both, other, out):
    s = ids[0]
    tok, model = x_own.shape
    half = model // 2
    normed, inverse = row_norm(x_own[...].astype(F32))
    mine, theirs = both[:tok, :], other[...].astype(F32)
    total = (mine[:, half : half + 1] + theirs[:, half : half + 1]) / model
    total_dot = (mine[:, half + 1 : half + 2] + theirs[:, half + 1 : half + 2]) / model
    first = jnp.where(s == 0, mine[:, :half], theirs[:, :half])
    second = jnp.where(s == 0, theirs[:, :half], mine[:, :half])
    out[:, :half] = (first - inverse * (total + normed[:, :half] * total_dot)).astype(BF16)
    out[:, half:] = (second - inverse * (total + normed[:, half:] * total_dot)).astype(BF16)


def head_norm_t(values):
    width, n = values.shape
    hat, inverse = row_norm(values.reshape(DHEADS, DHD, n), axis=1)
    return hat.reshape(width, n), inverse


def head_back_t(hat, inverse, gradient):
    width, n = hat.shape
    back = norm_back(
        hat.reshape(DHEADS, DHD, n), inverse, gradient.reshape(DHEADS, DHD, n), axis=1
    )
    return back.reshape(width, n)


def mask_kernel(ids, table_in, w_in, wk_t_in, vis_row, hidden, mask_out, pos_vis, k_t, v, table, w, wk_t, sems):
    loads = start(sems, 0, (table_in, table), (w_in.at[2], w), (wk_t_in, wk_t))
    loads[0].wait()
    members, pos_dev = table.shape[0], table.shape[1] - 16
    npos, width = members * pos_dev, table.shape[2]
    nvis = vis_row.shape[1]
    pos_all = table[:, :pos_dev, :].reshape(npos, width)
    codes = jnp.sum(table[:, pos_dev:, :].astype(F32), axis=0)
    row = codes[0:1, :nvis] * 32.0 + codes[1:2, :nvis]
    other = jnp.concatenate([row[:, nvis // 2 :], row[:, : nvis // 2]], axis=1)
    vis = jnp.where(ids[0] == 0, row, other).astype(jnp.int32)
    vis_row[...] = vis
    hot = jnp.where(lax.broadcasted_iota(jnp.int32, (npos, nvis), 0) == vis, 1.0, 0.0).astype(BF16)
    mask = table[0, pos_dev:, :].astype(F32)[2:3, :]
    mask_out[...] = mask
    hat, _ = row_norm(pos_all.astype(F32) + mask)
    low = hat.astype(BF16)
    finish(loads[1:])
    key_hat, _ = head_norm_t(dot_nt(wk_t[...], low))
    k_t[...] = key_hat.astype(BF16)
    v[...] = dot(low, w[...]).astype(BF16)
    pos_vis[...] = dot_tn(hot, pos_all).astype(BF16)
    hidden[...] = 1.0 - dot_nt(jnp.ones((16, nvis), BF16), hot)[0:1, :]


def decoder_kernel(ids, emb_own, emb_other, mask, vis_row, hidden, *refs):
    wk_t_in, w_in, pos_vis_in, pos_own_in, wq_t_in, km_t_in, vm_in, w_out_in, w_pix_in, target_in = refs[:10]
    pred, g_own, g_other, em_ref, ev_ref = refs[10:15]
    wk_t, w, pos_vis, pos_own, wq_t, km_t, vm, w_out, w_pix, target, sems = refs[15:]
    loads = start(
        sems,
        0,
        (pos_vis_in, pos_vis),
        (wk_t_in, wk_t),
        (w_in.at[2], w.at[2]),
        (pos_own_in, pos_own),
        (wq_t_in, wq_t),
        (km_t_in, km_t),
        (vm_in, vm),
        (w_out_in, w_out),
        (w_pix_in, w_pix),
        (target_in, target),
        (w_in.at[0], w.at[0]),
        (w_in.at[1], w.at[1]),
    )
    npos_dev, width = pos_own.shape
    nvis = pos_vis.shape[0]
    group = nvis // 2
    member = ids[2]
    groups = width // 128
    per = 128 // DHD
    rows = per * npos_dev
    factor = DHD**-0.5
    emb = jnp.concatenate([emb_own[...], emb_other[...]])
    loads[0].wait()
    vis_hat, vis_inv = row_norm(emb.astype(F32) + pos_vis[...].astype(F32))
    vis_low = vis_hat.astype(BF16)
    finish(loads[1:3])
    kv_hat, kv_inv = head_norm_t(dot_nt(wk_t[...], vis_low))
    kv_t = kv_hat.astype(BF16)
    vv = dot(vis_low, w[2]).astype(BF16)
    position = lax.broadcasted_iota(jnp.int32, (npos_dev, nvis), 0) + member * npos_dev
    hot = jnp.where(position == vis_row[...], 1.0, 0.0)
    seen = jnp.sum(hot, axis=1, keepdims=True)
    hot_low = hot.astype(BF16)
    filled = dot(hot_low, emb) + (1.0 - seen) * mask[...].astype(F32)
    finish(loads[3:5])
    stream = filled + pos_own[...].astype(F32)
    own_hat, own_inv = row_norm(stream)
    q_t, q_inv = head_norm_t(dot_nt(wq_t[...], own_hat.astype(BF16)))
    q_low = q_t.T.astype(BF16)
    head_mask = (
        lax.broadcasted_iota(jnp.int32, (rows, 128), 0) // npos_dev
        == lax.broadcasted_iota(jnp.int32, (rows, 128), 1) // DHD
    )

    def spread(values):
        return jnp.where(head_mask, jnp.concatenate([values] * per, axis=0), jnp.zeros((), values.dtype))

    def gather(values):
        return jnp.sum(jnp.where(head_mask, values, 0.0).reshape(per, npos_dev, 128), axis=0)

    finish(loads[5:7])
    attended, inv_l = [], []
    for at in range(groups):
        cols = slice(at * 128, (at + 1) * 128)
        q_wide = spread(q_low[:, cols])
        em = jnp.exp2(dot(q_wide, km_t[cols, :]) * (factor * LOG2E)) * hidden[...]
        ev = jnp.exp2(dot(q_wide, kv_t[cols, :]) * (factor * LOG2E))
        l_inv = 1.0 / (jnp.sum(em, axis=1, keepdims=True) + jnp.sum(ev, axis=1, keepdims=True))
        em_low, ev_low = em.astype(BF16), ev.astype(BF16)
        em_ref[at] = em_low
        ev_ref[at] = ev_low
        attended.append(gather((dot(em_low, vm[:, cols]) + dot(ev_low, vv[:, cols])) * l_inv))
        inv_l.append(l_inv)
    att = jnp.concatenate(attended, axis=1)
    finish(loads[7:])
    second = stream + dot(att.astype(BF16), w_out[...])
    final_hat, final_inv = row_norm(second)
    full = dot(final_hat.astype(BF16), w_pix[...])
    pred[...] = full.astype(BF16)
    error = jnp.where(seen > 0, 0.0, full - target[...].astype(F32)).astype(BF16)
    g_second = norm_back(final_hat, final_inv, dot_nt(error, w_pix[...]))
    g_att = dot_nt(g_second.astype(BF16), w_out[...]).astype(BF16)
    product = g_att.astype(F32) * att
    gq, gk_t, gv = [], [], []
    for at in range(groups):
        cols = slice(at * 128, (at + 1) * 128)
        q_wide = spread(q_low[:, cols])
        g_wide = spread(g_att[:, cols])
        delta = jnp.sum(spread(product[:, cols]), axis=1, keepdims=True)
        l_inv = inv_l[at]
        pv = ev_ref[at].astype(F32) * l_inv
        gs_v = (pv * (dot_nt(g_wide, vv[:, cols]) - delta)).astype(BF16)
        pm = em_ref[at].astype(F32) * l_inv
        gs_m = (pm * (dot_nt(g_wide, vm[:, cols]) - delta)).astype(BF16)
        gq.append(gather(dot_nt(gs_m, km_t[cols, :]) + dot_nt(gs_v, kv_t[cols, :])) * factor)
        gk_t.append(dot_tn(q_wide, gs_v) * factor)
        gv.append(dot_tn(pv.astype(BF16), g_wide).astype(BF16))
    gq_back = head_back_t(q_t, q_inv, jnp.concatenate(gq, axis=1).T).T.astype(BF16)
    g_stream_own = g_second + norm_back(own_hat, own_inv, dot_nt(gq_back, w[0]))
    gk_back = head_back_t(kv_hat, kv_inv, jnp.concatenate(gk_t, axis=0)).T.astype(BF16)
    from_keys = dot_nt(gk_back, w[1]) + dot_nt(jnp.concatenate(gv, axis=1), w[2])
    part = norm_back(vis_hat, vis_inv, from_keys) + dot_tn(hot_low, g_stream_own.astype(BF16))
    g_own[...] = part[:group]
    g_other[...] = part[group:].astype(BF16)


def shards(
    patches,
    vis_index,
    input_weight,
    output_weight,
    embed_weight,
    mask_token,
    position_table,
    decoder_input,
    decoder_output,
    pixel_weight,
    target,
):
    section = lax.axis_index("section")
    column = lax.axis_index("mp")
    member = lax.axis_index(("section", "mp"))
    copies = lax.axis_size("dp")
    ids = jnp.stack([section, column, member]).astype(jnp.int32)
    x_own = patches[0]
    tok, model = x_own.shape
    half = model // 2
    slab, dec_width = embed_weight.shape
    width = output_weight.shape[0]
    heads = width // HD
    group = 8 * tok
    nvis = 2 * group
    pos_dev = position_table.shape[0]
    npos = 16 * pos_dev

    def swap(value):
        return lax.ppermute(value, "section", [(0, 1), (1, 0)])

    def shift(value, by):
        return lax.ppermute(value, "mp", [(i, (i + by) % 8) for i in range(8)])

    def exchange(value, axis):
        return lax.all_to_all(value, axis, 0, 0, tiled=True)

    mine = lax.dynamic_slice_in_dim(x_own, section * half, half, 1)
    theirs = lax.dynamic_slice_in_dim(swap(x_own), section * half, half, 1)
    dec_cols = dec_width // copies
    we_t = lax.dynamic_slice_in_dim(embed_weight, lax.axis_index("dp") * dec_cols, dec_cols, 1).T
    we_t = we_t.reshape(dec_cols // 32, 32, slab).transpose(1, 0, 2).reshape(32, -1)
    we_right, we_left = shift(we_t, 1), shift(we_t, -1)
    chunk = jnp.concatenate([mine, theirs])
    right = jnp.concatenate([chunk, we_right], axis=1)
    left = jnp.concatenate([chunk, we_left], axis=1)
    chunks, columns = {0: right}, {0: we_t, -1: we_right, 1: we_left}
    for step in range(1, 5):
        right = shift(right, 1)
        if step < 4:
            left = shift(left, -1)
            right, left = lax.optimization_barrier((right, left))
            chunks[step] = left
            columns[step + 1] = left
        chunks[-step] = right
        columns[-step - 1] = right

    row = jnp.zeros((nvis,), jnp.int32)
    row = lax.dynamic_update_slice_in_dim(row, vis_index[0], member * tok, 0)
    codes = jnp.pad(jnp.stack([row // 32, row % 32]).astype(BF16), ((0, 0), (0, dec_width - nvis)))
    codes = jnp.concatenate([codes, mask_token[None], jnp.zeros((13, dec_width), BF16)])
    table = jnp.concatenate([position_table, codes])
    table, _ = lax.optimization_barrier((table, chunks[-3]))
    table = lax.all_gather(table, ("section", "mp"), axis=0, tiled=False)

    w_in = input_weight.transpose(1, 0, 2)
    held = sds((half, 3 * width), BF16)
    ordered = [chunks[offset] for offset in OFFSETS]
    (wp_parts,) = call(
        fold_kernel,
        [sds((copies, dec_cols, width), BF16)],
        ids,
        *[columns[offset] for offset in OFFSETS],
        output_weight,
        scratch=[sds((dec_cols, half), BF16), sds(output_weight.shape, BF16)],
        far=tuple(range(1, 10)),
        copies=1 + 8 * (dec_cols // 32),
    )
    wpt_own = exchange(wp_parts, "dp").reshape(dec_width, width)
    ids_late, _ = lax.optimization_barrier((ids, wp_parts))
    p_own, xp_own, xp_send = call(
        project_kernel,
        [
            sds((nvis + 16, 3 * width + 128), BF16),
            sds((group, dec_width), F32),
            sds((group, dec_width), BF16),
        ],
        ids_late,
        embed_weight,
        *ordered,
        w_in,
        scratch=[
            sds((8, 2 * tok, half), BF16),
            sds((nvis + 16, half), BF16),
            held,
            sds((nvis, slab), BF16),
        ],
        far=tuple(range(2, 11)),
        copies=20,
    )
    p_other = swap(p_own)
    xp_other = swap(xp_send)
    wpt_other = swap(wpt_own)
    saved = [
        sds((heads, nvis, nvis), BF16),
        sds((nvis, width), BF16),
        sds((nvis, width), BF16),
        sds((nvis, width), BF16),
        sds((nvis, 128), F32),
    ]
    (att,) = call(attend_kernel, [sds((group, width), BF16)], ids, p_own, p_other, limit=32)
    embed_part, wpt = call(
        embed_kernel,
        [sds((8, tok, dec_width), BF16), sds((dec_width, width), BF16)],
        ids,
        att,
        wpt_own,
        wpt_other,
        xp_own,
        xp_other,
    )

    w_dec = decoder_input.transpose(1, 0, 2)
    ids_saved, _ = lax.optimization_barrier((ids, embed_part))
    turned = sds((dec_width, dec_width), BF16)
    e_enc, q_enc, k_enc, v_enc, aux, wq_t, wk_t = call(
        save_kernel,
        saved + [turned, turned],
        ids_saved,
        p_own,
        p_other,
        w_dec,
        scratch=saved + [sds((2, dec_width, dec_width), BF16), sds((2, dec_width, dec_width), BF16)],
        far=(3,),
        far_out=(0, 1, 2, 3, 4, 5, 6),
        copies=12,
    )
    embed_parts, _ = lax.optimization_barrier((exchange(embed_part, "mp"), aux))
    (embed_sum,) = call(sum_kernel, [sds((8, tok, dec_width), BF16)], ids, embed_parts, limit=16)
    table, _ = lax.optimization_barrier((table, embed_sum))
    vis_row, hidden, mask_row, pos_vis, km_t, vm = call(
        mask_kernel,
        [
            sds((1, nvis), jnp.int32),
            sds((1, npos), F32),
            sds((1, dec_width), F32),
            sds((nvis, dec_width), BF16),
            sds((dec_width, npos), BF16),
            sds((npos, dec_width), BF16),
        ],
        ids,
        table,
        w_dec,
        wk_t,
        scratch=[sds(table.shape, BF16), turned, turned],
        far=(1, 2, 3),
        copies=3,
    )
    emb_own = exchange(embed_sum, "mp").reshape(group, dec_width)
    emb_own, _ = lax.optimization_barrier((emb_own, hidden))
    emb_other = swap(emb_own)

    groups = dec_width // 128
    rows = (128 // DHD) * pos_dev
    prediction, g_own, g_send = call(
        decoder_kernel,
        [
            sds((pos_dev, target.shape[2]), BF16),
            sds((group, dec_width), F32),
            sds((group, dec_width), BF16),
        ],
        ids,
        emb_own,
        emb_other,
        mask_row,
        vis_row,
        hidden,
        wk_t,
        w_dec,
        pos_vis,
        position_table,
        wq_t,
        km_t,
        vm,
        decoder_output,
        pixel_weight,
        target[0],
        scratch=[sds((groups, rows, npos), BF16), sds((groups, rows, nvis), BF16)]
        + [sds(wk_t.shape, BF16), sds(w_dec.shape, BF16), sds(pos_vis.shape, BF16)]
        + [sds(position_table.shape, BF16), sds(wq_t.shape, BF16), sds(km_t.shape, BF16), sds(vm.shape, BF16)]
        + [sds(decoder_output.shape, BF16), sds(pixel_weight.shape, BF16), sds(target.shape[1:], BF16)],
        far=tuple(range(6, 16)),
        copies=12,
    )
    g_part = (g_own + swap(g_send).astype(F32)).astype(BF16).reshape(8, tok, dec_width)
    (g_sum,) = call(sum_kernel, [sds((8, tok, dec_width), BF16)], ids, exchange(g_part, "mp"), limit=16)
    ge_own = exchange(g_sum, "mp").reshape(group, dec_width)
    ge_other = swap(ge_own)

    right, left, parts = call(
        encoder_back_kernel,
        [
            sds((tok, half + 128), BF16),
            sds((tok, half + 128), BF16),
            sds((8, 2 * tok, half + 128), BF16),
        ],
        ids,
        ge_own,
        ge_other,
        embed_weight,
        wpt,
        e_enc,
        q_enc,
        k_enc,
        v_enc,
        aux,
        w_in,
        *ordered,
        scratch=[sds((dec_width, width), BF16)]
        + saved
        + [sds((2, 8, tok, half), BF16), held]
        + [sds((nvis, 3 * width), BF16), sds((8, 2 * tok, half + 128), BF16)],
        far=tuple(range(4, 19)),
        far_out=(2,),
        copies=30,
    )

    def part(offset):
        return lax.dynamic_index_in_dim(parts, (column + offset) % 8, 0, False).astype(F32)

    right, left = lax.optimization_barrier((shift(right, 1), shift(left, -1)))
    ahead, behind = part(3), part(-3)
    right = jnp.concatenate([right.astype(F32) + ahead[:tok], ahead[tok:]]).astype(BF16)
    left = jnp.concatenate([behind[:tok], left.astype(F32) + behind[tok:]]).astype(BF16)
    for offset in (2, 1):
        right, left = lax.optimization_barrier((shift(right, 1), shift(left, -1)))
        right = (right.astype(F32) + part(offset)).astype(BF16)
        left = (left.astype(F32) + part(-offset)).astype(BF16)
    total = shift(right, 1).astype(F32) + shift(left, -1).astype(F32) + part(0)
    (patch_grad,) = call(
        final_kernel,
        [sds((tok, model), BF16)],
        ids,
        x_own,
        total,
        swap(total[tok:].astype(BF16)),
        limit=16,
    )
    return (prediction[None], patch_grad[None])


def solution(mesh):
    group = ("section", "mp")
    in_specs = (
        P("dp", group, None),
        P("dp", group),
        P("section", None, "mp"),
        P("mp", "section"),
        P(group, None),
        P(),
        P(group, None),
        P(),
        P(),
        P(),
        P("dp", group, None),
    )
    out_specs = (P("dp", group, None), P("dp", group, None))
    return jax.shard_map(shards, mesh=mesh, in_specs=in_specs, out_specs=out_specs, check_vma=False)
```
